32 devices in a mesh: pair: 2 (over core), seq: 4 (over z), asset: 4 (over y, x).
Axes of the slice: x: 2, y: 2, z: 4, core: 2. Of those that a mesh axis runs over, the one named last changes fastest.
Arguments:
- latents: float32 [4, 8, 512], P('asset', None, 'seq'), may hold values from -6 to 6
- voxel_coords: int32 [4, 3, 512], P('asset', None, 'seq'), may hold values from 0 to 63
- owner_map: int32 [4, 512, 1], P('asset', 'seq'), may hold values from 0 to 3; in each aligned block of 128 rows (0 to 127, 128 to 255, ..., all dimensions but the last counted through in order) at most 64 rows name the same one
- step_time: float32 [4], P('asset'), may hold values from 0.2 to 0.5
- modulation: float32 [4, 2, 5, 1024], P('asset', 'pair'), may hold values from -3 to 3
- in_proj: float32 [8, 1024], replicated, may hold values from -2 to 2
- qkv_proj: bfloat16 [1024, 1536], replicated, may hold values from -0.1875 to 0.1875
- norm_gain: float32 [2, 512], replicated, may hold values from 1.5 to 3
- out_proj: bfloat16 [512, 1024], replicated, may hold values from -0.25 to 0.25
- head_proj: float32 [1024, 8], replicated, may hold values from -0.1875 to 0.1875
- decoder_projection: float32 [8, 768], replicated, may hold values from -2 to 2
- border_blocks: int32 [4, 4, 2, 8], P('asset', 'seq'), may hold values from 0 to 15
- kernel_map: int32 [4, 4, 27, 1024], P('asset', 'seq'), may hold values from 0 to 512
- conv_weight: bfloat16 [27, 768, 192], P(None, None, 'pair'), may hold values from -0.0390625 to 0.0390625
Outputs:
- owned_latents: float32 [4, 4, 8, 256], P('asset', 'seq')
- decoded: bfloat16 [4, 4, 1024, 192], P('asset', 'seq', None, 'pair')
The draws below stay inside these ranges and needn't reach their ends.
Inputs may be any that keep to these rules, and one draw needn't show every extreme that they name: `owner_map`: in each aligned block of 128 tokens (the tokens of one device) no owner is named by more than 64 tokens. `kernel_map`: rows below 256 are the owner's slots, the next 128 come from the owner below, the next 128 from the owner above, and 512 is the zero row.
All inputs are finite; a program needn't handle non-finite values.
Results may differ from the reference program's by a relative error of at most 0.0075.
Values may be sent and summed in bfloat16 or wider, within the bound.
No kernel may reach another device: no remote copies, remote signals or barrier semaphores. Data moves between devices by JAX's collectives and lax.ppermute only.
A program may use at most 128 MiB of HBM per device.

```python
import math
import jax
import jax.numpy as jnp
import numpy as np
from jax import lax

D = 1024
HEADS = 8
HEAD = 64
LAT = 8
DEC = 768
OUTC = 192
KOFF = 27
BLK = 16
HB = 8
RES = 64
TOK_DEV = 128
ASSETS = 4
SEQ_LEN = 512
CAP = 64
SLOTS = 256
HALO = 128
TABLE = 512
FINE = 1024
HW = 512
N_SEQ = 4


def touch_ends(array, stream_key, smallest, top_value):
    extent = array.shape
    spot = [jax.random.randint(jax.random.fold_in(stream_key, axis), (), 0, extent[axis]) for axis in range(len(extent))]
    array = array.at[tuple(spot)].set(smallest)
    longest = extent.index(max(extent))
    spot[longest] = (spot[longest] + 1) % extent[longest]
    return array.at[tuple(spot)].set(top_value)


def steps_of(key, shape, cuts, smallest, top_value):
    level, own = 1.0, jax.random.fold_in(key, 6)
    for dim, blocks in cuts:
        heights = jnp.exp(jax.random.uniform(jax.random.fold_in(own, dim), (blocks,), jnp.float32, smallest / len(cuts), top_value / len(cuts)))
        level = level * jnp.repeat(heights, shape[dim] // blocks).reshape([-1 if axis == dim else 1 for axis in range(len(shape))])
    return level


def routed_block(rng, own, number, rows, count, top, reach, slope):
    order = jax.random.permutation(rng, count)
    packed, common = portions_of(count, rows * top, reach, slope, True), portions_of(count, rows * top, reach, slope, False)
    places = jnp.arange(count)

    def named(sizes, turn):
        used = int((sizes > 0).sum())
        fixed = max(1, used // 4)
        passed = fixed + (places - fixed + turn * (used - fixed)) % max(1, count - fixed)
        return jnp.zeros((count,), jnp.int32).at[order[jnp.where(places < fixed, places, passed)]].set(jnp.asarray(sizes, jnp.int32))

    sizes = jnp.where(number % 4 == 0, named(packed, number // 4), named(common, number - number // 4 - 1))
    mixed = jax.random.permutation(jax.random.fold_in(own, 3), count)
    source_of, sink = mixed[0:count // 2 * 2:2], mixed[1:count // 2 * 2:2]
    room = jnp.minimum(sizes[source_of] - 1, reach - sizes[sink]) // 2
    room = jnp.where((source_of == order[0]) | (sink == order[0]) | (sizes[sink] == 0), 0, jnp.maximum(room, 0))
    passed = jax.random.randint(jax.random.fold_in(own, 4), (count // 2,), 0, 1 << 20) % (room + 1)
    sizes = sizes.at[source_of].add(-passed).at[sink].add(passed)
    labels = jnp.searchsorted(jnp.cumsum(sizes), jnp.arange(rows * top), side="right").astype(jnp.int32)
    listing = labels.reshape(top, rows).T
    listing = listing[jax.random.permutation(jax.random.fold_in(own, 1), rows)]
    turn = jax.random.randint(jax.random.fold_in(own, 2), (rows, 1), 0, top)
    return jnp.take_along_axis(listing, (jnp.arange(top)[None, :] + turn) % top, axis=1)


def portions_of(count, total, most, slope, full):
    portions = [(1 << 20) // math.isqrt(standing ** slope) + 1 for standing in range(1, count + 1)]
    largest = most if full else min(most, max(-(-total // count), total * portions[0] // sum(portions)))
    least = 1 if total - largest >= count - 1 else 0
    counts, surplus = [largest] + [least] * (count - 1), total - largest - least * (count - 1)
    while surplus > 0:
        movable = [i for i in range(1, count) if counts[i] < largest] or [i for i in range(1, count) if counts[i] < most]
        pool, remaining = sum([portions[i] for i in movable]), surplus
        for i in movable:
            extra = min(most - counts[i], max(1, remaining * portions[i] // pool), surplus)
            counts[i] = counts[i] + extra
            surplus = surplus - extra
    return np.array(counts)


def centred(rng, extent, scale, bound, shards=(), held_as=jnp.bfloat16):
    values = jax.random.normal(rng, extent, jnp.float32) * scale
    if len(shards) > 0:
        values = steps_of(rng, extent, shards, -0.22, 0.18) * values
    return jnp.clip(values, min=-bound, max=bound).astype(held_as)


def setup_inputs(seed: int = 0) -> dict:
    key_of = jax.random.split(jax.random.key(seed), 15)
    latents = centred(key_of[0], (ASSETS, LAT, SEQ_LEN), 1.0, 6.0, ((0, 4), (2, 4)), jnp.float32)
    voxel_coords = touch_ends(jax.random.randint(key_of[1], (ASSETS, 3, SEQ_LEN), 0, RES), jax.random.fold_in(key_of[1], 1), 0, RES - 1).astype(jnp.int32)
    owner_map_keys = jax.random.split(jax.random.fold_in(key_of[2], 1), ASSETS * SEQ_LEN // TOK_DEV)
    owner_map_turns = jax.random.permutation(jax.random.fold_in(key_of[2], 3), ASSETS * SEQ_LEN // TOK_DEV)
    owner_map = jax.vmap(lambda own, number: routed_block(jax.random.fold_in(key_of[2], 2), own, number, TOK_DEV, N_SEQ, 1, CAP, 2))(owner_map_keys, owner_map_turns).reshape((ASSETS, SEQ_LEN, 1))
    step_time = jnp.clip(0.2 + 0.3 * jax.random.uniform(key_of[3], (ASSETS,), jnp.float32) ** steps_of(key_of[3], (ASSETS,), ((0, 4),), -0.2, 0.2), 0.2, 0.5)
    modulation = centred(key_of[4], (ASSETS, 2, 5, D), 0.5, 3.0, ((0, 4), (1, 2)), jnp.float32)
    in_proj = centred(key_of[5], (LAT, D), LAT ** -0.5, 2.0, (), jnp.float32)
    qkv_proj = centred(key_of[6], (D, 3 * HW), D ** -0.5, 0.1875)
    norm_gain = jnp.clip(jax.random.uniform(key_of[7], (2, HW), jnp.float32, 1.5, 3.0), 1.5, 3.0)
    out_proj = centred(key_of[8], (HW, D), HW ** -0.5, 0.25)
    head_proj = centred(key_of[9], (D, LAT), D ** -0.5, 0.1875, (), jnp.float32)
    decoder_projection = centred(key_of[10], (LAT, DEC), LAT ** -0.5, 2.0, (), jnp.float32)
    border_blocks = touch_ends(jax.random.randint(key_of[11], (ASSETS, N_SEQ, 2, HB), 0, SLOTS // BLK), jax.random.fold_in(key_of[11], 1), 0, (SLOTS // BLK) - 1).astype(jnp.int32)
    kernel_map = touch_ends(jax.random.randint(key_of[12], (ASSETS, N_SEQ, KOFF, FINE), 0, TABLE + 1), jax.random.fold_in(key_of[12], 1), 0, TABLE).astype(jnp.int32)
    conv_weight = centred(key_of[13], (KOFF, DEC, OUTC), (KOFF * DEC) ** -0.5, 0.0390625, ((2, 2),))
    return dict(latents=latents, voxel_coords=voxel_coords, owner_map=owner_map, step_time=step_time, modulation=modulation, in_proj=in_proj, qkv_proj=qkv_proj, norm_gain=norm_gain, out_proj=out_proj, head_proj=head_proj, decoder_projection=decoder_projection, border_blocks=border_blocks, kernel_map=kernel_map, conv_weight=conv_weight)


EPSILON = 1e-06
GUIDANCE = 3.0
TOP_PRECISION = lax.Precision.HIGHEST

def layer_norm(values):
    center = values - lax.optimization_barrier(jnp.mean(values, axis=-1, keepdims=True))
    variance = lax.optimization_barrier(jnp.mean(center * center, axis=-1, keepdims=True))
    return center / jnp.sqrt(variance + EPSILON)

def position_table(coord_rows, model_width):
    freqs = model_width // 6
    steps = jnp.arange(freqs, dtype=jnp.float32) / freqs
    omegas = jnp.exp(-math.log(10000.0) * steps)
    angles = coord_rows.astype(jnp.float32)[:, :, None] * omegas[None, None, :]
    halves = jnp.concatenate([jnp.sin(angles), jnp.cos(angles)], axis=2)
    rows_out = jnp.transpose(halves, (1, 0, 2)).reshape(coord_rows.shape[1], 6 * freqs)
    return jnp.pad(rows_out, ((0, 0), (0, model_width - 6 * freqs)))

def head_norm(values, gains):
    row_count = values.shape[0]
    per_head = values.reshape(row_count, HEADS, HEAD)
    mean_square = lax.optimization_barrier(jnp.mean(per_head * per_head, axis=2, keepdims=True))
    return (per_head / jnp.sqrt(mean_square + EPSILON)).reshape(row_count, HEADS * HEAD) * gains

def attention(queries, keys_in, values_in):
    row_count = queries.shape[0]
    block_rows = math.gcd(row_count, 512)
    factor = HEAD ** (-0.5)
    key_heads = keys_in.reshape(row_count, HEADS, HEAD).astype(jnp.float32)
    value_head_rows = values_in.reshape(row_count, HEADS, HEAD).astype(jnp.float32)

    def one_block(query_block):
        scores = jnp.einsum('qhd,khd->hqk', query_block.astype(jnp.float32), key_heads) * factor
        exp_scores = jnp.exp(scores)
        rounded_count = lax.optimization_barrier(exp_scores.astype(jnp.bfloat16))
        numerator = jnp.einsum('hqk,khd->qhd', rounded_count.astype(jnp.float32), value_head_rows)
        denominator = lax.optimization_barrier(jnp.sum(exp_scores, axis=2)).T
        return (numerator / denominator[:, :, None]).astype(jnp.bfloat16)
    blocks_out = lax.map(one_block, queries.reshape(row_count // block_rows, block_rows, HEADS, HEAD))
    return blocks_out.reshape(row_count, HEADS * HEAD)

def branch_velocity(latent_block, coord_rows, modulation_rows, in_proj, qkv_proj, norm_gain, out_proj, head_proj):
    hidden = jnp.dot(latent_block.T, in_proj, precision=TOP_PRECISION) + position_table(coord_rows, D)
    normed = (layer_norm(hidden) * (1.0 + modulation_rows[1]) + modulation_rows[0]).astype(jnp.bfloat16)
    projected = jnp.dot(normed, qkv_proj, preferred_element_type=jnp.float32)
    inner_width = HEADS * HEAD
    queries = head_norm(projected[:, :inner_width], norm_gain[0]).astype(jnp.bfloat16)
    keys_in = head_norm(projected[:, inner_width:2 * inner_width], norm_gain[1]).astype(jnp.bfloat16)
    values_in = projected[:, 2 * inner_width:].astype(jnp.bfloat16)
    attended = attention(queries, keys_in, values_in)
    hidden = hidden + modulation_rows[2] * jnp.dot(attended, out_proj, preferred_element_type=jnp.float32)
    final = layer_norm(hidden) * (1.0 + modulation_rows[4]) + modulation_rows[3]
    return jnp.dot(final, head_proj, precision=TOP_PRECISION).T

def relayout(clean, owner_rows):
    owner_ids = jnp.arange(N_SEQ, dtype=jnp.int32)
    onehot = (owner_rows[:, None] == owner_ids[None, :]).astype(jnp.int32)
    onehot = onehot.reshape(N_SEQ, TOK_DEV, N_SEQ)
    ranks = lax.optimization_barrier(jnp.sum(onehot * (jnp.cumsum(onehot, axis=1).astype(jnp.int32) - 1), axis=2)).astype(jnp.int32)
    ranks = ranks.reshape(SEQ_LEN)
    sources = jnp.arange(SEQ_LEN, dtype=jnp.int32) // TOK_DEV
    slot_ids = (sources * CAP + ranks).astype(jnp.int32)
    owned_rows = jnp.zeros((N_SEQ, SLOTS, LAT), jnp.float32).at[owner_rows, slot_ids].set(clean.T)
    return jnp.transpose(owned_rows, (0, 2, 1))

def decode(owned_rows, border_rows, map_rows, decoder_projection, conv_weight):
    owner_count = owned_rows.shape[0]
    voxel_features = jax.nn.silu(jnp.einsum('pjw,jm->pwm', owned_rows, decoder_projection, precision=TOP_PRECISION)).astype(jnp.bfloat16)
    tiles = voxel_features.reshape(owner_count, SLOTS // BLK, BLK, DEC)
    border = jax.vmap(lambda tile_rows, chosen: tile_rows[chosen.reshape(-1)])(tiles, border_rows)
    border = border.reshape(owner_count, 2, HALO, DEC)
    empty_rows = jnp.zeros((1, HALO, DEC), jnp.bfloat16)
    received_below = jnp.concatenate([empty_rows, border[:-1, 1]], axis=0)
    from_above = jnp.concatenate([border[1:, 0], empty_rows], axis=0)
    zero_row = jnp.zeros((owner_count, 1, DEC), jnp.bfloat16)
    tables = jnp.concatenate([voxel_features, received_below, from_above, zero_row], axis=1)
    offsets = jnp.arange(KOFF, dtype=jnp.int32)[:, None]
    weight_full = conv_weight.astype(jnp.float32)

    def one_owner(inputs):
        rows_table, index_map = inputs
        products = jnp.einsum('rc,kco->kro', rows_table.astype(jnp.float32), weight_full)
        return lax.optimization_barrier(jnp.sum(products[offsets, index_map], axis=0)).astype(jnp.bfloat16)
    return lax.map(one_owner, (tables, map_rows))

def reference(latents, voxel_coords, owner_map, step_time, modulation, in_proj, qkv_proj, norm_gain, out_proj, head_proj, decoder_projection, border_blocks, kernel_map, conv_weight):
    owned_list = []
    decoded_list = []
    for asset_id in range(ASSETS):
        velocities = [branch_velocity(latents[asset_id], voxel_coords[asset_id], modulation[asset_id, branch], in_proj, qkv_proj, norm_gain, out_proj, head_proj) for branch in range(2)]
        guided = velocities[1] + GUIDANCE * (velocities[0] - velocities[1])
        clean = latents[asset_id] - step_time[asset_id] * guided
        owned_rows = relayout(clean, owner_map[asset_id, :, 0])
        owned_list.append(owned_rows)
        decoded_list.append(decode(owned_rows, border_blocks[asset_id], kernel_map[asset_id], decoder_projection, conv_weight))
    return (jnp.stack(owned_list), jnp.stack(decoded_list))
```

```python
import functools
import math

import jax
import jax.numpy as jnp
import numpy as np
from jax import lax
from jax.experimental import pallas as pl
from jax.experimental.pallas import tpu as pltpu
from jax.sharding import PartitionSpec as P

HEADS = 8
HEAD = 64
LAT = 8
BLK = 16
RES = 64

EPSILON = 1e-06
GUIDANCE = 3.0
TOP_PRECISION = lax.Precision.HIGHEST
F32 = jnp.float32
BF16 = jnp.bfloat16
I32 = jnp.int32

ROW_COORD = 8
ROW_OWNER = 11
ROW_BORDER = 12
PACK_ROWS = 16
WHOLE_ASSET = 512

VMEM = pl.BlockSpec(memory_space=pltpu.VMEM)
SMEM = pl.BlockSpec(memory_space=pltpu.SMEM)


def dot_ab(a, b):
    return jnp.dot(a, b, preferred_element_type=F32)


def dot_abt(a, b):
    return lax.dot_general(a, b, (((1,), (1,)), ((), ())), preferred_element_type=F32)


def dot_atb(a, b):
    return lax.dot_general(a, b, (((0,), (0,)), ((), ())), preferred_element_type=F32)


def split_two(x):
    high = x.astype(BF16).astype(F32)
    return high, x - high


def split_three(x):
    high, rest = split_two(x)
    mid, low = split_two(rest)
    return high, mid, low


@functools.lru_cache(None)
def position_parts(model_width):
    freqs = model_width // 6
    steps = np.arange(freqs, dtype=np.float32) / np.float32(freqs)
    omegas = np.exp(np.float32(-math.log(10000.0)) * steps).astype(np.float32)
    angles = (np.arange(RES, dtype=np.float32)[:, None] * omegas[None, :]).astype(np.float64)
    halves = np.concatenate([np.sin(angles), np.cos(angles)], axis=1).astype(np.float32)
    table = np.zeros((3 * RES, model_width), np.float32)
    for c in range(3):
        table[c * RES : (c + 1) * RES, c * 2 * freqs : (c + 1) * 2 * freqs] = halves
    high = table.astype(jnp.bfloat16)
    low = (table - high.astype(np.float32)).astype(jnp.bfloat16)
    return np.concatenate([high, low], axis=0)


def velocity_kernel(
    own_ref,
    mixed_ref,
    swapped_ref,
    far_ref,
    mod_ref,
    in_ref,
    qkv_ref,
    gain_ref,
    out_ref,
    head_ref,
    pos_ref,
    vel_ref,
    blocks_ref,
    table_ref,
    hidden_ref,
    normed_ref,
    query_ref,
    key_ref,
    value_ref,
    att_ref,
):
    me = lax.axis_index("seq")
    side = lax.axis_index("pair")
    width = in_ref.shape[1]
    tokens = hidden_ref.shape[0]
    inner = out_ref.shape[0]
    block = own_ref.shape[1]

    blocks_ref[me] = own_ref[...]
    blocks_ref[me ^ 3] = far_ref[...]
    blocks_ref[me ^ (1 + side)] = mixed_ref[...]
    blocks_ref[me ^ (2 - side)] = swapped_ref[...]

    pos_rows = pos_ref.shape[0]
    table_ref[0:pos_rows, :] = pos_ref[...]
    in_high, in_low = split_two(in_ref[...])
    table_ref[pos_rows : pos_rows + 32, :] = jnp.concatenate(
        [in_high, in_high, in_low, jnp.zeros_like(in_low)], axis=0
    ).astype(BF16)

    shift = mod_ref[0]
    scale = 1.0 + mod_ref[1]
    for s in range(tokens // block):
        rows = blocks_ref[s]
        values = lax.broadcasted_iota(I32, (RES, block), 0).astype(F32)
        hots = [
            (values == rows[ROW_COORD + c : ROW_COORD + c + 1]).astype(F32).astype(BF16)
            for c in range(3)
        ]
        high, low = split_two(rows[0:LAT])
        tail = jnp.concatenate([high, low, high, jnp.zeros_like(low)], axis=0).astype(BF16)
        picks = jnp.concatenate(hots + hots + [tail], axis=0)
        hidden = dot_atb(picks, table_ref[...])
        hidden_ref[s * block : (s + 1) * block, :] = hidden
        center = hidden - jnp.mean(hidden, axis=1, keepdims=True)
        inverse = lax.rsqrt(jnp.mean(center * center, axis=1, keepdims=True) + EPSILON)
        normed_ref[s * block : (s + 1) * block, :] = (center * inverse * scale + shift).astype(BF16)

    group = 256
    same_head = (
        lax.broadcasted_iota(I32, (group, group), 0) // HEAD
        == lax.broadcasted_iota(I32, (group, group), 1) // HEAD
    )
    averager = jnp.where(same_head, 1.0 / HEAD, 0.0).astype(BF16)
    for j in range(3 * inner // group):
        projected = dot_ab(normed_ref[...], qkv_ref[:, j * group : (j + 1) * group])
        which, col = divmod(j * group, inner)
        if which == 2:
            for half in range(group // 128):
                pair = (col + half * 128) // 128
                value_ref[pair, :, 0:128] = projected[:, half * 128 : (half + 1) * 128].astype(BF16)
                value_ref[pair, :, 128:256] = jnp.ones((tokens, 128), BF16)
        else:
            square = dot_ab((projected * projected).astype(BF16), averager)
            gains = gain_ref[which : which + 1, col : col + group]
            if which == 0:
                gains = gains * (HEAD**-0.5)
            result = (projected * lax.rsqrt(square + EPSILON) * gains).astype(BF16)
            (query_ref, key_ref)[which][:, col : col + group] = result

    chunk = 256
    first = lax.broadcasted_iota(I32, (chunk, 128), 1) < HEAD
    for pair in range(inner // 128):
        lanes = slice(pair * 128, (pair + 1) * 128)
        for q in range(tokens // chunk):
            here = slice(q * chunk, (q + 1) * chunk)
            query = query_ref[here, lanes]
            parts = []
            for half in range(2):
                kept = jnp.where(first == (half == 0), query, jnp.zeros_like(query))
                scores = dot_abt(kept, key_ref[:, lanes])
                weights = jnp.exp(scores).astype(BF16)
                sums = dot_ab(weights, value_ref[pair])
                parts.append(sums[:, 0:128] / sums[:, 128:256])
            att_ref[here, lanes] = jnp.where(first, parts[0], parts[1]).astype(BF16)

    gate = mod_ref[2]
    head = head_ref[...]
    offset = jnp.sum(head * mod_ref[3], axis=1, keepdims=True)
    head_high, head_low = split_two(head * (1.0 + mod_ref[4]))
    heads = jnp.concatenate([head_high, head_low], axis=0).astype(BF16)
    for s in range(tokens // block):
        here = slice(s * block, (s + 1) * block)
        hidden = hidden_ref[here, :] + gate * dot_ab(att_ref[here, :], out_ref[...])
        center = hidden - jnp.mean(hidden, axis=1, keepdims=True)
        inverse = lax.rsqrt(jnp.mean(center * center, axis=1, keepdims=True) + EPSILON)
        final = center * inverse
        final_high, final_low = split_two(final)
        both = dot_abt(heads, final_high.astype(BF16))
        rest = dot_abt(heads, final_low.astype(BF16))
        vel_ref[:, here] = both[0:LAT] + both[LAT:] + rest[0:LAT] + offset


def decode_kernel(
    blocks_ref,
    mine_ref,
    other_ref,
    time_ref,
    proj_ref,
    map_ref,
    weight_ref,
    owned_ref,
    fine_ref,
    product_ref,
):
    me = lax.axis_index("seq")
    is_cond = lax.axis_index("pair") == 0
    count, _, block = blocks_ref.shape
    slots = owned_ref.shape[1]
    capacity = slots // count
    offsets, out_channels, dec_width = weight_ref.shape
    halo = 128
    table_rows = slots + 2 * halo

    mine, other = mine_ref[...], other_ref[...]
    cond = jnp.where(is_cond, mine, other)
    uncond = jnp.where(is_cond, other, mine)
    latents = jnp.concatenate([blocks_ref[s, 0:LAT, :] for s in range(count)], axis=1)
    clean = latents - time_ref[0] * (uncond + GUIDANCE * (cond - uncond))

    owners = jnp.concatenate(
        [blocks_ref[s, ROW_OWNER : ROW_OWNER + 1, :] for s in range(count)], axis=0
    ).astype(I32)
    earlier = (
        lax.broadcasted_iota(I32, (block, block), 0) < lax.broadcasted_iota(I32, (block, block), 1)
    ).astype(F32).astype(BF16)
    starts = lax.broadcasted_iota(I32, (count, block), 0) * capacity
    targets = []
    for step in (0, -1, 1):
        named = owners == me + step
        ranks = dot_ab(named.astype(F32).astype(BF16), earlier).astype(I32)
        slot_of = jnp.where(named, ranks + starts, -1)
        targets.append(jnp.concatenate([slot_of[s : s + 1] for s in range(count)], axis=1))
    tokens = count * block
    rows = lax.broadcasted_iota(I32, (slots, tokens), 0)
    picks = [(rows == targets[0]).astype(F32).astype(BF16)]
    small = lax.broadcasted_iota(I32, (BLK, tokens), 0)
    for step, direction in ((-1, 1), (1, 0)):
        source = jnp.clip(me + step, 0, count - 1)
        border = blocks_ref[source, ROW_BORDER : ROW_BORDER + 1, :].astype(I32)
        target = targets[1 if step < 0 else 2]
        for i in range(halo // BLK):
            at = direction * (halo // BLK) + i
            wanted = border[:, at : at + 1] * BLK
            picks.append((small + wanted == target).astype(F32).astype(BF16))
    picks = jnp.concatenate(picks, axis=0)
    parts = jnp.concatenate(split_three(clean), axis=0).astype(BF16)
    spread = dot_abt(parts, picks)
    table = spread[0:LAT] + spread[LAT : 2 * LAT] + spread[2 * LAT :]
    owned_ref[...] = table[:, 0:slots]

    proj_high, proj_low = split_two(proj_ref[...])
    table_high, table_low = split_two(table)
    left = jnp.concatenate([proj_high, proj_high, proj_low, jnp.zeros_like(proj_low)], axis=0)
    right = jnp.concatenate([table_high, table_low, table_high, jnp.zeros_like(table_low)], axis=0)
    before = dot_atb(left.astype(BF16), right.astype(BF16))
    features = (0.5 * before * (1.0 + jnp.tanh(0.5 * before))).astype(BF16)

    for k in range(offsets):
        product_ref[k] = dot_ab(weight_ref[k], features).astype(BF16)

    fine = map_ref.shape[2]
    width = 256
    table_ids = lax.broadcasted_iota(I32, (table_rows, width), 0)
    for f in range(fine // width):
        here = slice(f * width, (f + 1) * width)
        total = jnp.zeros((out_channels, width), F32)
        for k in range(offsets):
            chosen = (table_ids == map_ref[k, :, here]).astype(F32).astype(BF16)
            total = total + dot_ab(product_ref[k], chosen)
        fine_ref[:, here] = total.astype(BF16)


def swap_pair(x):
    return lax.ppermute(x, "pair", [(0, 1), (1, 0)])


def seq_swap(x, distance_of):
    count = lax.axis_size("seq")
    routes = [
        (p * count + (z ^ distance_of[p]), p * count + z) for p in range(2) for z in range(count)
    ]
    return lax.ppermute(x, ("pair", "seq"), routes)


def whole_asset_velocity(packed, modulation, in_proj, qkv_proj, norm_gain, out_proj, head_proj):
    count = lax.axis_size("seq")
    block = packed.shape[1]
    tokens = count * block
    width = in_proj.shape[1]
    inner = out_proj.shape[0]
    mixed = seq_swap(packed, (1, 2))
    far = seq_swap(packed, (3, 3))
    swapped = swap_pair(mixed)
    pos = jnp.asarray(position_parts(width))
    return pl.pallas_call(
        velocity_kernel,
        out_shape=(
            jax.ShapeDtypeStruct((LAT, tokens), F32),
            jax.ShapeDtypeStruct((count, PACK_ROWS, block), F32),
        ),
        in_specs=[VMEM] * 11,
        out_specs=(VMEM, VMEM),
        scratch_shapes=[
            pltpu.VMEM((pos.shape[0] + 32, width), BF16),
            pltpu.VMEM((tokens, width), F32),
            pltpu.VMEM((tokens, width), BF16),
            pltpu.VMEM((tokens, inner), BF16),
            pltpu.VMEM((tokens, inner), BF16),
            pltpu.VMEM((inner // 128, tokens, 256), BF16),
            pltpu.VMEM((tokens, inner), BF16),
        ],
        compiler_params=pltpu.CompilerParams(vmem_limit_bytes=40 << 20),
        name="velocity",
    )(
        packed,
        mixed,
        swapped,
        far,
        modulation[0, 0][:, None, :],
        in_proj,
        qkv_proj,
        norm_gain,
        out_proj,
        head_proj.T,
        pos,
    )


def layer_norm(values):
    center = values - jnp.mean(values, axis=-1, keepdims=True)
    variance = jnp.mean(center * center, axis=-1, keepdims=True)
    return center / jnp.sqrt(variance + EPSILON)


def position_table(coord_rows, model_width):
    freqs = model_width // 6
    steps = jnp.arange(freqs, dtype=F32) / freqs
    omegas = jnp.exp(-math.log(10000.0) * steps)
    angles = coord_rows.astype(F32)[:, :, None] * omegas[None, None, :]
    halves = jnp.concatenate([jnp.sin(angles), jnp.cos(angles)], axis=2)
    rows_out = jnp.transpose(halves, (1, 0, 2)).reshape(coord_rows.shape[1], 6 * freqs)
    return jnp.pad(rows_out, ((0, 0), (0, model_width - 6 * freqs)))


def head_norm(values, gains):
    row_count = values.shape[0]
    per_head = values.reshape(row_count, HEADS, HEAD)
    mean_square = jnp.mean(per_head * per_head, axis=2, keepdims=True)
    return (per_head / jnp.sqrt(mean_square + EPSILON)).reshape(row_count, HEADS * HEAD) * gains


def gathered_velocity(
    latent_block, coords, modulation, in_proj, qkv_proj, norm_gain, out_proj, head_proj
):
    token_count = latent_block.shape[1]
    model_width = in_proj.shape[1]
    inner_width = out_proj.shape[0]
    factor = HEAD ** (-0.5)
    mod_rows = modulation[0, 0]
    hidden = jnp.dot(latent_block.T, in_proj, precision=TOP_PRECISION) + position_table(
        coords, model_width
    )
    normed = (layer_norm(hidden) * (1.0 + mod_rows[1]) + mod_rows[0]).astype(BF16)
    projected = jnp.dot(normed, qkv_proj, preferred_element_type=F32)
    queries = head_norm(projected[:, :inner_width], norm_gain[0]).astype(BF16)
    keys_in = head_norm(projected[:, inner_width : 2 * inner_width], norm_gain[1]).astype(BF16)
    values_in = projected[:, 2 * inner_width :].astype(BF16)
    query_heads = queries.reshape(token_count, HEADS, HEAD)
    start_pair = (
        jnp.zeros((token_count, HEADS, HEAD), F32),
        jnp.zeros((token_count, HEADS), F32),
    )
    key_rows = lax.all_gather(keys_in, "seq", axis=0, tiled=True)
    value_rows = lax.all_gather(values_in, "seq", axis=0, tiled=True)
    row_count = key_rows.shape[0]
    block_rows = math.gcd(row_count, 512)
    key_blocks = key_rows.reshape(row_count // block_rows, block_rows, HEADS, HEAD)
    value_blocks = value_rows.reshape(row_count // block_rows, block_rows, HEADS, HEAD)

    def one_block(running, block_pair):
        numer_run, denom_run = running
        key_block, value_block = block_pair
        scores = (
            jnp.einsum("qhd,khd->hqk", query_heads, key_block, preferred_element_type=F32) * factor
        )
        exp_scores = jnp.exp(scores)
        numer_run = numer_run + jnp.einsum(
            "hqk,khd->qhd", exp_scores.astype(BF16), value_block, preferred_element_type=F32
        )
        denom_run = denom_run + jnp.sum(exp_scores, axis=2).T
        return ((numer_run, denom_run), None)

    (numerator, denominator), _ = lax.scan(one_block, start_pair, (key_blocks, value_blocks))
    attended = (
        (numerator / denominator[:, :, None]).reshape(token_count, inner_width).astype(BF16)
    )
    hidden = hidden + mod_rows[2] * jnp.dot(attended, out_proj, preferred_element_type=F32)
    final = layer_norm(hidden) * (1.0 + mod_rows[4]) + mod_rows[3]
    velocity = jnp.dot(final, head_proj, precision=TOP_PRECISION).T
    return lax.all_gather(velocity, "seq", axis=1, tiled=True)


def per_device(
    latents,
    voxel_coords,
    owner_map,
    step_time,
    modulation,
    in_proj,
    qkv_proj,
    norm_gain,
    out_proj,
    head_proj,
    decoder_projection,
    border_blocks,
    kernel_map,
    conv_weight,
):
    count = lax.axis_size("seq")
    block = latents.shape[2]
    chosen = border_blocks.reshape(1, -1)
    packed = jnp.concatenate(
        [
            latents[0],
            voxel_coords[0].astype(F32),
            owner_map[0].reshape(1, block).astype(F32),
            jnp.pad(chosen, ((0, 0), (0, block - chosen.shape[1]))).astype(F32),
            jnp.zeros((PACK_ROWS - ROW_BORDER - 1, block), F32),
        ],
        axis=0,
    )
    if count == 4 and count * block <= WHOLE_ASSET:
        velocity, blocks = whole_asset_velocity(
            packed, modulation, in_proj, qkv_proj, norm_gain, out_proj, head_proj
        )
    else:
        blocks = lax.all_gather(packed, "seq", axis=0)
        velocity = gathered_velocity(
            latents[0],
            voxel_coords[0],
            modulation,
            in_proj,
            qkv_proj,
            norm_gain,
            out_proj,
            head_proj,
        )
    partner = swap_pair(velocity)
    offsets, _, out_channels = conv_weight.shape
    fine = kernel_map.shape[3]
    slots = fine // 4
    table_rows = slots + 2 * border_blocks.shape[3] * BLK
    owned, decoded = pl.pallas_call(
        decode_kernel,
        out_shape=(
            jax.ShapeDtypeStruct((LAT, slots), F32),
            jax.ShapeDtypeStruct((out_channels, fine), BF16),
        ),
        in_specs=[VMEM, VMEM, VMEM, SMEM, VMEM, VMEM, VMEM],
        out_specs=(VMEM, VMEM),
        scratch_shapes=[pltpu.VMEM((offsets, out_channels, table_rows), BF16)],
        compiler_params=pltpu.CompilerParams(vmem_limit_bytes=40 << 20),
        name="decode",
    )(
        blocks,
        velocity,
        partner,
        step_time,
        decoder_projection,
        kernel_map.reshape(offsets, 1, fine),
        jnp.swapaxes(conv_weight, 1, 2),
    )
    return (owned[None, None], decoded.T[None, None])


def solution(mesh):
    placed = (
        P("asset", None, "seq"),
        P("asset", None, "seq"),
        P("asset", "seq", None),
        P("asset"),
        P("asset", "pair", None, None),
        P(),
        P(),
        P(),
        P(),
        P(),
        P(),
        P("asset", "seq", None, None),
        P("asset", "seq", None, None),
        P(None, None, "pair"),
    )
    return jax.shard_map(
        per_device,
        mesh=mesh,
        in_specs=placed,
        out_specs=(P("asset", "seq", None, None), P("asset", "seq", None, "pair")),
        check_vma=False,
    )
```

```python
import functools
import math

import jax
import jax.numpy as jnp
import numpy as np
from jax import lax
from jax.experimental import pallas as pl
from jax.experimental.pallas import tpu as pltpu
from jax.sharding import PartitionSpec as P

HEADS = 8
HEAD = 64
LAT = 8
BLK = 16
RES = 64

EPSILON = 1e-06
GUIDANCE = 3.0
TOP_PRECISION = lax.Precision.HIGHEST
F32 = jnp.float32
BF16 = jnp.bfloat16
I32 = jnp.int32

ROW_COORD = 8
ROW_OWNER = 11
ROW_BORDER = 12
PACK_ROWS = 16
WHOLE_ASSET = 512

VMEM_GRANT = 40 << 20

VMEM = pl.BlockSpec(memory_space=pltpu.VMEM)
HBM = pl.BlockSpec(memory_space=pltpu.HBM)
SMEM = pl.BlockSpec(memory_space=pltpu.SMEM)


def dot_ab(a, b):
    return jnp.dot(a, b, preferred_element_type=F32)


def dot_abt(a, b):
    return lax.dot_general(a, b, (((1,), (1,)), ((), ())), preferred_element_type=F32)


def dot_atb(a, b):
    return lax.dot_general(a, b, (((0,), (0,)), ((), ())), preferred_element_type=F32)


def in_hbm(*arrays):
    return [pltpu.with_memory_space_constraint(x, pltpu.HBM) for x in arrays]


def split_two(x):
    high = x.astype(BF16).astype(F32)
    return high, x - high


def split_three(x):
    high, rest = split_two(x)
    mid, low = split_two(rest)
    return high, mid, low


@functools.lru_cache(None)
def position_parts(model_width):
    freqs = model_width // 6
    steps = np.arange(freqs, dtype=np.float32) / np.float32(freqs)
    omegas = np.exp(np.float32(-math.log(10000.0)) * steps).astype(np.float32)
    angles = (np.arange(RES, dtype=np.float32)[:, None] * omegas[None, :]).astype(np.float64)
    halves = np.concatenate([np.sin(angles), np.cos(angles)], axis=1).astype(np.float32)
    table = np.zeros((3 * RES, model_width), np.float32)
    for c in range(3):
        table[c * RES : (c + 1) * RES, c * 2 * freqs : (c + 1) * 2 * freqs] = halves
    high = table.astype(jnp.bfloat16)
    low = (table - high.astype(np.float32)).astype(jnp.bfloat16)
    return np.concatenate([high, low], axis=0)


def pack_kernel(
    lat_hbm, coord_hbm, owner_hbm, border_hbm, pack_ref, coord_ref, owner_ref, border_ref, sems
):
    pack_ref[...] = jnp.zeros_like(pack_ref)
    copies = [
        pltpu.make_async_copy(source, target, sems.at[i])
        for i, (source, target) in enumerate(
            (
                (lat_hbm, pack_ref.at[0:LAT]),
                (coord_hbm, coord_ref),
                (owner_hbm, owner_ref),
                (border_hbm, border_ref),
            )
        )
    ]
    for copy in copies:
        copy.start()
    for copy in copies:
        copy.wait()
    for c in range(3):
        pack_ref[ROW_COORD + c : ROW_COORD + c + 1] = coord_ref[c].astype(F32)
    pack_ref[ROW_OWNER : ROW_OWNER + 1] = owner_ref[...].astype(F32)
    pack_ref[ROW_BORDER : ROW_BORDER + 2, 0 : border_ref.shape[1]] = border_ref[...].astype(F32)


def velocity_kernel(
    own_ref,
    mixed_ref,
    swapped_ref,
    far_ref,
    mod_hbm,
    in_hbm,
    qkv_hbm,
    gain_hbm,
    out_hbm,
    head_hbm,
    pos_hbm,
    vel_ref,
    blocks_ref,
    mod_ref,
    in_ref,
    qkv_ref,
    gain_ref,
    out_ref,
    head_ref,
    table_ref,
    hidden_ref,
    normed_ref,
    query_ref,
    key_ref,
    value_ref,
    att_ref,
    sems,
):
    pos_rows = pos_hbm.shape[0]
    copies = [
        pltpu.make_async_copy(source, target, sems.at[i])
        for i, (source, target) in enumerate(
            (
                (pos_hbm, table_ref.at[0:pos_rows]),
                (in_hbm, in_ref),
                (mod_hbm, mod_ref),
                (gain_hbm, gain_ref),
                (head_hbm, head_ref),
                (qkv_hbm, qkv_ref),
                (out_hbm, out_ref),
            )
        )
    ]
    for copy in copies:
        copy.start()
    me = lax.axis_index("seq")
    side = lax.axis_index("pair")
    width = in_ref.shape[1]
    tokens = hidden_ref.shape[0]
    inner = out_ref.shape[0]
    block = own_ref.shape[1]

    blocks_ref[me] = own_ref[...]
    blocks_ref[me ^ 3] = far_ref[...]
    blocks_ref[me ^ (1 + side)] = mixed_ref[...]
    blocks_ref[me ^ (2 - side)] = swapped_ref[...]

    for copy in copies[:5]:
        copy.wait()
    in_high, in_low = split_two(in_ref[...])
    table_ref[pos_rows : pos_rows + 32, :] = jnp.concatenate(
        [in_high, in_high, in_low, jnp.zeros_like(in_low)], axis=0
    ).astype(BF16)

    shift = mod_ref[0]
    scale = 1.0 + mod_ref[1]
    for s in range(tokens // block):
        rows = blocks_ref[s]
        values = lax.broadcasted_iota(I32, (RES, block), 0).astype(F32)
        hots = [
            (values == rows[ROW_COORD + c : ROW_COORD + c + 1]).astype(F32).astype(BF16)
            for c in range(3)
        ]
        high, low = split_two(rows[0:LAT])
        tail = jnp.concatenate([high, low, high, jnp.zeros_like(low)], axis=0).astype(BF16)
        picks = jnp.concatenate(hots + hots + [tail], axis=0)
        hidden = dot_atb(picks, table_ref[...])
        hidden_ref[s * block : (s + 1) * block, :] = hidden
        center = hidden - jnp.mean(hidden, axis=1, keepdims=True)
        inverse = lax.rsqrt(jnp.mean(center * center, axis=1, keepdims=True) + EPSILON)
        normed_ref[s * block : (s + 1) * block, :] = (center * inverse * scale + shift).astype(BF16)

    copies[5].wait()
    copies[6].wait()
    group = 256
    same_head = (
        lax.broadcasted_iota(I32, (group, group), 0) // HEAD
        == lax.broadcasted_iota(I32, (group, group), 1) // HEAD
    )
    averager = jnp.where(same_head, 1.0 / HEAD, 0.0).astype(BF16)
    for j in range(3 * inner // group):
        projected = dot_ab(normed_ref[...], qkv_ref[:, j * group : (j + 1) * group])
        which, col = divmod(j * group, inner)
        if which == 2:
            for half in range(group // 128):
                pair = (col + half * 128) // 128
                value_ref[pair, :, 0:128] = projected[:, half * 128 : (half + 1) * 128].astype(BF16)
                value_ref[pair, :, 128:256] = jnp.ones((tokens, 128), BF16)
        else:
            square = dot_ab((projected * projected).astype(BF16), averager)
            gains = gain_ref[which : which + 1, col : col + group]
            if which == 0:
                gains = gains * (HEAD**-0.5)
            result = (projected * lax.rsqrt(square + EPSILON) * gains).astype(BF16)
            (query_ref, key_ref)[which][:, col : col + group] = result

    chunk = 256
    first = lax.broadcasted_iota(I32, (chunk, 128), 1) < HEAD
    for pair in range(inner // 128):
        lanes = slice(pair * 128, (pair + 1) * 128)
        for q in range(tokens // chunk):
            here = slice(q * chunk, (q + 1) * chunk)
            query = query_ref[here, lanes]
            parts = []
            for half in range(2):
                kept = jnp.where(first == (half == 0), query, jnp.zeros_like(query))
                scores = dot_abt(kept, key_ref[:, lanes])
                weights = jnp.exp(scores).astype(BF16)
                sums = dot_ab(weights, value_ref[pair])
                parts.append(sums[:, 0:128] / sums[:, 128:256])
            att_ref[here, lanes] = jnp.where(first, parts[0], parts[1]).astype(BF16)

    gate = mod_ref[2]
    head = head_ref[...]
    offset = jnp.sum(head * mod_ref[3], axis=1, keepdims=True)
    head_high, head_low = split_two(head * (1.0 + mod_ref[4]))
    heads = jnp.concatenate([head_high, head_low], axis=0).astype(BF16)
    for s in range(tokens // block):
        here = slice(s * block, (s + 1) * block)
        hidden = hidden_ref[here, :] + gate * dot_ab(att_ref[here, :], out_ref[...])
        center = hidden - jnp.mean(hidden, axis=1, keepdims=True)
        inverse = lax.rsqrt(jnp.mean(center * center, axis=1, keepdims=True) + EPSILON)
        final = center * inverse
        final_high, final_low = split_two(final)
        both = dot_abt(heads, final_high.astype(BF16))
        rest = dot_abt(heads, final_low.astype(BF16))
        vel_ref[:, here] = both[0:LAT] + both[LAT:] + rest[0:LAT] + offset


def decode_kernel(
    blocks_ref,
    mine_ref,
    other_ref,
    time_ref,
    proj_hbm,
    map_hbm,
    weight_hbm,
    owned_ref,
    fine_ref,
    proj_ref,
    map_ref,
    weight_ref,
    product_ref,
    sems,
):
    copies = [
        pltpu.make_async_copy(source, target, sems.at[i])
        for i, (source, target) in enumerate(
            ((proj_hbm, proj_ref), (weight_hbm, weight_ref), (map_hbm, map_ref))
        )
    ]
    for copy in copies:
        copy.start()
    me = lax.axis_index("seq")
    is_cond = lax.axis_index("pair") == 0
    count, _, block = blocks_ref.shape
    slots = owned_ref.shape[1]
    capacity = slots // count
    offsets = map_ref.shape[0]
    out_channels = fine_ref.shape[0]
    table_rows = product_ref.shape[1]
    halo = (table_rows - slots) // 2

    mine, other = mine_ref[...], other_ref[...]
    cond = jnp.where(is_cond, mine, other)
    uncond = jnp.where(is_cond, other, mine)
    latents = jnp.concatenate([blocks_ref[s, 0:LAT, :] for s in range(count)], axis=1)
    clean = latents - time_ref[0] * (uncond + GUIDANCE * (cond - uncond))

    owners = jnp.concatenate(
        [blocks_ref[s, ROW_OWNER : ROW_OWNER + 1, :] for s in range(count)], axis=0
    ).astype(I32)
    earlier = (
        lax.broadcasted_iota(I32, (block, block), 0) < lax.broadcasted_iota(I32, (block, block), 1)
    ).astype(F32).astype(BF16)
    starts = lax.broadcasted_iota(I32, (count, block), 0) * capacity
    targets = []
    for step in (0, -1, 1):
        named = owners == me + step
        ranks = dot_ab(named.astype(F32).astype(BF16), earlier).astype(I32)
        slot_of = jnp.where(named, ranks + starts, -1)
        targets.append(jnp.concatenate([slot_of[s : s + 1] for s in range(count)], axis=1))
    tokens = count * block
    rows = lax.broadcasted_iota(I32, (slots, tokens), 0)
    picks = [(rows == targets[0]).astype(F32).astype(BF16)]
    small = lax.broadcasted_iota(I32, (BLK, tokens), 0)
    for step, direction in ((-1, 1), (1, 0)):
        source = jnp.clip(me + step, 0, count - 1)
        border = blocks_ref[source, ROW_BORDER : ROW_BORDER + 2, :].astype(I32)
        target = targets[1 if step < 0 else 2]
        for i in range(halo // BLK):
            wanted = border[direction : direction + 1, i : i + 1] * BLK
            picks.append((small + wanted == target).astype(F32).astype(BF16))
    picks = jnp.concatenate(picks, axis=0)
    parts = jnp.concatenate(split_three(clean), axis=0).astype(BF16)
    spread = dot_abt(parts, picks)
    table = spread[0:LAT] + spread[LAT : 2 * LAT] + spread[2 * LAT :]
    owned_ref[...] = table[:, 0:slots]

    copies[0].wait()
    proj_high, proj_low = split_two(proj_ref[...])
    table_high, table_low = split_two(table)
    left = jnp.concatenate([proj_high, proj_high, proj_low, jnp.zeros_like(proj_low)], axis=0)
    right = jnp.concatenate([table_high, table_low, table_high, jnp.zeros_like(table_low)], axis=0)
    before = dot_atb(left.astype(BF16), right.astype(BF16))
    features = (0.5 * before * (1.0 + jnp.tanh(0.5 * before))).astype(BF16)

    copies[1].wait()
    step = 9 * out_channels
    for k in range(0, offsets * out_channels, step):
        product_ref[k : k + step] = dot_ab(weight_ref[k : k + step], features).astype(BF16)

    copies[2].wait()
    fine = map_ref.shape[2]
    width = 256
    table_ids = lax.broadcasted_iota(I32, (table_rows, width), 0)
    for f in range(fine // width):
        here = slice(f * width, (f + 1) * width)
        total = jnp.zeros((out_channels, width), F32)
        for k in range(offsets):
            chosen = (table_ids == map_ref[k, :, here]).astype(F32).astype(BF16)
            products = product_ref[k * out_channels : (k + 1) * out_channels]
            total = total + dot_ab(products, chosen)
        fine_ref[:, here] = total.astype(BF16)


def swap_pair(x):
    return lax.ppermute(x, "pair", [(0, 1), (1, 0)])


def seq_swap(x, distance_of):
    count = lax.axis_size("seq")
    routes = [
        (p * count + (z ^ distance_of[p]), p * count + z) for p in range(2) for z in range(count)
    ]
    return lax.ppermute(x, ("pair", "seq"), routes)


def whole_asset_velocity(packed, modulation, in_proj, qkv_proj, norm_gain, out_proj, head_proj):
    count = lax.axis_size("seq")
    block = packed.shape[1]
    tokens = count * block
    width = in_proj.shape[1]
    inner = out_proj.shape[0]
    mixed = seq_swap(packed, (1, 2))
    far = seq_swap(packed, (3, 3))
    swapped = swap_pair(mixed)
    pos = jnp.asarray(position_parts(width))
    return pl.pallas_call(
        velocity_kernel,
        out_shape=(
            pltpu.VMEM((LAT, tokens), F32),
            pltpu.VMEM((count, PACK_ROWS, block), F32),
        ),
        in_specs=[VMEM] * 4 + [HBM] * 7,
        out_specs=(VMEM, VMEM),
        scratch_shapes=[
            pltpu.VMEM((5, 1, width), F32),
            pltpu.VMEM(in_proj.shape, F32),
            pltpu.VMEM(qkv_proj.shape, BF16),
            pltpu.VMEM(norm_gain.shape, F32),
            pltpu.VMEM(out_proj.shape, BF16),
            pltpu.VMEM((LAT, width), F32),
            pltpu.VMEM((pos.shape[0] + 32, width), BF16),
            pltpu.VMEM((tokens, width), F32),
            pltpu.VMEM((tokens, width), BF16),
            pltpu.VMEM((tokens, inner), BF16),
            pltpu.VMEM((tokens, inner), BF16),
            pltpu.VMEM((inner // 128, tokens, 256), BF16),
            pltpu.VMEM((tokens, inner), BF16),
            pltpu.SemaphoreType.DMA((7,)),
        ],
        compiler_params=pltpu.CompilerParams(vmem_limit_bytes=VMEM_GRANT),
        name="velocity",
    )(
        packed,
        mixed,
        swapped,
        far,
        *in_hbm(
            modulation[0, 0][:, None, :],
            in_proj,
            qkv_proj,
            norm_gain,
            out_proj,
            head_proj.T,
            pos,
        ),
    )


def layer_norm(values):
    center = values - jnp.mean(values, axis=-1, keepdims=True)
    variance = jnp.mean(center * center, axis=-1, keepdims=True)
    return center / jnp.sqrt(variance + EPSILON)


def position_table(coord_rows, model_width):
    freqs = model_width // 6
    steps = jnp.arange(freqs, dtype=F32) / freqs
    omegas = jnp.exp(-math.log(10000.0) * steps)
    angles = coord_rows.astype(F32)[:, :, None] * omegas[None, None, :]
    halves = jnp.concatenate([jnp.sin(angles), jnp.cos(angles)], axis=2)
    rows_out = jnp.transpose(halves, (1, 0, 2)).reshape(coord_rows.shape[1], 6 * freqs)
    return jnp.pad(rows_out, ((0, 0), (0, model_width - 6 * freqs)))


def head_norm(values, gains):
    row_count = values.shape[0]
    per_head = values.reshape(row_count, HEADS, HEAD)
    mean_square = jnp.mean(per_head * per_head, axis=2, keepdims=True)
    return (per_head / jnp.sqrt(mean_square + EPSILON)).reshape(row_count, HEADS * HEAD) * gains


def gathered_velocity(
    latent_block, coords, modulation, in_proj, qkv_proj, norm_gain, out_proj, head_proj
):
    token_count = latent_block.shape[1]
    model_width = in_proj.shape[1]
    inner_width = out_proj.shape[0]
    factor = HEAD ** (-0.5)
    mod_rows = modulation[0, 0]
    hidden = jnp.dot(latent_block.T, in_proj, precision=TOP_PRECISION) + position_table(
        coords, model_width
    )
    normed = (layer_norm(hidden) * (1.0 + mod_rows[1]) + mod_rows[0]).astype(BF16)
    projected = jnp.dot(normed, qkv_proj, preferred_element_type=F32)
    queries = head_norm(projected[:, :inner_width], norm_gain[0]).astype(BF16)
    keys_in = head_norm(projected[:, inner_width : 2 * inner_width], norm_gain[1]).astype(BF16)
    values_in = projected[:, 2 * inner_width :].astype(BF16)
    query_heads = queries.reshape(token_count, HEADS, HEAD)
    start_pair = (
        jnp.zeros((token_count, HEADS, HEAD), F32),
        jnp.zeros((token_count, HEADS), F32),
    )
    key_rows = lax.all_gather(keys_in, "seq", axis=0, tiled=True)
    value_rows = lax.all_gather(values_in, "seq", axis=0, tiled=True)
    row_count = key_rows.shape[0]
    block_rows = math.gcd(row_count, 512)
    key_blocks = key_rows.reshape(row_count // block_rows, block_rows, HEADS, HEAD)
    value_blocks = value_rows.reshape(row_count // block_rows, block_rows, HEADS, HEAD)

    def one_block(running, block_pair):
        numer_run, denom_run = running
        key_block, value_block = block_pair
        scores = (
            jnp.einsum("qhd,khd->hqk", query_heads, key_block, preferred_element_type=F32) * factor
        )
        exp_scores = jnp.exp(scores)
        numer_run = numer_run + jnp.einsum(
            "hqk,khd->qhd", exp_scores.astype(BF16), value_block, preferred_element_type=F32
        )
        denom_run = denom_run + jnp.sum(exp_scores, axis=2).T
        return ((numer_run, denom_run), None)

    (numerator, denominator), _ = lax.scan(one_block, start_pair, (key_blocks, value_blocks))
    attended = (
        (numerator / denominator[:, :, None]).reshape(token_count, inner_width).astype(BF16)
    )
    hidden = hidden + mod_rows[2] * jnp.dot(attended, out_proj, preferred_element_type=F32)
    final = layer_norm(hidden) * (1.0 + mod_rows[4]) + mod_rows[3]
    velocity = jnp.dot(final, head_proj, precision=TOP_PRECISION).T
    return lax.all_gather(velocity, "seq", axis=1, tiled=True)


def per_device(
    latents,
    voxel_coords,
    owner_map,
    step_time,
    modulation,
    in_proj,
    qkv_proj,
    norm_gain,
    out_proj,
    head_proj,
    decoder_projection,
    border_blocks,
    kernel_map,
    conv_weight,
):
    count = lax.axis_size("seq")
    block = latents.shape[2]
    packed = pl.pallas_call(
        pack_kernel,
        out_shape=pltpu.VMEM((PACK_ROWS, block), F32),
        in_specs=[HBM] * 4,
        out_specs=VMEM,
        scratch_shapes=[
            pltpu.VMEM((3, 1, block), I32),
            pltpu.VMEM((1, block), I32),
            pltpu.VMEM(border_blocks.shape[2:], I32),
            pltpu.SemaphoreType.DMA((4,)),
        ],
        compiler_params=pltpu.CompilerParams(vmem_limit_bytes=VMEM_GRANT),
        name="pack",
    )(
        *in_hbm(
            latents[0],
            jnp.swapaxes(voxel_coords, 0, 1),
            owner_map.reshape(1, block),
            border_blocks[0, 0],
        )
    )
    if count == 4 and count * block <= WHOLE_ASSET:
        velocity, blocks = whole_asset_velocity(
            packed, modulation, in_proj, qkv_proj, norm_gain, out_proj, head_proj
        )
    else:
        blocks = lax.all_gather(packed, "seq", axis=0)
        velocity = gathered_velocity(
            latents[0],
            voxel_coords[0],
            modulation,
            in_proj,
            qkv_proj,
            norm_gain,
            out_proj,
            head_proj,
        )
    partner = swap_pair(velocity)
    offsets, _, out_channels = conv_weight.shape
    fine = kernel_map.shape[3]
    slots = fine // 4
    table_rows = slots + 2 * border_blocks.shape[3] * BLK
    owned, decoded = pl.pallas_call(
        decode_kernel,
        out_shape=(
            jax.ShapeDtypeStruct((LAT, slots), F32),
            jax.ShapeDtypeStruct((out_channels, fine), BF16),
        ),
        in_specs=[VMEM, VMEM, VMEM, SMEM, HBM, HBM, HBM],
        out_specs=(VMEM, VMEM),
        scratch_shapes=[
            pltpu.VMEM(decoder_projection.shape, F32),
            pltpu.VMEM((offsets, 1, fine), I32),
            pltpu.VMEM((offsets * out_channels, decoder_projection.shape[1]), BF16),
            pltpu.VMEM((offsets * out_channels, table_rows), BF16),
            pltpu.SemaphoreType.DMA((3,)),
        ],
        compiler_params=pltpu.CompilerParams(vmem_limit_bytes=VMEM_GRANT),
        name="decode",
    )(
        blocks,
        velocity,
        partner,
        step_time,
        *in_hbm(
            decoder_projection,
            kernel_map.reshape(offsets, 1, fine),
            jnp.swapaxes(conv_weight, 1, 2).reshape(offsets * out_channels, -1),
        ),
    )
    return (owned[None, None], decoded.T[None, None])


def solution(mesh):
    placed = (
        P("asset", None, "seq"),
        P("asset", None, "seq"),
        P("asset", "seq", None),
        P("asset"),
        P("asset", "pair", None, None),
        P(),
        P(),
        P(),
        P(),
        P(),
        P(),
        P("asset", "seq", None, None),
        P("asset", "seq", None, None),
        P(None, None, "pair"),
    )
    return jax.shard_map(
        per_device,
        mesh=mesh,
        in_specs=placed,
        out_specs=(P("asset", "seq", None, None), P("asset", "seq", None, "pair")),
        check_vma=False,
    )
```

```python
import functools
import math

import jax
import jax.numpy as jnp
import numpy as np
from jax import lax
from jax.experimental import pallas as pl
from jax.experimental.pallas import tpu as pltpu
from jax.sharding import PartitionSpec as P

HEADS = 8
HEAD = 64
LAT = 8
BLK = 16
RES = 64

EPSILON = 1e-06
GUIDANCE = 3.0
TOP_PRECISION = lax.Precision.HIGHEST
F32 = jnp.float32
BF16 = jnp.bfloat16
I32 = jnp.int32

ROW_COORD = 8
ROW_OWNER = 11
ROW_BORDER = 12
PACK_ROWS = 16
WHOLE_ASSET = 512

VMEM_GRANT = 40 << 20

VMEM = pl.BlockSpec(memory_space=pltpu.VMEM)
HBM = pl.BlockSpec(memory_space=pltpu.HBM)
SMEM = pl.BlockSpec(memory_space=pltpu.SMEM)


def dot_ab(a, b):
    return jnp.dot(a, b, preferred_element_type=F32)


def dot_abt(a, b):
    return lax.dot_general(a, b, (((1,), (1,)), ((), ())), preferred_element_type=F32)


def dot_atb(a, b):
    return lax.dot_general(a, b, (((0,), (0,)), ((), ())), preferred_element_type=F32)


def in_hbm(*arrays):
    return [pltpu.with_memory_space_constraint(x, pltpu.HBM) for x in arrays]


def split_two(x):
    high = x.astype(BF16).astype(F32)
    return high, x - high


def split_three(x):
    high, rest = split_two(x)
    mid, low = split_two(rest)
    return high, mid, low


@functools.lru_cache(None)
def position_parts(model_width):
    freqs = model_width // 6
    steps = np.arange(freqs, dtype=np.float32) / np.float32(freqs)
    omegas = np.exp(np.float32(-math.log(10000.0)) * steps).astype(np.float32)
    angles = (np.arange(RES, dtype=np.float32)[:, None] * omegas[None, :]).astype(np.float64)
    halves = np.concatenate([np.sin(angles), np.cos(angles)], axis=1).astype(np.float32)
    table = np.zeros((3 * RES, model_width), np.float32)
    for c in range(3):
        table[c * RES : (c + 1) * RES, c * 2 * freqs : (c + 1) * 2 * freqs] = halves
    high = table.astype(jnp.bfloat16)
    low = (table - high.astype(np.float32)).astype(jnp.bfloat16)
    return np.concatenate([high, low], axis=0)


def pack_kernel(
    lat_hbm, coord_hbm, owner_hbm, border_hbm, pack_ref, coord_ref, owner_ref, border_ref, sems
):
    pack_ref[...] = jnp.zeros_like(pack_ref)
    copies = [
        pltpu.make_async_copy(source, target, sems.at[i])
        for i, (source, target) in enumerate(
            (
                (lat_hbm, pack_ref.at[0:LAT]),
                (coord_hbm, coord_ref),
                (owner_hbm, owner_ref),
                (border_hbm, border_ref),
            )
        )
    ]
    for copy in copies:
        copy.start()
    for copy in copies:
        copy.wait()
    for c in range(3):
        pack_ref[ROW_COORD + c : ROW_COORD + c + 1] = coord_ref[c].astype(F32)
    pack_ref[ROW_OWNER : ROW_OWNER + 1] = owner_ref[...].astype(F32)
    pack_ref[ROW_BORDER : ROW_BORDER + 2, 0 : border_ref.shape[1]] = border_ref[...].astype(F32)


def hidden_rows(rows, table_ref):
    block = rows.shape[1]
    values = lax.broadcasted_iota(I32, (RES, block), 0).astype(F32)
    hots = [
        (values == rows[ROW_COORD + c : ROW_COORD + c + 1]).astype(F32).astype(BF16)
        for c in range(3)
    ]
    high, low = split_two(rows[0:LAT])
    tail = jnp.concatenate([high, low, high, jnp.zeros_like(low)], axis=0).astype(BF16)
    return dot_atb(jnp.concatenate(hots + hots + [tail], axis=0), table_ref[...])


def modulated(hidden, mod_ref):
    center = hidden - jnp.mean(hidden, axis=1, keepdims=True)
    inverse = lax.rsqrt(jnp.mean(center * center, axis=1, keepdims=True) + EPSILON)
    return (center * inverse * (1.0 + mod_ref[1]) + mod_ref[0]).astype(BF16)


def project(normed, qkv_ref, gain_ref, query_ref, key_ref, value_ref, rows):
    inner = gain_ref.shape[1]
    group = 256
    same_head = (
        lax.broadcasted_iota(I32, (group, group), 0) // HEAD
        == lax.broadcasted_iota(I32, (group, group), 1) // HEAD
    )
    averager = jnp.where(same_head, 1.0 / HEAD, 0.0).astype(BF16)
    for j in range(3 * inner // group):
        projected = dot_ab(normed, qkv_ref[:, j * group : (j + 1) * group])
        which, col = divmod(j * group, inner)
        if which == 2:
            value_ref[col : col + group, rows] = projected.astype(BF16).T
        else:
            square = dot_ab((projected * projected).astype(BF16), averager)
            gains = gain_ref[which : which + 1, col : col + group]
            if which == 0:
                gains = gains * (HEAD**-0.5)
            result = (projected * lax.rsqrt(square + EPSILON) * gains).astype(BF16)
            (query_ref, key_ref)[which][rows, col : col + group] = result


def own_kernel(
    own_ref,
    later_ref,
    mod_hbm,
    in_hbm,
    qkv_hbm,
    gain_hbm,
    out_hbm,
    head_hbm,
    pos_hbm,
    mod_ref,
    qkv_ref,
    gain_ref,
    out_ref,
    head_ref,
    table_ref,
    hidden_ref,
    query_ref,
    key_ref,
    value_ref,
    in_ref,
    sems,
):
    pos_rows = pos_hbm.shape[0]
    copies = [
        pltpu.make_async_copy(source, target, sems.at[i])
        for i, (source, target) in enumerate(
            (
                (pos_hbm, table_ref.at[0:pos_rows]),
                (in_hbm, in_ref),
                (mod_hbm, mod_ref),
                (gain_hbm, gain_ref),
                (qkv_hbm, qkv_ref),
                (head_hbm, head_ref),
                (out_hbm, out_ref),
            )
        )
    ]
    for copy in copies:
        copy.start()
    for copy in copies[:4]:
        copy.wait()
    in_high, in_low = split_two(in_ref[...])
    table_ref[pos_rows : pos_rows + 32, :] = jnp.concatenate(
        [in_high, in_high, in_low, jnp.zeros_like(in_low)], axis=0
    ).astype(BF16)
    hidden = hidden_rows(own_ref[...], table_ref)
    hidden_ref[...] = hidden
    normed = modulated(hidden, mod_ref)
    copies[4].wait()
    block = own_ref.shape[1]
    project(normed, qkv_ref, gain_ref, query_ref, key_ref, value_ref, slice(0, block))
    copies[5].wait()
    copies[6].wait()


def velocity_kernel(
    own_ref,
    mixed_ref,
    swapped_ref,
    far_ref,
    mod_ref,
    qkv_ref,
    gain_ref,
    out_ref,
    head_ref,
    table_ref,
    own_hidden_ref,
    own_query_ref,
    own_key_ref,
    own_value_ref,
    vel_ref,
    blocks_ref,
    hidden_ref,
    normed_ref,
    query_ref,
    key_ref,
    value_ref,
    att_ref,
):
    me = lax.axis_index("seq")
    side = lax.axis_index("pair")
    width = qkv_ref.shape[0]
    tokens = hidden_ref.shape[0]
    inner = out_ref.shape[0]
    block = own_ref.shape[1]
    places = (me, me ^ (1 + side), me ^ (2 - side), me ^ 3)
    sources = (own_ref, mixed_ref, swapped_ref, far_ref)
    for place, source in zip(places, sources):
        blocks_ref[place] = source[...]

    hidden_ref[0:block, :] = own_hidden_ref[...]
    query_ref[0:block, :] = own_query_ref[...]
    key_ref[0:block, :] = own_key_ref[...]
    value_ref[:, 0:block] = own_value_ref[...]
    for s in range(1, len(sources)):
        hidden = hidden_rows(sources[s][...], table_ref)
        hidden_ref[s * block : (s + 1) * block, :] = hidden
        normed_ref[s * block : (s + 1) * block, :] = modulated(hidden, mod_ref)
    others = slice(block, tokens)
    project(normed_ref[others, :], qkv_ref, gain_ref, query_ref, key_ref, value_ref, others)

    chunk = 256
    first = lax.broadcasted_iota(I32, (tokens, 128), 1) < HEAD
    for pair in range(inner // 128):
        lanes = slice(pair * 128, (pair + 1) * 128)
        for half in range(2):
            keys = key_ref[:, lanes]
            keys = jnp.where(first == (half == 0), keys, jnp.zeros_like(keys))
            dims = slice(pair * 128 + half * HEAD, pair * 128 + (half + 1) * HEAD)
            values = jnp.concatenate(
                [value_ref[dims, :], jnp.ones((16, tokens), BF16)], axis=0
            )
            for q in range(tokens // chunk):
                here = slice(q * chunk, (q + 1) * chunk)
                scores = dot_abt(keys, query_ref[here, lanes])
                sums = dot_ab(values, jnp.exp(scores).astype(BF16))
                att_ref[dims, here] = (sums[0:HEAD] / sums[HEAD : HEAD + 1]).astype(BF16)

    gate = mod_ref[2]
    head = head_ref[...]
    offset = jnp.sum(head * mod_ref[3], axis=1, keepdims=True)
    head_high, head_low = split_two(head * (1.0 + mod_ref[4]))
    heads = jnp.concatenate([head_high, head_low], axis=0).astype(BF16)
    ones = jnp.ones((16, width), BF16)
    for s in range(len(sources)):
        here = slice(s * block, (s + 1) * block)
        hidden = hidden_ref[here, :] + gate * dot_atb(att_ref[:, here], out_ref[...])
        center = hidden - jnp.mean(hidden, axis=1, keepdims=True)
        high = center.astype(BF16)
        low = (center - high.astype(F32)).astype(BF16)
        both = dot_abt(heads, high)
        rest = dot_abt(heads, low)
        square = dot_abt(ones, (center * center).astype(BF16))
        inverse = lax.rsqrt(square[0:LAT] * (1.0 / width) + EPSILON)
        vel_ref[places[s]] = (both[0:LAT] + both[LAT:] + rest[0:LAT]) * inverse + offset


def decode_kernel(
    blocks_ref,
    mine_ref,
    other_ref,
    time_ref,
    proj_ref,
    map_ref,
    weight_ref,
    owned_ref,
    fine_ref,
    product_ref,
):
    me = lax.axis_index("seq")
    is_cond = lax.axis_index("pair") == 0
    count, _, block = blocks_ref.shape
    slots = owned_ref.shape[1]
    capacity = slots // count
    offsets = map_ref.shape[0]
    out_channels = fine_ref.shape[0]
    table_rows = product_ref.shape[1]
    halo = (table_rows - slots) // 2

    cleans = []
    for s in range(count):
        mine, other = mine_ref[s], other_ref[s]
        cond = jnp.where(is_cond, mine, other)
        uncond = jnp.where(is_cond, other, mine)
        guided = uncond + GUIDANCE * (cond - uncond)
        cleans.append(blocks_ref[s, 0:LAT, :] - time_ref[0] * guided)
    clean = jnp.concatenate(cleans, axis=1)

    owners = jnp.concatenate(
        [blocks_ref[s, ROW_OWNER : ROW_OWNER + 1, :] for s in range(count)], axis=0
    ).astype(I32)
    earlier = (
        lax.broadcasted_iota(I32, (block, block), 0) < lax.broadcasted_iota(I32, (block, block), 1)
    ).astype(F32).astype(BF16)
    starts = lax.broadcasted_iota(I32, (count, block), 0) * capacity
    targets = []
    for step in (0, -1, 1):
        named = owners == me + step
        ranks = dot_ab(named.astype(F32).astype(BF16), earlier).astype(I32)
        slot_of = jnp.where(named, ranks + starts, -1)
        targets.append(jnp.concatenate([slot_of[s : s + 1] for s in range(count)], axis=1))
    tokens = count * block
    rows = lax.broadcasted_iota(I32, (slots, tokens), 0)
    picks = [(rows == targets[0]).astype(F32).astype(BF16)]
    small = lax.broadcasted_iota(I32, (BLK, tokens), 0)
    for step, direction in ((-1, 1), (1, 0)):
        source = jnp.clip(me + step, 0, count - 1)
        border = blocks_ref[source, ROW_BORDER : ROW_BORDER + 2, :].astype(I32)
        target = targets[1 if step < 0 else 2]
        for i in range(halo // BLK):
            wanted = border[direction : direction + 1, i : i + 1] * BLK
            picks.append((small + wanted == target).astype(F32).astype(BF16))
    picks = jnp.concatenate(picks, axis=0)
    parts = jnp.concatenate(split_three(clean), axis=0).astype(BF16)
    spread = dot_abt(parts, picks)
    table = spread[0:LAT] + spread[LAT : 2 * LAT] + spread[2 * LAT :]
    owned_ref[...] = table[:, 0:slots]

    proj_high, proj_low = split_two(proj_ref[...])
    table_high, table_low = split_two(table)
    left = jnp.concatenate([proj_high, proj_high, proj_low, jnp.zeros_like(proj_low)], axis=0)
    right = jnp.concatenate([table_high, table_low, table_high, jnp.zeros_like(table_low)], axis=0)
    before = dot_atb(left.astype(BF16), right.astype(BF16))
    features = (0.5 * before * (1.0 + jnp.tanh(0.5 * before))).astype(BF16)

    step = 9 * out_channels
    for k in range(0, offsets * out_channels, step):
        product_ref[k : k + step] = dot_ab(weight_ref[k : k + step], features).astype(BF16)

    fine = map_ref.shape[2]
    width = 256
    table_ids = lax.broadcasted_iota(I32, (table_rows, width), 0)
    for f in range(fine // width):
        here = slice(f * width, (f + 1) * width)
        total = jnp.zeros((out_channels, width), F32)
        for k in range(offsets):
            chosen = (table_ids == map_ref[k, :, here]).astype(F32).astype(BF16)
            products = product_ref[k * out_channels : (k + 1) * out_channels]
            total = total + dot_ab(products, chosen)
        fine_ref[:, here] = total.astype(BF16)


def swap_pair(x):
    return lax.ppermute(x, "pair", [(0, 1), (1, 0)])


def seq_swap(x, distance_of):
    count = lax.axis_size("seq")
    routes = [
        (p * count + (z ^ distance_of[p]), p * count + z) for p in range(2) for z in range(count)
    ]
    return lax.ppermute(x, ("pair", "seq"), routes)


def whole_asset_velocity(packed, modulation, in_proj, qkv_proj, norm_gain, out_proj, head_proj):
    count = lax.axis_size("seq")
    block = packed.shape[1]
    tokens = count * block
    width = in_proj.shape[1]
    inner = out_proj.shape[0]
    mixed = seq_swap(packed, (1, 2))
    far = seq_swap(packed, (3, 3))
    swapped = swap_pair(mixed)
    pos = jnp.asarray(position_parts(width))
    held = pl.pallas_call(
        own_kernel,
        out_shape=(
            pltpu.VMEM((5, 1, width), F32),
            pltpu.VMEM(qkv_proj.shape, BF16),
            pltpu.VMEM(norm_gain.shape, F32),
            pltpu.VMEM(out_proj.shape, BF16),
            pltpu.VMEM((LAT, width), F32),
            pltpu.VMEM((pos.shape[0] + 32, width), BF16),
            pltpu.VMEM((block, width), F32),
            pltpu.VMEM((block, inner), BF16),
            pltpu.VMEM((block, inner), BF16),
            pltpu.VMEM((inner, block), BF16),
        ),
        in_specs=[VMEM] * 2 + [HBM] * 7,
        out_specs=(VMEM,) * 10,
        scratch_shapes=[
            pltpu.VMEM(in_proj.shape, F32),
            pltpu.SemaphoreType.DMA((7,)),
        ],
        compiler_params=pltpu.CompilerParams(vmem_limit_bytes=VMEM_GRANT),
        cost_estimate=pl.CostEstimate(
            flops=2 * block * width * 4 * inner, bytes_accessed=6 << 20, transcendentals=0
        ),
        name="own_block",
    )(
        packed,
        mixed,
        *in_hbm(
            modulation[0, 0][:, None, :],
            in_proj,
            qkv_proj,
            norm_gain,
            out_proj,
            head_proj.T,
            pos,
        ),
    )
    return pl.pallas_call(
        velocity_kernel,
        out_shape=(
            pltpu.VMEM((count, LAT, block), F32),
            pltpu.VMEM((count, PACK_ROWS, block), F32),
        ),
        in_specs=[VMEM] * 14,
        out_specs=(VMEM, VMEM),
        scratch_shapes=[
            pltpu.VMEM((tokens, width), F32),
            pltpu.VMEM((tokens, width), BF16),
            pltpu.VMEM((tokens, inner), BF16),
            pltpu.VMEM((tokens, inner), BF16),
            pltpu.VMEM((inner, tokens), BF16),
            pltpu.VMEM((inner, tokens), BF16),
        ],
        compiler_params=pltpu.CompilerParams(vmem_limit_bytes=VMEM_GRANT),
        name="velocity",
    )(packed, mixed, swapped, far, *held)


def layer_norm(values):
    center = values - jnp.mean(values, axis=-1, keepdims=True)
    variance = jnp.mean(center * center, axis=-1, keepdims=True)
    return center / jnp.sqrt(variance + EPSILON)


def position_table(coord_rows, model_width):
    freqs = model_width // 6
    steps = jnp.arange(freqs, dtype=F32) / freqs
    omegas = jnp.exp(-math.log(10000.0) * steps)
    angles = coord_rows.astype(F32)[:, :, None] * omegas[None, None, :]
    halves = jnp.concatenate([jnp.sin(angles), jnp.cos(angles)], axis=2)
    rows_out = jnp.transpose(halves, (1, 0, 2)).reshape(coord_rows.shape[1], 6 * freqs)
    return jnp.pad(rows_out, ((0, 0), (0, model_width - 6 * freqs)))


def head_norm(values, gains):
    row_count = values.shape[0]
    per_head = values.reshape(row_count, HEADS, HEAD)
    mean_square = jnp.mean(per_head * per_head, axis=2, keepdims=True)
    return (per_head / jnp.sqrt(mean_square + EPSILON)).reshape(row_count, HEADS * HEAD) * gains


def gathered_velocity(
    latent_block, coords, modulation, in_proj, qkv_proj, norm_gain, out_proj, head_proj
):
    token_count = latent_block.shape[1]
    model_width = in_proj.shape[1]
    inner_width = out_proj.shape[0]
    factor = HEAD ** (-0.5)
    mod_rows = modulation[0, 0]
    hidden = jnp.dot(latent_block.T, in_proj, precision=TOP_PRECISION) + position_table(
        coords, model_width
    )
    normed = (layer_norm(hidden) * (1.0 + mod_rows[1]) + mod_rows[0]).astype(BF16)
    projected = jnp.dot(normed, qkv_proj, preferred_element_type=F32)
    queries = head_norm(projected[:, :inner_width], norm_gain[0]).astype(BF16)
    keys_in = head_norm(projected[:, inner_width : 2 * inner_width], norm_gain[1]).astype(BF16)
    values_in = projected[:, 2 * inner_width :].astype(BF16)
    query_heads = queries.reshape(token_count, HEADS, HEAD)
    start_pair = (
        jnp.zeros((token_count, HEADS, HEAD), F32),
        jnp.zeros((token_count, HEADS), F32),
    )
    key_rows = lax.all_gather(keys_in, "seq", axis=0, tiled=True)
    value_rows = lax.all_gather(values_in, "seq", axis=0, tiled=True)
    row_count = key_rows.shape[0]
    block_rows = math.gcd(row_count, 512)
    key_blocks = key_rows.reshape(row_count // block_rows, block_rows, HEADS, HEAD)
    value_blocks = value_rows.reshape(row_count // block_rows, block_rows, HEADS, HEAD)

    def one_block(running, block_pair):
        numer_run, denom_run = running
        key_block, value_block = block_pair
        scores = (
            jnp.einsum("qhd,khd->hqk", query_heads, key_block, preferred_element_type=F32) * factor
        )
        exp_scores = jnp.exp(scores)
        numer_run = numer_run + jnp.einsum(
            "hqk,khd->qhd", exp_scores.astype(BF16), value_block, preferred_element_type=F32
        )
        denom_run = denom_run + jnp.sum(exp_scores, axis=2).T
        return ((numer_run, denom_run), None)

    (numerator, denominator), _ = lax.scan(one_block, start_pair, (key_blocks, value_blocks))
    attended = (
        (numerator / denominator[:, :, None]).reshape(token_count, inner_width).astype(BF16)
    )
    hidden = hidden + mod_rows[2] * jnp.dot(attended, out_proj, preferred_element_type=F32)
    final = layer_norm(hidden) * (1.0 + mod_rows[4]) + mod_rows[3]
    velocity = jnp.dot(final, head_proj, precision=TOP_PRECISION).T
    return lax.all_gather(velocity, "seq", axis=0)


def per_device(
    latents,
    voxel_coords,
    owner_map,
    step_time,
    modulation,
    in_proj,
    qkv_proj,
    norm_gain,
    out_proj,
    head_proj,
    decoder_projection,
    border_blocks,
    kernel_map,
    conv_weight,
):
    count = lax.axis_size("seq")
    block = latents.shape[2]
    packed = pl.pallas_call(
        pack_kernel,
        out_shape=pltpu.VMEM((PACK_ROWS, block), F32),
        in_specs=[HBM] * 4,
        out_specs=VMEM,
        scratch_shapes=[
            pltpu.VMEM((3, 1, block), I32),
            pltpu.VMEM((1, block), I32),
            pltpu.VMEM(border_blocks.shape[2:], I32),
            pltpu.SemaphoreType.DMA((4,)),
        ],
        compiler_params=pltpu.CompilerParams(vmem_limit_bytes=VMEM_GRANT),
        name="pack",
    )(
        *in_hbm(
            latents[0],
            jnp.swapaxes(voxel_coords, 0, 1),
            owner_map.reshape(1, block),
            border_blocks[0, 0],
        )
    )
    if count == 4 and count * block <= WHOLE_ASSET:
        velocity, blocks = whole_asset_velocity(
            packed, modulation, in_proj, qkv_proj, norm_gain, out_proj, head_proj
        )
    else:
        blocks = lax.all_gather(packed, "seq", axis=0)
        velocity = gathered_velocity(
            latents[0],
            voxel_coords[0],
            modulation,
            in_proj,
            qkv_proj,
            norm_gain,
            out_proj,
            head_proj,
        )
    partner = swap_pair(velocity)
    offsets, _, out_channels = conv_weight.shape
    fine = kernel_map.shape[3]
    slots = fine // 4
    table_rows = slots + 2 * border_blocks.shape[3] * BLK
    owned, decoded = pl.pallas_call(
        decode_kernel,
        out_shape=(
            jax.ShapeDtypeStruct((LAT, slots), F32),
            jax.ShapeDtypeStruct((out_channels, fine), BF16),
        ),
        in_specs=[VMEM, VMEM, VMEM, SMEM, VMEM, VMEM, VMEM],
        out_specs=(VMEM, VMEM),
        scratch_shapes=[pltpu.VMEM((offsets * out_channels, table_rows), BF16)],
        compiler_params=pltpu.CompilerParams(vmem_limit_bytes=VMEM_GRANT),
        name="decode",
    )(
        blocks,
        velocity,
        partner,
        step_time,
        decoder_projection,
        kernel_map.reshape(offsets, 1, fine),
        jnp.swapaxes(conv_weight, 1, 2).reshape(offsets * out_channels, -1),
    )
    return (owned[None, None], decoded.T[None, None])


def solution(mesh):
    placed = (
        P("asset", None, "seq"),
        P("asset", None, "seq"),
        P("asset", "seq", None),
        P("asset"),
        P("asset", "pair", None, None),
        P(),
        P(),
        P(),
        P(),
        P(),
        P(),
        P("asset", "seq", None, None),
        P("asset", "seq", None, None),
        P(None, None, "pair"),
    )
    return jax.shard_map(
        per_device,
        mesh=mesh,
        in_specs=placed,
        out_specs=(P("asset", "seq", None, None), P("asset", "seq", None, "pair")),
        check_vma=False,
    )
```

```python
import functools
import math

import jax
import jax.numpy as jnp
import numpy as np
from jax import lax
from jax.experimental import pallas as pl
from jax.experimental.pallas import tpu as pltpu
from jax.sharding import PartitionSpec as P

HEADS = 8
HEAD = 64
LAT = 8
BLK = 16
RES = 64

EPSILON = 1e-06
GUIDANCE = 3.0
TOP_PRECISION = lax.Precision.HIGHEST
F32 = jnp.float32
BF16 = jnp.bfloat16
I32 = jnp.int32

ROW_COORD = 8
ROW_OWNER = 11
ROW_BORDER = 12
PACK_ROWS = 16
WHOLE_ASSET = 512

VMEM_GRANT = 40 << 20

VMEM = pl.BlockSpec(memory_space=pltpu.VMEM)
HBM = pl.BlockSpec(memory_space=pltpu.HBM)
SMEM = pl.BlockSpec(memory_space=pltpu.SMEM)


def dot_ab(a, b):
    return jnp.dot(a, b, preferred_element_type=F32)


def dot_abt(a, b):
    return lax.dot_general(a, b, (((1,), (1,)), ((), ())), preferred_element_type=F32)


def dot_atb(a, b):
    return lax.dot_general(a, b, (((0,), (0,)), ((), ())), preferred_element_type=F32)


def in_hbm(*arrays):
    return [pltpu.with_memory_space_constraint(x, pltpu.HBM) for x in arrays]


def split_two(x):
    high = x.astype(BF16).astype(F32)
    return high, x - high


def split_three(x):
    high, rest = split_two(x)
    mid, low = split_two(rest)
    return high, mid, low


@functools.lru_cache(None)
def position_parts(model_width):
    freqs = model_width // 6
    steps = np.arange(freqs, dtype=np.float32) / np.float32(freqs)
    omegas = np.exp(np.float32(-math.log(10000.0)) * steps).astype(np.float32)
    angles = (np.arange(RES, dtype=np.float32)[:, None] * omegas[None, :]).astype(np.float64)
    halves = np.concatenate([np.sin(angles), np.cos(angles)], axis=1).astype(np.float32)
    table = np.zeros((3 * RES, model_width), np.float32)
    for c in range(3):
        table[c * RES : (c + 1) * RES, c * 2 * freqs : (c + 1) * 2 * freqs] = halves
    high = table.astype(jnp.bfloat16)
    low = (table - high.astype(np.float32)).astype(jnp.bfloat16)
    return np.concatenate([high, low], axis=0)


def pack_kernel(
    lat_hbm, coord_hbm, owner_hbm, border_hbm, pack_ref, coord_ref, owner_ref, border_ref, sems
):
    pack_ref[...] = jnp.zeros_like(pack_ref)
    copies = [
        pltpu.make_async_copy(source, target, sems.at[i])
        for i, (source, target) in enumerate(
            (
                (lat_hbm, pack_ref.at[0:LAT]),
                (coord_hbm, coord_ref),
                (owner_hbm, owner_ref),
                (border_hbm, border_ref),
            )
        )
    ]
    for copy in copies:
        copy.start()
    for copy in copies:
        copy.wait()
    for c in range(3):
        pack_ref[ROW_COORD + c : ROW_COORD + c + 1] = coord_ref[c].astype(F32)
    pack_ref[ROW_OWNER : ROW_OWNER + 1] = owner_ref[...].astype(F32)
    pack_ref[ROW_BORDER : ROW_BORDER + 2, 0 : border_ref.shape[1]] = border_ref[...].astype(F32)


def hidden_rows(rows, table_ref):
    block = rows.shape[1]
    values = lax.broadcasted_iota(I32, (RES, block), 0).astype(F32)
    hots = [
        (values == rows[ROW_COORD + c : ROW_COORD + c + 1]).astype(F32).astype(BF16)
        for c in range(3)
    ]
    high, low = split_two(rows[0:LAT])
    tail = jnp.concatenate([high, low, high, jnp.zeros_like(low)], axis=0).astype(BF16)
    return dot_atb(jnp.concatenate(hots + hots + [tail], axis=0), table_ref[...])


def modulated(hidden, mod_ref):
    center = hidden - jnp.mean(hidden, axis=1, keepdims=True)
    inverse = lax.rsqrt(jnp.mean(center * center, axis=1, keepdims=True) + EPSILON)
    return (center * inverse * (1.0 + mod_ref[1]) + mod_ref[0]).astype(BF16)


def project(normed, qkv_ref, gain_ref, query_ref, key_ref, value_ref, rows):
    inner = gain_ref.shape[1]
    group = 256
    same_head = (
        lax.broadcasted_iota(I32, (group, group), 0) // HEAD
        == lax.broadcasted_iota(I32, (group, group), 1) // HEAD
    )
    averager = jnp.where(same_head, 1.0 / HEAD, 0.0).astype(BF16)

    def finish(j, projected):
        which, col = divmod(j * group, inner)
        if which == 2:
            for half in range(group // 128):
                lanes = slice(half * 128, (half + 1) * 128)
                value_ref[col // 128 + half, rows, 0:128] = projected[:, lanes].astype(BF16)
        else:
            square = dot_ab((projected * projected).astype(BF16), averager)
            gains = gain_ref[which : which + 1, col : col + group]
            if which == 0:
                gains = gains * (HEAD**-0.5)
            result = (projected * lax.rsqrt(square + EPSILON) * gains).astype(BF16)
            (query_ref, key_ref)[which][rows, col : col + group] = result

    previous = None
    for j in range(3 * inner // group):
        projected = dot_ab(normed, qkv_ref[:, j * group : (j + 1) * group])
        if previous is not None:
            finish(*previous)
        previous = (j, projected)
    finish(*previous)


def own_kernel(
    own_ref,
    later_ref,
    mod_hbm,
    in_hbm,
    qkv_hbm,
    gain_hbm,
    out_hbm,
    head_hbm,
    pos_hbm,
    mod_ref,
    qkv_ref,
    gain_ref,
    out_ref,
    head_ref,
    table_ref,
    hidden_ref,
    query_ref,
    key_ref,
    value_ref,
    in_ref,
    sems,
):
    pos_rows = pos_hbm.shape[0]
    copies = [
        pltpu.make_async_copy(source, target, sems.at[i])
        for i, (source, target) in enumerate(
            (
                (pos_hbm, table_ref.at[0:pos_rows]),
                (in_hbm, in_ref),
                (mod_hbm, mod_ref),
                (gain_hbm, gain_ref),
                (qkv_hbm, qkv_ref),
                (head_hbm, head_ref),
                (out_hbm, out_ref),
            )
        )
    ]
    for copy in copies:
        copy.start()
    for copy in copies[:4]:
        copy.wait()
    in_high, in_low = split_two(in_ref[...])
    table_ref[pos_rows : pos_rows + 32, :] = jnp.concatenate(
        [in_high, in_high, in_low, jnp.zeros_like(in_low)], axis=0
    ).astype(BF16)
    hidden = hidden_rows(own_ref[...], table_ref)
    hidden_ref[...] = hidden
    normed = modulated(hidden, mod_ref)
    copies[4].wait()
    block = own_ref.shape[1]
    project(normed, qkv_ref, gain_ref, query_ref, key_ref, value_ref, slice(0, block))
    copies[5].wait()
    copies[6].wait()


def velocity_kernel(
    own_ref,
    mixed_ref,
    swapped_ref,
    far_ref,
    mod_ref,
    qkv_ref,
    gain_ref,
    out_ref,
    head_ref,
    table_ref,
    own_hidden_ref,
    own_query_ref,
    own_key_ref,
    own_value_ref,
    vel_ref,
    blocks_ref,
    hidden_ref,
    normed_ref,
    query_ref,
    key_ref,
    value_ref,
    att_ref,
):
    me = lax.axis_index("seq")
    side = lax.axis_index("pair")
    width = qkv_ref.shape[0]
    tokens = hidden_ref.shape[0]
    inner = out_ref.shape[0]
    block = own_ref.shape[1]
    places = (me, me ^ (1 + side), me ^ (2 - side), me ^ 3)
    sources = (own_ref, mixed_ref, swapped_ref, far_ref)
    for place, source in zip(places, sources):
        blocks_ref[place] = source[...]

    hidden_ref[0:block, :] = own_hidden_ref[...]
    query_ref[0:block, :] = own_query_ref[...]
    key_ref[0:block, :] = own_key_ref[...]
    for pair in range(inner // 128):
        value_ref[pair, 0:block, 0:128] = own_value_ref[pair]
    value_ref[:, :, 128:256] = jnp.ones((inner // 128, tokens, 128), BF16)
    ready = hidden_rows(sources[1][...], table_ref)
    for s in range(1, len(sources)):
        hidden = ready
        if s + 1 < len(sources):
            ready = hidden_rows(sources[s + 1][...], table_ref)
        hidden_ref[s * block : (s + 1) * block, :] = hidden
        normed_ref[s * block : (s + 1) * block, :] = modulated(hidden, mod_ref)
    others = slice(block, tokens)
    project(normed_ref[others, :], qkv_ref, gain_ref, query_ref, key_ref, value_ref, others)

    chunk = 256
    first = lax.broadcasted_iota(I32, (chunk, 128), 1) < HEAD
    todo = [(pair, q, half) for pair in range(inner // 128) for q in range(tokens // chunk) for half in range(2)]
    def score(pair, q, half):
        lanes = slice(pair * 128, (pair + 1) * 128)
        query = query_ref[q * chunk : (q + 1) * chunk, lanes]
        kept = jnp.where(first == (half == 0), query, jnp.zeros_like(query))
        return dot_abt(kept, key_ref[:, lanes])
    ready = score(*todo[0])
    parts = []
    for at, (pair, q, half) in enumerate(todo):
        scores = ready
        if at + 1 < len(todo):
            ready = score(*todo[at + 1])
        sums = dot_ab(jnp.exp(scores).astype(BF16), value_ref[pair])
        parts.append(sums[:, 0:128] / sums[:, 128:256])
        if half == 1:
            att_ref[q * chunk : (q + 1) * chunk, pair * 128 : (pair + 1) * 128] = jnp.where(first, parts[0], parts[1]).astype(BF16)
            parts = []

    gate = mod_ref[2]
    head = head_ref[...]
    offset = jnp.sum(head * mod_ref[3], axis=1, keepdims=True)
    head_high, head_low = split_two(head * (1.0 + mod_ref[4]))
    heads = jnp.concatenate([head_high, head_low], axis=0).astype(BF16)
    ones = jnp.ones((16, width), BF16)
    step = 128
    def attended(q):
        return dot_ab(att_ref[q * step : (q + 1) * step, :], out_ref[...])
    def middle(q, product):
        hidden = hidden_ref[q * step : (q + 1) * step, :] + gate * product
        center = hidden - jnp.mean(hidden, axis=1, keepdims=True)
        high = center.astype(BF16)
        low = (center - high.astype(F32)).astype(BF16)
        return high, low
    def last(q, high, low):
        both = dot_abt(heads, high)
        rest = dot_abt(heads, low)
        square = dot_abt(ones, high * high)
        inverse = lax.rsqrt(square[0:LAT] * (1.0 / width) + EPSILON)
        velocity = (both[0:LAT] + both[LAT:] + rest[0:LAT]) * inverse + offset
        for i in range(step // block):
            vel_ref[places[q * (step // block) + i]] = velocity[:, i * block : (i + 1) * block]
    count = tokens // step
    product = attended(0)
    waiting = None
    for q in range(count):
        following = attended(q + 1) if q + 1 < count else None
        centered = middle(q, product)
        if waiting is not None:
            last(*waiting)
        waiting = (q, *centered)
        product = following
    last(*waiting)


def decode_kernel(
    blocks_ref,
    mine_ref,
    other_ref,
    time_ref,
    proj_ref,
    map_ref,
    weight_ref,
    owned_ref,
    fine_ref,
    product_ref,
):
    me = lax.axis_index("seq")
    is_cond = lax.axis_index("pair") == 0
    count, _, block = blocks_ref.shape
    slots = owned_ref.shape[1]
    capacity = slots // count
    offsets = map_ref.shape[0]
    out_channels = fine_ref.shape[0]
    table_rows = product_ref.shape[1]
    halo = (table_rows - slots) // 2

    cleans = []
    for s in range(count):
        mine, other = mine_ref[s], other_ref[s]
        cond = jnp.where(is_cond, mine, other)
        uncond = jnp.where(is_cond, other, mine)
        guided = uncond + GUIDANCE * (cond - uncond)
        cleans.append(blocks_ref[s, 0:LAT, :] - time_ref[0] * guided)
    clean = jnp.concatenate(cleans, axis=1)

    owners = jnp.concatenate(
        [blocks_ref[s, ROW_OWNER : ROW_OWNER + 1, :] for s in range(count)], axis=0
    ).astype(I32)
    earlier = (
        lax.broadcasted_iota(I32, (block, block), 0) < lax.broadcasted_iota(I32, (block, block), 1)
    ).astype(F32).astype(BF16)
    starts = lax.broadcasted_iota(I32, (count, block), 0) * capacity
    targets = []
    for step in (0, -1, 1):
        named = owners == me + step
        ranks = dot_ab(named.astype(F32).astype(BF16), earlier).astype(I32)
        slot_of = jnp.where(named, ranks + starts, -1)
        targets.append(jnp.concatenate([slot_of[s : s + 1] for s in range(count)], axis=1))
    tokens = count * block
    rows = lax.broadcasted_iota(I32, (slots, tokens), 0)
    picks = [(rows == targets[0]).astype(F32).astype(BF16)]
    small = lax.broadcasted_iota(I32, (BLK, tokens), 0)
    for step, direction in ((-1, 1), (1, 0)):
        source = jnp.clip(me + step, 0, count - 1)
        border = blocks_ref[source, ROW_BORDER : ROW_BORDER + 2, :].astype(I32)
        target = targets[1 if step < 0 else 2]
        for i in range(halo // BLK):
            wanted = border[direction : direction + 1, i : i + 1] * BLK
            picks.append((small + wanted == target).astype(F32).astype(BF16))
    picks = jnp.concatenate(picks, axis=0)
    parts = jnp.concatenate(split_three(clean), axis=0).astype(BF16)
    spread = dot_abt(parts, picks)
    table = spread[0:LAT] + spread[LAT : 2 * LAT] + spread[2 * LAT :]
    owned_ref[...] = table[:, 0:slots]

    proj_high, proj_low = split_two(proj_ref[...])
    table_high, table_low = split_two(table)
    left = jnp.concatenate([proj_high, proj_high, proj_low, jnp.zeros_like(proj_low)], axis=0)
    right = jnp.concatenate([table_high, table_low, table_high, jnp.zeros_like(table_low)], axis=0)
    before = dot_atb(left.astype(BF16), right.astype(BF16))
    features = (0.5 * before * (1.0 + jnp.tanh(0.5 * before))).astype(BF16)

    step = 9 * out_channels
    for k in range(0, offsets * out_channels, step):
        product_ref[k : k + step] = dot_ab(weight_ref[k : k + step], features).astype(BF16)

    fine = map_ref.shape[2]
    width = 256
    table_ids = lax.broadcasted_iota(I32, (table_rows, width), 0)
    for f in range(fine // width):
        here = slice(f * width, (f + 1) * width)
        total = jnp.zeros((out_channels, width), F32)
        for k in range(offsets):
            chosen = (table_ids == map_ref[k, :, here]).astype(F32).astype(BF16)
            products = product_ref[k * out_channels : (k + 1) * out_channels]
            total = total + dot_ab(products, chosen)
        fine_ref[:, here] = total.astype(BF16)


def swap_pair(x):
    return lax.ppermute(x, "pair", [(0, 1), (1, 0)])


def seq_swap(x, distance_of):
    count = lax.axis_size("seq")
    routes = [
        (p * count + (z ^ distance_of[p]), p * count + z) for p in range(2) for z in range(count)
    ]
    return lax.ppermute(x, ("pair", "seq"), routes)


def whole_asset_velocity(packed, modulation, in_proj, qkv_proj, norm_gain, out_proj, head_proj):
    count = lax.axis_size("seq")
    block = packed.shape[1]
    tokens = count * block
    width = in_proj.shape[1]
    inner = out_proj.shape[0]
    far = seq_swap(packed, (3, 3))
    mixed = seq_swap(packed, (1, 2))
    swapped = swap_pair(mixed)
    pos = jnp.asarray(position_parts(width))
    held = pl.pallas_call(
        own_kernel,
        out_shape=(
            pltpu.VMEM((5, 1, width), F32),
            pltpu.VMEM(qkv_proj.shape, BF16),
            pltpu.VMEM(norm_gain.shape, F32),
            pltpu.VMEM(out_proj.shape, BF16),
            pltpu.VMEM((LAT, width), F32),
            pltpu.VMEM((pos.shape[0] + 32, width), BF16),
            pltpu.VMEM((block, width), F32),
            pltpu.VMEM((block, inner), BF16),
            pltpu.VMEM((block, inner), BF16),
            pltpu.VMEM((inner // 128, block, 128), BF16),
        ),
        in_specs=[VMEM] * 2 + [HBM] * 7,
        out_specs=(VMEM,) * 10,
        scratch_shapes=[
            pltpu.VMEM(in_proj.shape, F32),
            pltpu.SemaphoreType.DMA((7,)),
        ],
        compiler_params=pltpu.CompilerParams(vmem_limit_bytes=VMEM_GRANT),
        cost_estimate=pl.CostEstimate(
            flops=2 * block * width * 4 * inner, bytes_accessed=6 << 20, transcendentals=0
        ),
        name="own_block",
    )(
        packed,
        mixed,
        *in_hbm(
            modulation[0, 0][:, None, :],
            in_proj,
            qkv_proj,
            norm_gain,
            out_proj,
            head_proj.T,
            pos,
        ),
    )
    return pl.pallas_call(
        velocity_kernel,
        out_shape=(
            pltpu.VMEM((count, LAT, block), F32),
            pltpu.VMEM((count, PACK_ROWS, block), F32),
        ),
        in_specs=[VMEM] * 14,
        out_specs=(VMEM, VMEM),
        scratch_shapes=[
            pltpu.VMEM((tokens, width), F32),
            pltpu.VMEM((tokens, width), BF16),
            pltpu.VMEM((tokens, inner), BF16),
            pltpu.VMEM((tokens, inner), BF16),
            pltpu.VMEM((inner // 128, tokens, 256), BF16),
            pltpu.VMEM((tokens, inner), BF16),
        ],
        compiler_params=pltpu.CompilerParams(vmem_limit_bytes=VMEM_GRANT),
        name="velocity",
    )(packed, mixed, swapped, far, *held)


def layer_norm(values):
    center = values - jnp.mean(values, axis=-1, keepdims=True)
    variance = jnp.mean(center * center, axis=-1, keepdims=True)
    return center / jnp.sqrt(variance + EPSILON)


def position_table(coord_rows, model_width):
    freqs = model_width // 6
    steps = jnp.arange(freqs, dtype=F32) / freqs
    omegas = jnp.exp(-math.log(10000.0) * steps)
    angles = coord_rows.astype(F32)[:, :, None] * omegas[None, None, :]
    halves = jnp.concatenate([jnp.sin(angles), jnp.cos(angles)], axis=2)
    rows_out = jnp.transpose(halves, (1, 0, 2)).reshape(coord_rows.shape[1], 6 * freqs)
    return jnp.pad(rows_out, ((0, 0), (0, model_width - 6 * freqs)))


def head_norm(values, gains):
    row_count = values.shape[0]
    per_head = values.reshape(row_count, HEADS, HEAD)
    mean_square = jnp.mean(per_head * per_head, axis=2, keepdims=True)
    return (per_head / jnp.sqrt(mean_square + EPSILON)).reshape(row_count, HEADS * HEAD) * gains


def gathered_velocity(
    latent_block, coords, modulation, in_proj, qkv_proj, norm_gain, out_proj, head_proj
):
    token_count = latent_block.shape[1]
    model_width = in_proj.shape[1]
    inner_width = out_proj.shape[0]
    factor = HEAD ** (-0.5)
    mod_rows = modulation[0, 0]
    hidden = jnp.dot(latent_block.T, in_proj, precision=TOP_PRECISION) + position_table(
        coords, model_width
    )
    normed = (layer_norm(hidden) * (1.0 + mod_rows[1]) + mod_rows[0]).astype(BF16)
    projected = jnp.dot(normed, qkv_proj, preferred_element_type=F32)
    queries = head_norm(projected[:, :inner_width], norm_gain[0]).astype(BF16)
    keys_in = head_norm(projected[:, inner_width : 2 * inner_width], norm_gain[1]).astype(BF16)
    values_in = projected[:, 2 * inner_width :].astype(BF16)
    query_heads = queries.reshape(token_count, HEADS, HEAD)
    start_pair = (
        jnp.zeros((token_count, HEADS, HEAD), F32),
        jnp.zeros((token_count, HEADS), F32),
    )
    key_rows = lax.all_gather(keys_in, "seq", axis=0, tiled=True)
    value_rows = lax.all_gather(values_in, "seq", axis=0, tiled=True)
    row_count = key_rows.shape[0]
    block_rows = math.gcd(row_count, 512)
    key_blocks = key_rows.reshape(row_count // block_rows, block_rows, HEADS, HEAD)
    value_blocks = value_rows.reshape(row_count // block_rows, block_rows, HEADS, HEAD)

    def one_block(running, block_pair):
        numer_run, denom_run = running
        key_block, value_block = block_pair
        scores = (
            jnp.einsum("qhd,khd->hqk", query_heads, key_block, preferred_element_type=F32) * factor
        )
        exp_scores = jnp.exp(scores)
        numer_run = numer_run + jnp.einsum(
            "hqk,khd->qhd", exp_scores.astype(BF16), value_block, preferred_element_type=F32
        )
        denom_run = denom_run + jnp.sum(exp_scores, axis=2).T
        return ((numer_run, denom_run), None)

    (numerator, denominator), _ = lax.scan(one_block, start_pair, (key_blocks, value_blocks))
    attended = (
        (numerator / denominator[:, :, None]).reshape(token_count, inner_width).astype(BF16)
    )
    hidden = hidden + mod_rows[2] * jnp.dot(attended, out_proj, preferred_element_type=F32)
    final = layer_norm(hidden) * (1.0 + mod_rows[4]) + mod_rows[3]
    velocity = jnp.dot(final, head_proj, precision=TOP_PRECISION).T
    return lax.all_gather(velocity, "seq", axis=0)


def per_device(
    latents,
    voxel_coords,
    owner_map,
    step_time,
    modulation,
    in_proj,
    qkv_proj,
    norm_gain,
    out_proj,
    head_proj,
    decoder_projection,
    border_blocks,
    kernel_map,
    conv_weight,
):
    count = lax.axis_size("seq")
    block = latents.shape[2]
    packed = pl.pallas_call(
        pack_kernel,
        out_shape=pltpu.VMEM((PACK_ROWS, block), F32),
        in_specs=[HBM] * 4,
        out_specs=VMEM,
        scratch_shapes=[
            pltpu.VMEM((3, 1, block), I32),
            pltpu.VMEM((1, block), I32),
            pltpu.VMEM(border_blocks.shape[2:], I32),
            pltpu.SemaphoreType.DMA((4,)),
        ],
        compiler_params=pltpu.CompilerParams(vmem_limit_bytes=VMEM_GRANT),
        name="pack",
    )(
        *in_hbm(
            latents[0],
            jnp.swapaxes(voxel_coords, 0, 1),
            owner_map.reshape(1, block),
            border_blocks[0, 0],
        )
    )
    if count == 4 and count * block <= WHOLE_ASSET:
        velocity, blocks = whole_asset_velocity(
            packed, modulation, in_proj, qkv_proj, norm_gain, out_proj, head_proj
        )
    else:
        blocks = lax.all_gather(packed, "seq", axis=0)
        velocity = gathered_velocity(
            latents[0],
            voxel_coords[0],
            modulation,
            in_proj,
            qkv_proj,
            norm_gain,
            out_proj,
            head_proj,
        )
    partner = swap_pair(velocity)
    offsets, _, out_channels = conv_weight.shape
    fine = kernel_map.shape[3]
    slots = fine // 4
    table_rows = slots + 2 * border_blocks.shape[3] * BLK
    owned, decoded = pl.pallas_call(
        decode_kernel,
        out_shape=(
            jax.ShapeDtypeStruct((LAT, slots), F32),
            jax.ShapeDtypeStruct((out_channels, fine), BF16),
        ),
        in_specs=[VMEM, VMEM, VMEM, SMEM, VMEM, VMEM, VMEM],
        out_specs=(VMEM, VMEM),
        scratch_shapes=[pltpu.VMEM((offsets * out_channels, table_rows), BF16)],
        compiler_params=pltpu.CompilerParams(vmem_limit_bytes=VMEM_GRANT),
        name="decode",
    )(
        blocks,
        velocity,
        partner,
        step_time,
        decoder_projection,
        kernel_map.reshape(offsets, 1, fine),
        jnp.swapaxes(conv_weight, 1, 2).reshape(offsets * out_channels, -1),
    )
    return (owned[None, None], decoded.T[None, None])


def solution(mesh):
    placed = (
        P("asset", None, "seq"),
        P("asset", None, "seq"),
        P("asset", "seq", None),
        P("asset"),
        P("asset", "pair", None, None),
        P(),
        P(),
        P(),
        P(),
        P(),
        P(),
        P("asset", "seq", None, None),
        P("asset", "seq", None, None),
        P(None, None, "pair"),
    )
    return jax.shard_map(
        per_device,
        mesh=mesh,
        in_specs=placed,
        out_specs=(P("asset", "seq", None, None), P("asset", "seq", None, "pair")),
        check_vma=False,
    )
```

```python
import functools
import math

import jax
import jax.numpy as jnp
import numpy as np
from jax import lax
from jax.experimental import pallas as pl
from jax.experimental.pallas import tpu as pltpu
from jax.sharding import PartitionSpec as P

HEADS = 8
HEAD = 64
LAT = 8
BLK = 16
RES = 64

EPSILON = 1e-06
GUIDANCE = 3.0
TOP_PRECISION = lax.Precision.HIGHEST
F32 = jnp.float32
BF16 = jnp.bfloat16
I32 = jnp.int32
F8 = jnp.float8_e4m3fn
CODE_TOP = 256.0
TINY = 1e-30

ROW_COORD = 8
ROW_OWNER = 11
ROW_BORDER = 12
PACK_ROWS = 16
WHOLE_ASSET = 512

VMEM_GRANT = 40 << 20

VMEM = pl.BlockSpec(memory_space=pltpu.VMEM)
HBM = pl.BlockSpec(memory_space=pltpu.HBM)
SMEM = pl.BlockSpec(memory_space=pltpu.SMEM)


def dot_ab(a, b):
    return jnp.dot(a, b, preferred_element_type=F32)


def dot_abt(a, b):
    return lax.dot_general(a, b, (((1,), (1,)), ((), ())), preferred_element_type=F32)


def dot_atb(a, b):
    return lax.dot_general(a, b, (((0,), (0,)), ((), ())), preferred_element_type=F32)


def in_hbm(*arrays):
    return [pltpu.with_memory_space_constraint(x, pltpu.HBM) for x in arrays]


def split_two(x):
    high = x.astype(BF16).astype(F32)
    return high, x - high


def split_three(x):
    high, rest = split_two(x)
    mid, low = split_two(rest)
    return high, mid, low


@functools.lru_cache(None)
def position_parts(model_width):
    freqs = model_width // 6
    steps = np.arange(freqs, dtype=np.float32) / np.float32(freqs)
    omegas = np.exp(np.float32(-math.log(10000.0)) * steps).astype(np.float32)
    angles = (np.arange(RES, dtype=np.float32)[:, None] * omegas[None, :]).astype(np.float64)
    halves = np.concatenate([np.sin(angles), np.cos(angles)], axis=1).astype(np.float32)
    table = np.zeros((3 * RES, model_width), np.float32)
    for c in range(3):
        table[c * RES : (c + 1) * RES, c * 2 * freqs : (c + 1) * 2 * freqs] = halves
    high = table.astype(jnp.bfloat16)
    low = (table - high.astype(np.float32)).astype(jnp.bfloat16)
    return np.concatenate([high, low], axis=0)


def pack_kernel(
    lat_hbm, coord_hbm, owner_hbm, border_hbm, pack_ref, coord_ref, owner_ref, border_ref, sems
):
    pack_ref[...] = jnp.zeros_like(pack_ref)
    copies = [
        pltpu.make_async_copy(source, target, sems.at[i])
        for i, (source, target) in enumerate(
            (
                (lat_hbm, pack_ref.at[0:LAT]),
                (coord_hbm, coord_ref),
                (owner_hbm, owner_ref),
                (border_hbm, border_ref),
            )
        )
    ]
    for copy in copies:
        copy.start()
    for copy in copies:
        copy.wait()
    for c in range(3):
        pack_ref[ROW_COORD + c : ROW_COORD + c + 1] = coord_ref[c].astype(F32)
    pack_ref[ROW_OWNER : ROW_OWNER + 1] = owner_ref[...].astype(F32)
    pack_ref[ROW_BORDER : ROW_BORDER + 2, 0 : border_ref.shape[1]] = border_ref[...].astype(F32)


def hidden_rows(rows, table_ref):
    block = rows.shape[1]
    values = lax.broadcasted_iota(I32, (RES, block), 0).astype(F32)
    hots = [
        (values == rows[ROW_COORD + c : ROW_COORD + c + 1]).astype(F32).astype(BF16)
        for c in range(3)
    ]
    high, low = split_two(rows[0:LAT])
    tail = jnp.concatenate([high, low, high, jnp.zeros_like(low)], axis=0).astype(BF16)
    return dot_atb(jnp.concatenate(hots + hots + [tail], axis=0), table_ref[...])


def modulated(hidden, mod_ref):
    center = hidden - jnp.mean(hidden, axis=1, keepdims=True)
    inverse = lax.rsqrt(jnp.mean(center * center, axis=1, keepdims=True) + EPSILON)
    return (center * inverse * (1.0 + mod_ref[1]) + mod_ref[0]).astype(BF16)


def project(normed, qkv_ref, gain_ref, query_ref, key_ref, value_ref, rows):
    inner = gain_ref.shape[1]
    group = 256
    same_head = (
        lax.broadcasted_iota(I32, (group, group), 0) // HEAD
        == lax.broadcasted_iota(I32, (group, group), 1) // HEAD
    )
    averager = jnp.where(same_head, 1.0 / HEAD, 0.0).astype(BF16)

    def finish(j, projected):
        which, col = divmod(j * group, inner)
        if which == 2:
            for half in range(group // 128):
                lanes = slice(half * 128, (half + 1) * 128)
                value_ref[col // 128 + half, rows, 0:128] = projected[:, lanes].astype(BF16)
        else:
            square = dot_ab((projected * projected).astype(BF16), averager)
            gains = gain_ref[which : which + 1, col : col + group]
            if which == 0:
                gains = gains * (HEAD**-0.5)
            result = (projected * lax.rsqrt(square + EPSILON) * gains).astype(BF16)
            (query_ref, key_ref)[which][rows, col : col + group] = result

    previous = None
    for j in range(3 * inner // group):
        projected = dot_ab(normed, qkv_ref[:, j * group : (j + 1) * group])
        if previous is not None:
            finish(*previous)
        previous = (j, projected)
    finish(*previous)


def own_kernel(
    own_ref,
    later_ref,
    mod_hbm,
    in_hbm,
    qkv_hbm,
    gain_hbm,
    out_hbm,
    head_hbm,
    pos_hbm,
    mod_ref,
    qkv_ref,
    gain_ref,
    out_ref,
    head_ref,
    table_ref,
    hidden_ref,
    query_ref,
    key_ref,
    value_ref,
    in_ref,
    sems,
):
    pos_rows = pos_hbm.shape[0]
    copies = [
        pltpu.make_async_copy(source, target, sems.at[i])
        for i, (source, target) in enumerate(
            (
                (pos_hbm, table_ref.at[0:pos_rows]),
                (in_hbm, in_ref),
                (mod_hbm, mod_ref),
                (gain_hbm, gain_ref),
                (qkv_hbm, qkv_ref),
                (head_hbm, head_ref),
                (out_hbm, out_ref),
            )
        )
    ]
    for copy in copies:
        copy.start()
    for copy in copies[:4]:
        copy.wait()
    in_high, in_low = split_two(in_ref[...])
    table_ref[pos_rows : pos_rows + 32, :] = jnp.concatenate(
        [in_high, in_high, in_low, jnp.zeros_like(in_low)], axis=0
    ).astype(BF16)
    hidden = hidden_rows(own_ref[...], table_ref)
    hidden_ref[...] = hidden
    normed = modulated(hidden, mod_ref)
    copies[4].wait()
    block = own_ref.shape[1]
    project(normed, qkv_ref, gain_ref, query_ref, key_ref, value_ref, slice(0, block))
    copies[5].wait()
    copies[6].wait()


def velocity_kernel(
    own_ref,
    mixed_ref,
    swapped_ref,
    far_ref,
    mod_ref,
    qkv_ref,
    gain_ref,
    out_ref,
    head_ref,
    table_ref,
    own_hidden_ref,
    own_query_ref,
    own_key_ref,
    own_value_ref,
    vel_ref,
    blocks_ref,
    hidden_ref,
    normed_ref,
    query_ref,
    key_ref,
    value_ref,
    att_ref,
):
    me = lax.axis_index("seq")
    side = lax.axis_index("pair")
    width = qkv_ref.shape[0]
    tokens = hidden_ref.shape[0]
    inner = out_ref.shape[0]
    block = own_ref.shape[1]
    places = (me, me ^ (1 + side), me ^ (2 - side), me ^ 3)
    sources = (own_ref, mixed_ref, swapped_ref, far_ref)
    for place, source in zip(places, sources):
        blocks_ref[place] = source[...]

    hidden_ref[0:block, :] = own_hidden_ref[...]
    query_ref[0:block, :] = own_query_ref[...]
    key_ref[0:block, :] = own_key_ref[...]
    for pair in range(inner // 128):
        value_ref[pair, 0:block, 0:128] = own_value_ref[pair]
    value_ref[:, :, 128:256] = jnp.ones((inner // 128, tokens, 128), BF16)
    ready = hidden_rows(sources[1][...], table_ref)
    for s in range(1, len(sources)):
        hidden = ready
        if s + 1 < len(sources):
            ready = hidden_rows(sources[s + 1][...], table_ref)
        hidden_ref[s * block : (s + 1) * block, :] = hidden
        normed_ref[s * block : (s + 1) * block, :] = modulated(hidden, mod_ref)
    others = slice(block, tokens)
    project(normed_ref[others, :], qkv_ref, gain_ref, query_ref, key_ref, value_ref, others)

    chunk = 256
    first = lax.broadcasted_iota(I32, (chunk, 128), 1) < HEAD
    todo = [(pair, q, half) for pair in range(inner // 128) for q in range(tokens // chunk) for half in range(2)]
    def score(pair, q, half):
        lanes = slice(pair * 128, (pair + 1) * 128)
        query = query_ref[q * chunk : (q + 1) * chunk, lanes]
        kept = jnp.where(first == (half == 0), query, jnp.zeros_like(query))
        return dot_abt(kept, key_ref[:, lanes])
    ready = score(*todo[0])
    parts = []
    for at, (pair, q, half) in enumerate(todo):
        scores = ready
        if at + 1 < len(todo):
            ready = score(*todo[at + 1])
        sums = dot_ab(jnp.exp(scores).astype(BF16), value_ref[pair])
        parts.append(sums[:, 0:128] / sums[:, 128:256])
        if half == 1:
            att_ref[q * chunk : (q + 1) * chunk, pair * 128 : (pair + 1) * 128] = jnp.where(first, parts[0], parts[1]).astype(BF16)
            parts = []

    gate = mod_ref[2]
    head = head_ref[...]
    offset = jnp.sum(head * mod_ref[3], axis=1, keepdims=True)
    head_high, head_low = split_two(head * (1.0 + mod_ref[4]))
    heads = jnp.concatenate([head_high, head_low], axis=0).astype(BF16)
    ones = jnp.ones((16, width), BF16)
    step = 128
    def attended(q):
        return dot_ab(att_ref[q * step : (q + 1) * step, :], out_ref[...])
    def middle(q, product):
        hidden = hidden_ref[q * step : (q + 1) * step, :] + gate * product
        center = hidden - jnp.mean(hidden, axis=1, keepdims=True)
        high = center.astype(BF16)
        low = (center - high.astype(F32)).astype(BF16)
        return high, low
    def last(q, high, low):
        both = dot_abt(heads, high)
        rest = dot_abt(heads, low)
        square = dot_abt(ones, high * high)
        inverse = lax.rsqrt(square[0:LAT] * (1.0 / width) + EPSILON)
        velocity = (both[0:LAT] + both[LAT:] + rest[0:LAT]) * inverse + offset
        for i in range(step // block):
            vel_ref[places[q * (step // block) + i]] = velocity[:, i * block : (i + 1) * block]
    count = tokens // step
    product = attended(0)
    waiting = None
    for q in range(count):
        following = attended(q + 1) if q + 1 < count else None
        centered = middle(q, product)
        if waiting is not None:
            last(*waiting)
        waiting = (q, *centered)
        product = following
    last(*waiting)


def decode_kernel(
    blocks_ref,
    mine_ref,
    other_ref,
    time_ref,
    proj_ref,
    map_ref,
    weight_ref,
    owned_ref,
    fine_ref,
    code_ref,
):
    me = lax.axis_index("seq")
    is_cond = lax.axis_index("pair") == 0
    count, _, block = blocks_ref.shape
    slots = owned_ref.shape[1]
    capacity = slots // count
    offsets = map_ref.shape[0]
    out_channels = fine_ref.shape[0]
    table_rows = code_ref.shape[2]
    halo = (table_rows - slots) // 2

    cleans = []
    for s in range(count):
        mine, other = mine_ref[s], other_ref[s]
        cond = jnp.where(is_cond, mine, other)
        uncond = jnp.where(is_cond, other, mine)
        guided = uncond + GUIDANCE * (cond - uncond)
        cleans.append(blocks_ref[s, 0:LAT, :] - time_ref[0] * guided)
    clean = jnp.concatenate(cleans, axis=1)

    owners = jnp.concatenate(
        [blocks_ref[s, ROW_OWNER : ROW_OWNER + 1, :] for s in range(count)], axis=0
    ).astype(I32)
    earlier = (
        lax.broadcasted_iota(I32, (block, block), 0) < lax.broadcasted_iota(I32, (block, block), 1)
    ).astype(F32).astype(BF16)
    starts = lax.broadcasted_iota(I32, (count, block), 0) * capacity
    targets = []
    for step in (0, -1, 1):
        named = owners == me + step
        ranks = dot_ab(named.astype(F32).astype(BF16), earlier).astype(I32)
        slot_of = jnp.where(named, ranks + starts, -1)
        targets.append(jnp.concatenate([slot_of[s : s + 1] for s in range(count)], axis=1))
    tokens = count * block
    rows = lax.broadcasted_iota(I32, (slots, tokens), 0)
    picks = [(rows == targets[0]).astype(F32).astype(BF16)]
    small = lax.broadcasted_iota(I32, (BLK, tokens), 0)
    for step, direction in ((-1, 1), (1, 0)):
        source = jnp.clip(me + step, 0, count - 1)
        border = blocks_ref[source, ROW_BORDER : ROW_BORDER + 2, :].astype(I32)
        target = targets[1 if step < 0 else 2]
        for i in range(halo // BLK):
            wanted = border[direction : direction + 1, i : i + 1] * BLK
            picks.append((small + wanted == target).astype(F32).astype(BF16))
    picks = jnp.concatenate(picks, axis=0)
    parts = jnp.concatenate(split_three(clean), axis=0).astype(BF16)
    spread = dot_abt(parts, picks)
    table = spread[0:LAT] + spread[LAT : 2 * LAT] + spread[2 * LAT :]
    owned_ref[...] = table[:, 0:slots]

    proj_high, proj_low = split_two(proj_ref[...])
    table_high, table_low = split_two(table)
    left = jnp.concatenate([proj_high, proj_high, proj_low, jnp.zeros_like(proj_low)], axis=0)
    right = jnp.concatenate([table_high, table_low, table_high, jnp.zeros_like(table_low)], axis=0)
    before = dot_atb(left.astype(BF16), right.astype(BF16))
    features = (0.5 * before * (1.0 + jnp.tanh(0.5 * before))).astype(BF16)

    count = 3
    groups = [range(k, min(k + count, offsets)) for k in range(0, offsets, count)]

    def multiply(group):
        rows = weight_ref[group[0] * out_channels : (group[-1] + 1) * out_channels]
        return dot_ab(rows, features)

    def code(group, product):
        top = jnp.max(jnp.abs(product), axis=0, keepdims=True)
        top = jnp.maximum(jnp.max(top, axis=1, keepdims=True), TINY)
        scaled = product * (CODE_TOP / top)
        high = scaled.astype(F8)
        low = (scaled - high.astype(F32)).astype(F8)
        for i, k in enumerate(group):
            rows = slice(i * out_channels, (i + 1) * out_channels)
            code_ref[k, 0:out_channels] = high[rows]
            code_ref[k, out_channels : 2 * out_channels] = low[rows]
        return top * (1.0 / CODE_TOP)

    units = []
    ready = multiply(groups[0])
    for i, group in enumerate(groups):
        product = ready
        if i + 1 < len(groups):
            ready = multiply(groups[i + 1])
        units.append(code(group, product))

    fine = map_ref.shape[2]
    width = 256
    table_ids = lax.broadcasted_iota(jnp.int16, (table_rows, width), 0)
    one = jnp.ones((table_rows, width), F8)
    zero = jnp.zeros((table_rows, width), F8)
    for f in range(fine // width):
        here = slice(f * width, (f + 1) * width)
        total = jnp.zeros((out_channels, width), F32)
        for group, unit in zip(groups, units):
            part = jnp.zeros((2 * out_channels, width), F32)
            for k in group:
                index = jnp.broadcast_to(map_ref[k, :, here], (16, width)).astype(jnp.int16)
                index = jnp.broadcast_to(index[None], (table_rows // 16, 16, width))
                chosen = jnp.where(table_ids == index.reshape(table_rows, width), one, zero)
                part = part + dot_ab(code_ref[k], chosen)
            total = total + (part[0:out_channels] + part[out_channels:]) * unit
        fine_ref[:, here] = total.astype(BF16)


def decode_call(blocks, velocity, partner, step_time, decoder_projection, index_rows, weights):
    offsets, _, fine = index_rows.shape
    out_channels = weights.shape[0] // offsets
    slots = fine // 4
    table_rows = 2 * slots
    return pl.pallas_call(
        decode_kernel,
        out_shape=(
            jax.ShapeDtypeStruct((LAT, slots), F32),
            jax.ShapeDtypeStruct((out_channels, fine), BF16),
        ),
        in_specs=[VMEM, VMEM, VMEM, SMEM, VMEM, VMEM, VMEM],
        out_specs=(VMEM, VMEM),
        scratch_shapes=[pltpu.VMEM((offsets, 2 * out_channels, table_rows), F8)],
        compiler_params=pltpu.CompilerParams(vmem_limit_bytes=VMEM_GRANT),
        name="decode",
    )(blocks, velocity, partner, step_time, decoder_projection, index_rows, weights)


def swap_pair(x):
    return lax.ppermute(x, "pair", [(0, 1), (1, 0)])


def seq_swap(x, distance_of):
    count = lax.axis_size("seq")
    routes = [
        (p * count + (z ^ distance_of[p]), p * count + z) for p in range(2) for z in range(count)
    ]
    return lax.ppermute(x, ("pair", "seq"), routes)


def whole_asset_velocity(packed, modulation, in_proj, qkv_proj, norm_gain, out_proj, head_proj):
    count = lax.axis_size("seq")
    block = packed.shape[1]
    tokens = count * block
    width = in_proj.shape[1]
    inner = out_proj.shape[0]
    far = seq_swap(packed, (3, 3))
    mixed = seq_swap(packed, (1, 2))
    swapped = swap_pair(mixed)
    pos = jnp.asarray(position_parts(width))
    held = pl.pallas_call(
        own_kernel,
        out_shape=(
            pltpu.VMEM((5, 1, width), F32),
            pltpu.VMEM(qkv_proj.shape, BF16),
            pltpu.VMEM(norm_gain.shape, F32),
            pltpu.VMEM(out_proj.shape, BF16),
            pltpu.VMEM((LAT, width), F32),
            pltpu.VMEM((pos.shape[0] + 32, width), BF16),
            pltpu.VMEM((block, width), F32),
            pltpu.VMEM((block, inner), BF16),
            pltpu.VMEM((block, inner), BF16),
            pltpu.VMEM((inner // 128, block, 128), BF16),
        ),
        in_specs=[VMEM] * 2 + [HBM] * 7,
        out_specs=(VMEM,) * 10,
        scratch_shapes=[
            pltpu.VMEM(in_proj.shape, F32),
            pltpu.SemaphoreType.DMA((7,)),
        ],
        compiler_params=pltpu.CompilerParams(vmem_limit_bytes=VMEM_GRANT),
        cost_estimate=pl.CostEstimate(
            flops=2 * block * width * 4 * inner, bytes_accessed=6 << 20, transcendentals=0
        ),
        name="own_block",
    )(
        packed,
        mixed,
        *in_hbm(
            modulation[0, 0][:, None, :],
            in_proj,
            qkv_proj,
            norm_gain,
            out_proj,
            head_proj.T,
            pos,
        ),
    )
    return pl.pallas_call(
        velocity_kernel,
        out_shape=(
            pltpu.VMEM((count, LAT, block), F32),
            pltpu.VMEM((count, PACK_ROWS, block), F32),
        ),
        in_specs=[VMEM] * 14,
        out_specs=(VMEM, VMEM),
        scratch_shapes=[
            pltpu.VMEM((tokens, width), F32),
            pltpu.VMEM((tokens, width), BF16),
            pltpu.VMEM((tokens, inner), BF16),
            pltpu.VMEM((tokens, inner), BF16),
            pltpu.VMEM((inner // 128, tokens, 256), BF16),
            pltpu.VMEM((tokens, inner), BF16),
        ],
        compiler_params=pltpu.CompilerParams(vmem_limit_bytes=VMEM_GRANT),
        name="velocity",
    )(packed, mixed, swapped, far, *held)


def layer_norm(values):
    center = values - jnp.mean(values, axis=-1, keepdims=True)
    variance = jnp.mean(center * center, axis=-1, keepdims=True)
    return center / jnp.sqrt(variance + EPSILON)


def position_table(coord_rows, model_width):
    freqs = model_width // 6
    steps = jnp.arange(freqs, dtype=F32) / freqs
    omegas = jnp.exp(-math.log(10000.0) * steps)
    angles = coord_rows.astype(F32)[:, :, None] * omegas[None, None, :]
    halves = jnp.concatenate([jnp.sin(angles), jnp.cos(angles)], axis=2)
    rows_out = jnp.transpose(halves, (1, 0, 2)).reshape(coord_rows.shape[1], 6 * freqs)
    return jnp.pad(rows_out, ((0, 0), (0, model_width - 6 * freqs)))


def head_norm(values, gains):
    row_count = values.shape[0]
    per_head = values.reshape(row_count, HEADS, HEAD)
    mean_square = jnp.mean(per_head * per_head, axis=2, keepdims=True)
    return (per_head / jnp.sqrt(mean_square + EPSILON)).reshape(row_count, HEADS * HEAD) * gains


def gathered_velocity(
    latent_block, coords, modulation, in_proj, qkv_proj, norm_gain, out_proj, head_proj
):
    token_count = latent_block.shape[1]
    model_width = in_proj.shape[1]
    inner_width = out_proj.shape[0]
    factor = HEAD ** (-0.5)
    mod_rows = modulation[0, 0]
    hidden = jnp.dot(latent_block.T, in_proj, precision=TOP_PRECISION) + position_table(
        coords, model_width
    )
    normed = (layer_norm(hidden) * (1.0 + mod_rows[1]) + mod_rows[0]).astype(BF16)
    projected = jnp.dot(normed, qkv_proj, preferred_element_type=F32)
    queries = head_norm(projected[:, :inner_width], norm_gain[0]).astype(BF16)
    keys_in = head_norm(projected[:, inner_width : 2 * inner_width], norm_gain[1]).astype(BF16)
    values_in = projected[:, 2 * inner_width :].astype(BF16)
    query_heads = queries.reshape(token_count, HEADS, HEAD)
    start_pair = (
        jnp.zeros((token_count, HEADS, HEAD), F32),
        jnp.zeros((token_count, HEADS), F32),
    )
    key_rows = lax.all_gather(keys_in, "seq", axis=0, tiled=True)
    value_rows = lax.all_gather(values_in, "seq", axis=0, tiled=True)
    row_count = key_rows.shape[0]
    block_rows = math.gcd(row_count, 512)
    key_blocks = key_rows.reshape(row_count // block_rows, block_rows, HEADS, HEAD)
    value_blocks = value_rows.reshape(row_count // block_rows, block_rows, HEADS, HEAD)

    def one_block(running, block_pair):
        numer_run, denom_run = running
        key_block, value_block = block_pair
        scores = (
            jnp.einsum("qhd,khd->hqk", query_heads, key_block, preferred_element_type=F32) * factor
        )
        exp_scores = jnp.exp(scores)
        numer_run = numer_run + jnp.einsum(
            "hqk,khd->qhd", exp_scores.astype(BF16), value_block, preferred_element_type=F32
        )
        denom_run = denom_run + jnp.sum(exp_scores, axis=2).T
        return ((numer_run, denom_run), None)

    (numerator, denominator), _ = lax.scan(one_block, start_pair, (key_blocks, value_blocks))
    attended = (
        (numerator / denominator[:, :, None]).reshape(token_count, inner_width).astype(BF16)
    )
    hidden = hidden + mod_rows[2] * jnp.dot(attended, out_proj, preferred_element_type=F32)
    final = layer_norm(hidden) * (1.0 + mod_rows[4]) + mod_rows[3]
    velocity = jnp.dot(final, head_proj, precision=TOP_PRECISION).T
    return lax.all_gather(velocity, "seq", axis=0)


def per_device(
    latents,
    voxel_coords,
    owner_map,
    step_time,
    modulation,
    in_proj,
    qkv_proj,
    norm_gain,
    out_proj,
    head_proj,
    decoder_projection,
    border_blocks,
    kernel_map,
    conv_weight,
):
    count = lax.axis_size("seq")
    block = latents.shape[2]
    packed = pl.pallas_call(
        pack_kernel,
        out_shape=pltpu.VMEM((PACK_ROWS, block), F32),
        in_specs=[HBM] * 4,
        out_specs=VMEM,
        scratch_shapes=[
            pltpu.VMEM((3, 1, block), I32),
            pltpu.VMEM((1, block), I32),
            pltpu.VMEM(border_blocks.shape[2:], I32),
            pltpu.SemaphoreType.DMA((4,)),
        ],
        compiler_params=pltpu.CompilerParams(vmem_limit_bytes=VMEM_GRANT),
        name="pack",
    )(
        *in_hbm(
            latents[0],
            jnp.swapaxes(voxel_coords, 0, 1),
            owner_map.reshape(1, block),
            border_blocks[0, 0],
        )
    )
    if count == 4 and count * block <= WHOLE_ASSET:
        velocity, blocks = whole_asset_velocity(
            packed, modulation, in_proj, qkv_proj, norm_gain, out_proj, head_proj
        )
    else:
        blocks = lax.all_gather(packed, "seq", axis=0)
        velocity = gathered_velocity(
            latents[0],
            voxel_coords[0],
            modulation,
            in_proj,
            qkv_proj,
            norm_gain,
            out_proj,
            head_proj,
        )
    partner = swap_pair(velocity)
    offsets, _, out_channels = conv_weight.shape
    fine = kernel_map.shape[3]
    owned, decoded = decode_call(
        blocks,
        velocity,
        partner,
        step_time,
        decoder_projection,
        kernel_map.reshape(offsets, 1, fine),
        jnp.swapaxes(conv_weight, 1, 2).reshape(offsets * out_channels, -1),
    )
    return (owned[None, None], decoded.T[None, None])


def solution(mesh):
    placed = (
        P("asset", None, "seq"),
        P("asset", None, "seq"),
        P("asset", "seq", None),
        P("asset"),
        P("asset", "pair", None, None),
        P(),
        P(),
        P(),
        P(),
        P(),
        P(),
        P("asset", "seq", None, None),
        P("asset", "seq", None, None),
        P(None, None, "pair"),
    )
    return jax.shard_map(
        per_device,
        mesh=mesh,
        in_specs=placed,
        out_specs=(P("asset", "seq", None, None), P("asset", "seq", None, "pair")),
        check_vma=False,
    )
```

```python
import functools
import math

import jax
import jax.numpy as jnp
import numpy as np
from jax import lax
from jax.experimental import pallas as pl
from jax.experimental.pallas import tpu as pltpu
from jax.sharding import PartitionSpec as P

HEADS = 8
HEAD = 64
LAT = 8
BLK = 16
RES = 64

EPSILON = 1e-06
GUIDANCE = 3.0
TOP_PRECISION = lax.Precision.HIGHEST
F32 = jnp.float32
BF16 = jnp.bfloat16
I32 = jnp.int32
F8 = jnp.float8_e4m3fn
CODE_TOP = 256.0
TINY = 1e-30

ROW_COORD = 8
ROW_OWNER = 11
ROW_BORDER = 12
PACK_ROWS = 16
WHOLE_ASSET = 512

VMEM_GRANT = 40 << 20

VMEM = pl.BlockSpec(memory_space=pltpu.VMEM)
HBM = pl.BlockSpec(memory_space=pltpu.HBM)
SMEM = pl.BlockSpec(memory_space=pltpu.SMEM)


def dot_ab(a, b):
    return jnp.dot(a, b, preferred_element_type=F32)


def dot_abt(a, b):
    return lax.dot_general(a, b, (((1,), (1,)), ((), ())), preferred_element_type=F32)


def dot_atb(a, b):
    return lax.dot_general(a, b, (((0,), (0,)), ((), ())), preferred_element_type=F32)


def in_hbm(*arrays):
    return [pltpu.with_memory_space_constraint(x, pltpu.HBM) for x in arrays]


def split_two(x):
    high = x.astype(BF16).astype(F32)
    return high, x - high


def split_three(x):
    high, rest = split_two(x)
    mid, low = split_two(rest)
    return high, mid, low


@functools.lru_cache(None)
def position_parts(model_width):
    freqs = model_width // 6
    steps = np.arange(freqs, dtype=np.float32) / np.float32(freqs)
    omegas = np.exp(np.float32(-math.log(10000.0)) * steps).astype(np.float32)
    angles = (np.arange(RES, dtype=np.float32)[:, None] * omegas[None, :]).astype(np.float64)
    halves = np.concatenate([np.sin(angles), np.cos(angles)], axis=1).astype(np.float32)
    table = np.zeros((3 * RES, model_width), np.float32)
    for c in range(3):
        table[c * RES : (c + 1) * RES, c * 2 * freqs : (c + 1) * 2 * freqs] = halves
    high = table.astype(jnp.bfloat16)
    low = (table - high.astype(np.float32)).astype(jnp.bfloat16)
    return np.concatenate([high, low], axis=0)


def pack_kernel(
    lat_hbm, coord_hbm, owner_hbm, border_hbm, pack_ref, coord_ref, owner_ref, border_ref, sems
):
    pack_ref[...] = jnp.zeros_like(pack_ref)
    copies = [
        pltpu.make_async_copy(source, target, sems.at[i])
        for i, (source, target) in enumerate(
            (
                (lat_hbm, pack_ref.at[0:LAT]),
                (coord_hbm, coord_ref),
                (owner_hbm, owner_ref),
                (border_hbm, border_ref),
            )
        )
    ]
    for copy in copies:
        copy.start()
    for copy in copies:
        copy.wait()
    for c in range(3):
        pack_ref[ROW_COORD + c : ROW_COORD + c + 1] = coord_ref[c].astype(F32)
    pack_ref[ROW_OWNER : ROW_OWNER + 1] = owner_ref[...].astype(F32)
    pack_ref[ROW_BORDER : ROW_BORDER + 2, 0 : border_ref.shape[1]] = border_ref[...].astype(F32)


def hidden_rows(rows, table_ref):
    block = rows.shape[1]
    values = lax.broadcasted_iota(I32, (RES, block), 0).astype(F32)
    hots = [
        (values == rows[ROW_COORD + c : ROW_COORD + c + 1]).astype(F32).astype(BF16)
        for c in range(3)
    ]
    high, low = split_two(rows[0:LAT])
    tail = jnp.concatenate([high, low, high, jnp.zeros_like(low)], axis=0).astype(BF16)
    return dot_atb(jnp.concatenate(hots + hots + [tail], axis=0), table_ref[...])


def modulated(hidden, mod_ref):
    center = hidden - jnp.mean(hidden, axis=1, keepdims=True)
    inverse = lax.rsqrt(jnp.mean(center * center, axis=1, keepdims=True) + EPSILON)
    return (center * inverse * (1.0 + mod_ref[1]) + mod_ref[0]).astype(BF16)


def project(normed, qkv_ref, gain_ref, query_ref, key_ref, value_ref, rows):
    inner = gain_ref.shape[1]
    group = 256
    same_head = (
        lax.broadcasted_iota(I32, (group, group), 0) // HEAD
        == lax.broadcasted_iota(I32, (group, group), 1) // HEAD
    )
    averager = jnp.where(same_head, 1.0 / HEAD, 0.0).astype(BF16)

    def finish(j, projected):
        which, col = divmod(j * group, inner)
        if which == 2:
            for half in range(group // 128):
                lanes = slice(half * 128, (half + 1) * 128)
                value_ref[col // 128 + half, rows, 0:128] = projected[:, lanes].astype(BF16)
        else:
            square = dot_ab((projected * projected).astype(BF16), averager)
            gains = gain_ref[which : which + 1, col : col + group]
            if which == 0:
                gains = gains * (HEAD**-0.5)
            result = (projected * lax.rsqrt(square + EPSILON) * gains).astype(BF16)
            (query_ref, key_ref)[which][rows, col : col + group] = result

    previous = None
    for j in range(3 * inner // group):
        projected = dot_ab(normed, qkv_ref[:, j * group : (j + 1) * group])
        if previous is not None:
            finish(*previous)
        previous = (j, projected)
    finish(*previous)


def own_kernel(
    own_ref,
    later_ref,
    mod_hbm,
    in_hbm,
    qkv_hbm,
    gain_hbm,
    out_hbm,
    head_hbm,
    pos_hbm,
    mod_ref,
    qkv_ref,
    gain_ref,
    out_ref,
    head_ref,
    table_ref,
    hidden_ref,
    query_ref,
    key_ref,
    value_ref,
    in_ref,
    sems,
):
    pos_rows = pos_hbm.shape[0]
    copies = [
        pltpu.make_async_copy(source, target, sems.at[i])
        for i, (source, target) in enumerate(
            (
                (pos_hbm, table_ref.at[0:pos_rows]),
                (in_hbm, in_ref),
                (mod_hbm, mod_ref),
                (gain_hbm, gain_ref),
                (qkv_hbm, qkv_ref),
                (head_hbm, head_ref),
                (out_hbm, out_ref),
            )
        )
    ]
    for copy in copies:
        copy.start()
    for copy in copies[:4]:
        copy.wait()
    in_high, in_low = split_two(in_ref[...])
    table_ref[pos_rows : pos_rows + 32, :] = jnp.concatenate(
        [in_high, in_high, in_low, jnp.zeros_like(in_low)], axis=0
    ).astype(BF16)
    hidden = hidden_rows(own_ref[...], table_ref)
    hidden_ref[...] = hidden
    normed = modulated(hidden, mod_ref)
    copies[4].wait()
    block = own_ref.shape[1]
    project(normed, qkv_ref, gain_ref, query_ref, key_ref, value_ref, slice(0, block))
    copies[5].wait()
    copies[6].wait()


def velocity_kernel(
    own_ref,
    mixed_ref,
    swapped_ref,
    far_ref,
    mod_ref,
    qkv_ref,
    gain_ref,
    out_ref,
    head_ref,
    table_ref,
    own_hidden_ref,
    own_query_ref,
    own_key_ref,
    own_value_ref,
    vel_ref,
    blocks_ref,
    hidden_ref,
    normed_ref,
    query_ref,
    key_ref,
    value_ref,
    att_ref,
):
    me = lax.axis_index("seq")
    side = lax.axis_index("pair")
    width = qkv_ref.shape[0]
    tokens = hidden_ref.shape[0]
    inner = out_ref.shape[0]
    block = own_ref.shape[1]
    places = (me, me ^ (1 + side), me ^ (2 - side), me ^ 3)
    sources = (own_ref, mixed_ref, swapped_ref, far_ref)
    for place, source in zip(places, sources):
        blocks_ref[place] = source[...]

    hidden_ref[0:block, :] = own_hidden_ref[...]
    query_ref[0:block, :] = own_query_ref[...]
    key_ref[0:block, :] = own_key_ref[...]
    for pair in range(inner // 128):
        value_ref[pair, 0:block, 0:128] = own_value_ref[pair]
    value_ref[:, :, 128:256] = jnp.ones((inner // 128, tokens, 128), BF16)
    ready = hidden_rows(sources[1][...], table_ref)
    for s in range(1, len(sources)):
        hidden = ready
        if s + 1 < len(sources):
            ready = hidden_rows(sources[s + 1][...], table_ref)
        hidden_ref[s * block : (s + 1) * block, :] = hidden
        normed_ref[s * block : (s + 1) * block, :] = modulated(hidden, mod_ref)
    others = slice(block, tokens)
    project(normed_ref[others, :], qkv_ref, gain_ref, query_ref, key_ref, value_ref, others)

    chunk = 256
    first = lax.broadcasted_iota(I32, (chunk, 128), 1) < HEAD
    todo = [(pair, q, half) for pair in range(inner // 128) for q in range(tokens // chunk) for half in range(2)]
    def score(pair, q, half):
        lanes = slice(pair * 128, (pair + 1) * 128)
        query = query_ref[q * chunk : (q + 1) * chunk, lanes]
        kept = jnp.where(first == (half == 0), query, jnp.zeros_like(query))
        return dot_abt(kept, key_ref[:, lanes])
    ready = score(*todo[0])
    parts = []
    for at, (pair, q, half) in enumerate(todo):
        scores = ready
        if at + 1 < len(todo):
            ready = score(*todo[at + 1])
        sums = dot_ab(jnp.exp(scores).astype(BF16), value_ref[pair])
        parts.append(sums[:, 0:128] / sums[:, 128:256])
        if half == 1:
            att_ref[q * chunk : (q + 1) * chunk, pair * 128 : (pair + 1) * 128] = jnp.where(first, parts[0], parts[1]).astype(BF16)
            parts = []

    gate = mod_ref[2]
    head = head_ref[...]
    offset = jnp.sum(head * mod_ref[3], axis=1, keepdims=True)
    head_high, head_low = split_two(head * (1.0 + mod_ref[4]))
    heads = jnp.concatenate([head_high, head_low], axis=0).astype(BF16)
    ones = jnp.ones((16, width), BF16)
    step = 128
    def attended(q):
        return dot_ab(att_ref[q * step : (q + 1) * step, :], out_ref[...])
    def middle(q, product):
        hidden = hidden_ref[q * step : (q + 1) * step, :] + gate * product
        center = hidden - jnp.mean(hidden, axis=1, keepdims=True)
        high = center.astype(BF16)
        low = (center - high.astype(F32)).astype(BF16)
        return high, low
    def last(q, high, low):
        both = dot_abt(heads, high)
        rest = dot_abt(heads, low)
        square = dot_abt(ones, high * high)
        inverse = lax.rsqrt(square[0:LAT] * (1.0 / width) + EPSILON)
        velocity = (both[0:LAT] + both[LAT:] + rest[0:LAT]) * inverse + offset
        for i in range(step // block):
            vel_ref[places[q * (step // block) + i]] = velocity[:, i * block : (i + 1) * block]
    count = tokens // step
    product = attended(0)
    waiting = None
    for q in range(count):
        following = attended(q + 1) if q + 1 < count else None
        centered = middle(q, product)
        if waiting is not None:
            last(*waiting)
        waiting = (q, *centered)
        product = following
    last(*waiting)


def route_kernel(blocks_ref, picks_ref):
    me = lax.axis_index("seq")
    count, _, block = blocks_ref.shape
    table_rows = picks_ref.shape[0]
    slots = table_rows // 2
    capacity = slots // count
    halo = (table_rows - slots) // 2

    owners = jnp.concatenate(
        [blocks_ref[s, ROW_OWNER : ROW_OWNER + 1, :] for s in range(count)], axis=0
    ).astype(I32)
    earlier = (
        lax.broadcasted_iota(I32, (block, block), 0) < lax.broadcasted_iota(I32, (block, block), 1)
    ).astype(F32).astype(BF16)
    starts = lax.broadcasted_iota(I32, (count, block), 0) * capacity
    targets = []
    for step in (0, -1, 1):
        named = owners == me + step
        ranks = dot_ab(named.astype(F32).astype(BF16), earlier).astype(I32)
        slot_of = jnp.where(named, ranks + starts, -1)
        targets.append(jnp.concatenate([slot_of[s : s + 1] for s in range(count)], axis=1))
    tokens = count * block
    rows = lax.broadcasted_iota(I32, (slots, tokens), 0)
    picks_ref[0:slots] = (rows == targets[0]).astype(F32).astype(BF16)
    small = lax.broadcasted_iota(I32, (BLK, tokens), 0)
    for step, direction in ((-1, 1), (1, 0)):
        source = jnp.clip(me + step, 0, count - 1)
        border = blocks_ref[source, ROW_BORDER : ROW_BORDER + 2, :].astype(I32)
        target = targets[1 if step < 0 else 2]
        start = slots + (0 if step < 0 else halo)
        for i in range(halo // BLK):
            wanted = border[direction : direction + 1, i : i + 1] * BLK
            here = slice(start + i * BLK, start + (i + 1) * BLK)
            picks_ref[here] = (small + wanted == target).astype(F32).astype(BF16)


def decode_kernel(
    blocks_ref,
    picks_ref,
    mine_ref,
    other_ref,
    time_ref,
    proj_ref,
    map_ref,
    weight_ref,
    owned_ref,
    fine_ref,
    code_ref,
):
    is_cond = lax.axis_index("pair") == 0
    slots = owned_ref.shape[1]
    offsets = map_ref.shape[0]
    out_channels = fine_ref.shape[0]
    table_rows = code_ref.shape[2]

    cleans = []
    for s in range(blocks_ref.shape[0]):
        mine, other = mine_ref[s], other_ref[s]
        cond = jnp.where(is_cond, mine, other)
        uncond = jnp.where(is_cond, other, mine)
        guided = uncond + GUIDANCE * (cond - uncond)
        cleans.append(blocks_ref[s, 0:LAT, :] - time_ref[0] * guided)
    clean = jnp.concatenate(cleans, axis=1)

    parts = jnp.concatenate(split_three(clean), axis=0).astype(BF16)
    spread = dot_abt(parts, picks_ref[...])
    table = spread[0:LAT] + spread[LAT : 2 * LAT] + spread[2 * LAT :]
    owned_ref[...] = table[:, 0:slots]

    proj_high, proj_low = split_two(proj_ref[...])
    table_high, table_low = split_two(table)
    left = jnp.concatenate([proj_high, proj_high, proj_low, jnp.zeros_like(proj_low)], axis=0)
    right = jnp.concatenate([table_high, table_low, table_high, jnp.zeros_like(table_low)], axis=0)
    before = dot_atb(left.astype(BF16), right.astype(BF16))
    features = (0.5 * before * (1.0 + jnp.tanh(0.5 * before))).astype(BF16)

    count = 3
    groups = [range(k, min(k + count, offsets)) for k in range(0, offsets, count)]

    def multiply(group):
        rows = weight_ref[group[0] * out_channels : (group[-1] + 1) * out_channels]
        return dot_ab(rows, features)

    def code(group, product):
        top = jnp.max(jnp.abs(product), axis=0, keepdims=True)
        top = jnp.maximum(jnp.max(top, axis=1, keepdims=True), TINY)
        scaled = product * (CODE_TOP / top)
        high = scaled.astype(F8)
        low = (scaled - high.astype(F32)).astype(F8)
        for i, k in enumerate(group):
            rows = slice(i * out_channels, (i + 1) * out_channels)
            code_ref[k, 0:out_channels] = high[rows]
            code_ref[k, out_channels : 2 * out_channels] = low[rows]
        return top * (1.0 / CODE_TOP)

    units = []
    ready = multiply(groups[0])
    for i, group in enumerate(groups):
        product = ready
        if i + 1 < len(groups):
            ready = multiply(groups[i + 1])
        units.append(code(group, product))

    fine = map_ref.shape[2]
    width = 256
    table_ids = lax.broadcasted_iota(jnp.int16, (table_rows, width), 0)
    one = jnp.ones((table_rows, width), F8)
    zero = jnp.zeros((table_rows, width), F8)
    for f in range(fine // width):
        here = slice(f * width, (f + 1) * width)
        total = jnp.zeros((out_channels, width), F32)
        for group, unit in zip(groups, units):
            part = jnp.zeros((2 * out_channels, width), F32)
            for k in group:
                index = jnp.broadcast_to(map_ref[k, :, here], (16, width)).astype(jnp.int16)
                index = jnp.broadcast_to(index[None], (table_rows // 16, 16, width))
                chosen = jnp.where(table_ids == index.reshape(table_rows, width), one, zero)
                part = part + dot_ab(code_ref[k], chosen)
            total = total + (part[0:out_channels] + part[out_channels:]) * unit
        fine_ref[:, here] = total.astype(BF16)


def route_call(blocks, table_rows):
    count, _, block = blocks.shape
    return pl.pallas_call(
        route_kernel,
        out_shape=pltpu.VMEM((table_rows, count * block), BF16),
        in_specs=[VMEM],
        out_specs=VMEM,
        compiler_params=pltpu.CompilerParams(vmem_limit_bytes=VMEM_GRANT),
        cost_estimate=pl.CostEstimate(flops=0, bytes_accessed=1 << 20, transcendentals=0),
        name="route",
    )(blocks)


def decode_call(
    blocks, picks, velocity, partner, step_time, decoder_projection, index_rows, weights
):
    offsets, _, fine = index_rows.shape
    out_channels = weights.shape[0] // offsets
    slots = fine // 4
    table_rows = picks.shape[0]
    return pl.pallas_call(
        decode_kernel,
        out_shape=(
            jax.ShapeDtypeStruct((LAT, slots), F32),
            jax.ShapeDtypeStruct((out_channels, fine), BF16),
        ),
        in_specs=[VMEM, VMEM, VMEM, VMEM, SMEM, VMEM, VMEM, VMEM],
        out_specs=(VMEM, VMEM),
        scratch_shapes=[pltpu.VMEM((offsets, 2 * out_channels, table_rows), F8)],
        compiler_params=pltpu.CompilerParams(vmem_limit_bytes=VMEM_GRANT),
        name="decode",
    )(blocks, picks, velocity, partner, step_time, decoder_projection, index_rows, weights)


def swap_pair(x):
    return lax.ppermute(x, "pair", [(0, 1), (1, 0)])


def seq_swap(x, distance_of):
    count = lax.axis_size("seq")
    routes = [
        (p * count + (z ^ distance_of[p]), p * count + z) for p in range(2) for z in range(count)
    ]
    return lax.ppermute(x, ("pair", "seq"), routes)


def whole_asset_velocity(packed, modulation, in_proj, qkv_proj, norm_gain, out_proj, head_proj):
    count = lax.axis_size("seq")
    block = packed.shape[1]
    tokens = count * block
    width = in_proj.shape[1]
    inner = out_proj.shape[0]
    far = seq_swap(packed, (3, 3))
    mixed = seq_swap(packed, (1, 2))
    swapped = swap_pair(mixed)
    pos = jnp.asarray(position_parts(width))
    held = pl.pallas_call(
        own_kernel,
        out_shape=(
            pltpu.VMEM((5, 1, width), F32),
            pltpu.VMEM(qkv_proj.shape, BF16),
            pltpu.VMEM(norm_gain.shape, F32),
            pltpu.VMEM(out_proj.shape, BF16),
            pltpu.VMEM((LAT, width), F32),
            pltpu.VMEM((pos.shape[0] + 32, width), BF16),
            pltpu.VMEM((block, width), F32),
            pltpu.VMEM((block, inner), BF16),
            pltpu.VMEM((block, inner), BF16),
            pltpu.VMEM((inner // 128, block, 128), BF16),
        ),
        in_specs=[VMEM] * 2 + [HBM] * 7,
        out_specs=(VMEM,) * 10,
        scratch_shapes=[
            pltpu.VMEM(in_proj.shape, F32),
            pltpu.SemaphoreType.DMA((7,)),
        ],
        compiler_params=pltpu.CompilerParams(vmem_limit_bytes=VMEM_GRANT),
        cost_estimate=pl.CostEstimate(
            flops=2 * block * width * 4 * inner, bytes_accessed=6 << 20, transcendentals=0
        ),
        name="own_block",
    )(
        packed,
        mixed,
        *in_hbm(
            modulation[0, 0][:, None, :],
            in_proj,
            qkv_proj,
            norm_gain,
            out_proj,
            head_proj.T,
            pos,
        ),
    )
    return pl.pallas_call(
        velocity_kernel,
        out_shape=(
            pltpu.VMEM((count, LAT, block), F32),
            pltpu.VMEM((count, PACK_ROWS, block), F32),
        ),
        in_specs=[VMEM] * 14,
        out_specs=(VMEM, VMEM),
        scratch_shapes=[
            pltpu.VMEM((tokens, width), F32),
            pltpu.VMEM((tokens, width), BF16),
            pltpu.VMEM((tokens, inner), BF16),
            pltpu.VMEM((tokens, inner), BF16),
            pltpu.VMEM((inner // 128, tokens, 256), BF16),
            pltpu.VMEM((tokens, inner), BF16),
        ],
        compiler_params=pltpu.CompilerParams(vmem_limit_bytes=VMEM_GRANT),
        name="velocity",
    )(packed, mixed, swapped, far, *held)


def layer_norm(values):
    center = values - jnp.mean(values, axis=-1, keepdims=True)
    variance = jnp.mean(center * center, axis=-1, keepdims=True)
    return center / jnp.sqrt(variance + EPSILON)


def position_table(coord_rows, model_width):
    freqs = model_width // 6
    steps = jnp.arange(freqs, dtype=F32) / freqs
    omegas = jnp.exp(-math.log(10000.0) * steps)
    angles = coord_rows.astype(F32)[:, :, None] * omegas[None, None, :]
    halves = jnp.concatenate([jnp.sin(angles), jnp.cos(angles)], axis=2)
    rows_out = jnp.transpose(halves, (1, 0, 2)).reshape(coord_rows.shape[1], 6 * freqs)
    return jnp.pad(rows_out, ((0, 0), (0, model_width - 6 * freqs)))


def head_norm(values, gains):
    row_count = values.shape[0]
    per_head = values.reshape(row_count, HEADS, HEAD)
    mean_square = jnp.mean(per_head * per_head, axis=2, keepdims=True)
    return (per_head / jnp.sqrt(mean_square + EPSILON)).reshape(row_count, HEADS * HEAD) * gains


def gathered_velocity(
    latent_block, coords, modulation, in_proj, qkv_proj, norm_gain, out_proj, head_proj
):
    token_count = latent_block.shape[1]
    model_width = in_proj.shape[1]
    inner_width = out_proj.shape[0]
    factor = HEAD ** (-0.5)
    mod_rows = modulation[0, 0]
    hidden = jnp.dot(latent_block.T, in_proj, precision=TOP_PRECISION) + position_table(
        coords, model_width
    )
    normed = (layer_norm(hidden) * (1.0 + mod_rows[1]) + mod_rows[0]).astype(BF16)
    projected = jnp.dot(normed, qkv_proj, preferred_element_type=F32)
    queries = head_norm(projected[:, :inner_width], norm_gain[0]).astype(BF16)
    keys_in = head_norm(projected[:, inner_width : 2 * inner_width], norm_gain[1]).astype(BF16)
    values_in = projected[:, 2 * inner_width :].astype(BF16)
    query_heads = queries.reshape(token_count, HEADS, HEAD)
    start_pair = (
        jnp.zeros((token_count, HEADS, HEAD), F32),
        jnp.zeros((token_count, HEADS), F32),
    )
    key_rows = lax.all_gather(keys_in, "seq", axis=0, tiled=True)
    value_rows = lax.all_gather(values_in, "seq", axis=0, tiled=True)
    row_count = key_rows.shape[0]
    block_rows = math.gcd(row_count, 512)
    key_blocks = key_rows.reshape(row_count // block_rows, block_rows, HEADS, HEAD)
    value_blocks = value_rows.reshape(row_count // block_rows, block_rows, HEADS, HEAD)

    def one_block(running, block_pair):
        numer_run, denom_run = running
        key_block, value_block = block_pair
        scores = (
            jnp.einsum("qhd,khd->hqk", query_heads, key_block, preferred_element_type=F32) * factor
        )
        exp_scores = jnp.exp(scores)
        numer_run = numer_run + jnp.einsum(
            "hqk,khd->qhd", exp_scores.astype(BF16), value_block, preferred_element_type=F32
        )
        denom_run = denom_run + jnp.sum(exp_scores, axis=2).T
        return ((numer_run, denom_run), None)

    (numerator, denominator), _ = lax.scan(one_block, start_pair, (key_blocks, value_blocks))
    attended = (
        (numerator / denominator[:, :, None]).reshape(token_count, inner_width).astype(BF16)
    )
    hidden = hidden + mod_rows[2] * jnp.dot(attended, out_proj, preferred_element_type=F32)
    final = layer_norm(hidden) * (1.0 + mod_rows[4]) + mod_rows[3]
    velocity = jnp.dot(final, head_proj, precision=TOP_PRECISION).T
    return lax.all_gather(velocity, "seq", axis=0)


def per_device(
    latents,
    voxel_coords,
    owner_map,
    step_time,
    modulation,
    in_proj,
    qkv_proj,
    norm_gain,
    out_proj,
    head_proj,
    decoder_projection,
    border_blocks,
    kernel_map,
    conv_weight,
):
    count = lax.axis_size("seq")
    block = latents.shape[2]
    packed = pl.pallas_call(
        pack_kernel,
        out_shape=pltpu.VMEM((PACK_ROWS, block), F32),
        in_specs=[HBM] * 4,
        out_specs=VMEM,
        scratch_shapes=[
            pltpu.VMEM((3, 1, block), I32),
            pltpu.VMEM((1, block), I32),
            pltpu.VMEM(border_blocks.shape[2:], I32),
            pltpu.SemaphoreType.DMA((4,)),
        ],
        compiler_params=pltpu.CompilerParams(vmem_limit_bytes=VMEM_GRANT),
        name="pack",
    )(
        *in_hbm(
            latents[0],
            jnp.swapaxes(voxel_coords, 0, 1),
            owner_map.reshape(1, block),
            border_blocks[0, 0],
        )
    )
    if count == 4 and count * block <= WHOLE_ASSET:
        velocity, blocks = whole_asset_velocity(
            packed, modulation, in_proj, qkv_proj, norm_gain, out_proj, head_proj
        )
    else:
        blocks = lax.all_gather(packed, "seq", axis=0)
        velocity = gathered_velocity(
            latents[0],
            voxel_coords[0],
            modulation,
            in_proj,
            qkv_proj,
            norm_gain,
            out_proj,
            head_proj,
        )
    partner = swap_pair(velocity)
    picks = route_call(blocks, kernel_map.shape[3] // 2)
    offsets, _, out_channels = conv_weight.shape
    fine = kernel_map.shape[3]
    owned, decoded = decode_call(
        blocks,
        picks,
        velocity,
        partner,
        step_time,
        decoder_projection,
        kernel_map.reshape(offsets, 1, fine),
        jnp.swapaxes(conv_weight, 1, 2).reshape(offsets * out_channels, -1),
    )
    return (owned[None, None], decoded.T[None, None])


def solution(mesh):
    placed = (
        P("asset", None, "seq"),
        P("asset", None, "seq"),
        P("asset", "seq", None),
        P("asset"),
        P("asset", "pair", None, None),
        P(),
        P(),
        P(),
        P(),
        P(),
        P(),
        P("asset", "seq", None, None),
        P("asset", "seq", None, None),
        P(None, None, "pair"),
    )
    return jax.shard_map(
        per_device,
        mesh=mesh,
        in_specs=placed,
        out_specs=(P("asset", "seq", None, None), P("asset", "seq", None, "pair")),
        check_vma=False,
    )
```

```python
import functools
import math

import jax
import jax.numpy as jnp
import numpy as np
from jax import lax
from jax.experimental import pallas as pl
from jax.experimental.pallas import tpu as pltpu
from jax.sharding import PartitionSpec as P

HEADS = 8
HEAD = 64
LAT = 8
BLK = 16
RES = 64

EPSILON = 1e-06
GUIDANCE = 3.0
TOP_PRECISION = lax.Precision.HIGHEST
F32 = jnp.float32
BF16 = jnp.bfloat16
I32 = jnp.int32
F8 = jnp.float8_e4m3fn
CODE_TOP = 256.0
TINY = 1e-30

ROW_COORD = 8
ROW_OWNER = 11
ROW_BORDER = 12
PACK_ROWS = 16
WHOLE_ASSET = 512

VMEM_GRANT = 40 << 20

VMEM = pl.BlockSpec(memory_space=pltpu.VMEM)
HBM = pl.BlockSpec(memory_space=pltpu.HBM)
SMEM = pl.BlockSpec(memory_space=pltpu.SMEM)


def dot_ab(a, b):
    return jnp.dot(a, b, preferred_element_type=F32)


def dot_abt(a, b):
    return lax.dot_general(a, b, (((1,), (1,)), ((), ())), preferred_element_type=F32)


def dot_atb(a, b):
    return lax.dot_general(a, b, (((0,), (0,)), ((), ())), preferred_element_type=F32)


def in_hbm(*arrays):
    return [pltpu.with_memory_space_constraint(x, pltpu.HBM) for x in arrays]


def split_two(x):
    high = x.astype(BF16).astype(F32)
    return high, x - high


def split_three(x):
    high, rest = split_two(x)
    mid, low = split_two(rest)
    return high, mid, low


@functools.lru_cache(None)
def position_parts(model_width):
    freqs = model_width // 6
    steps = np.arange(freqs, dtype=np.float32) / np.float32(freqs)
    omegas = np.exp(np.float32(-math.log(10000.0)) * steps).astype(np.float32)
    angles = (np.arange(RES, dtype=np.float32)[:, None] * omegas[None, :]).astype(np.float64)
    halves = np.concatenate([np.sin(angles), np.cos(angles)], axis=1).astype(np.float32)
    table = np.zeros((3 * RES, model_width), np.float32)
    for c in range(3):
        table[c * RES : (c + 1) * RES, c * 2 * freqs : (c + 1) * 2 * freqs] = halves
    high = table.astype(jnp.bfloat16)
    low = (table - high.astype(np.float32)).astype(jnp.bfloat16)
    return np.concatenate([high, low], axis=0)


def pack_kernel(
    lat_hbm, coord_hbm, owner_hbm, border_hbm, pack_ref, coord_ref, owner_ref, border_ref, sems
):
    pack_ref[...] = jnp.zeros_like(pack_ref)
    copies = [
        pltpu.make_async_copy(source, target, sems.at[i])
        for i, (source, target) in enumerate(
            (
                (lat_hbm, pack_ref.at[0:LAT]),
                (coord_hbm, coord_ref),
                (owner_hbm, owner_ref),
                (border_hbm, border_ref),
            )
        )
    ]
    for copy in copies:
        copy.start()
    for copy in copies:
        copy.wait()
    for c in range(3):
        pack_ref[ROW_COORD + c : ROW_COORD + c + 1] = coord_ref[c].astype(F32)
    pack_ref[ROW_OWNER : ROW_OWNER + 1] = owner_ref[...].astype(F32)
    pack_ref[ROW_BORDER : ROW_BORDER + 2, 0 : border_ref.shape[1]] = border_ref[...].astype(F32)


def hidden_rows(rows, table_ref):
    block = rows.shape[1]
    values = lax.broadcasted_iota(I32, (RES, block), 0).astype(F32)
    hots = [
        (values == rows[ROW_COORD + c : ROW_COORD + c + 1]).astype(F32).astype(BF16)
        for c in range(3)
    ]
    high, low = split_two(rows[0:LAT])
    tail = jnp.concatenate([high, low, high, jnp.zeros_like(low)], axis=0).astype(BF16)
    return dot_atb(jnp.concatenate(hots + hots + [tail], axis=0), table_ref[...])


def modulated(hidden, mod_ref):
    center = hidden - jnp.mean(hidden, axis=1, keepdims=True)
    inverse = lax.rsqrt(jnp.mean(center * center, axis=1, keepdims=True) + EPSILON)
    return (center * inverse * (1.0 + mod_ref[1]) + mod_ref[0]).astype(BF16)


def project(normed, qkv_ref, gain_ref, query_ref, key_ref, value_ref, rows):
    inner = gain_ref.shape[1]
    group = 256
    same_head = (
        lax.broadcasted_iota(I32, (group, group), 0) // HEAD
        == lax.broadcasted_iota(I32, (group, group), 1) // HEAD
    )
    averager = jnp.where(same_head, 1.0 / HEAD, 0.0).astype(BF16)

    def finish(j, projected):
        which, col = divmod(j * group, inner)
        if which == 2:
            for half in range(group // 128):
                lanes = slice(half * 128, (half + 1) * 128)
                value_ref[col // 128 + half, rows, 0:128] = projected[:, lanes].astype(BF16)
        else:
            square = dot_ab((projected * projected).astype(BF16), averager)
            gains = gain_ref[which : which + 1, col : col + group]
            if which == 0:
                gains = gains * (HEAD**-0.5)
            result = (projected * lax.rsqrt(square + EPSILON) * gains).astype(BF16)
            (query_ref, key_ref)[which][rows, col : col + group] = result

    previous = None
    for j in range(3 * inner // group):
        projected = dot_ab(normed, qkv_ref[:, j * group : (j + 1) * group])
        if previous is not None:
            finish(*previous)
        previous = (j, projected)
    finish(*previous)


def own_kernel(
    own_ref,
    mod_hbm,
    in_hbm,
    qkv_hbm,
    gain_hbm,
    out_hbm,
    head_hbm,
    pos_hbm,
    mod_ref,
    qkv_ref,
    gain_ref,
    out_ref,
    head_ref,
    table_ref,
    hidden_ref,
    query_ref,
    key_ref,
    value_ref,
    in_ref,
    sems,
):
    pos_rows = pos_hbm.shape[0]
    copies = [
        pltpu.make_async_copy(source, target, sems.at[i])
        for i, (source, target) in enumerate(
            (
                (pos_hbm, table_ref.at[0:pos_rows]),
                (in_hbm, in_ref),
                (mod_hbm, mod_ref),
                (gain_hbm, gain_ref),
                (qkv_hbm, qkv_ref),
                (head_hbm, head_ref),
                (out_hbm, out_ref),
            )
        )
    ]
    for copy in copies:
        copy.start()
    for copy in copies[:4]:
        copy.wait()
    in_high, in_low = split_two(in_ref[...])
    table_ref[pos_rows : pos_rows + 32, :] = jnp.concatenate(
        [in_high, in_high, in_low, jnp.zeros_like(in_low)], axis=0
    ).astype(BF16)
    hidden = hidden_rows(own_ref[...], table_ref)
    hidden_ref[...] = hidden
    normed = modulated(hidden, mod_ref)
    copies[4].wait()
    block = own_ref.shape[1]
    project(normed, qkv_ref, gain_ref, query_ref, key_ref, value_ref, slice(0, block))
    copies[5].wait()
    copies[6].wait()


def near_kernel(
    near_ref,
    later_ref,
    mod_ref,
    qkv_ref,
    gain_ref,
    table_ref,
    hidden_ref,
    query_ref,
    key_ref,
    value_ref,
):
    hidden = hidden_rows(near_ref[...], table_ref)
    hidden_ref[...] = hidden
    normed = modulated(hidden, mod_ref)
    rows = slice(0, near_ref.shape[1])
    project(normed, qkv_ref, gain_ref, query_ref, key_ref, value_ref, rows)


def velocity_kernel(
    own_ref,
    near_ref,
    first_ref,
    swapped_ref,
    mod_ref,
    qkv_ref,
    gain_ref,
    out_ref,
    head_ref,
    table_ref,
    own_hidden_ref,
    own_query_ref,
    own_key_ref,
    own_value_ref,
    near_hidden_ref,
    near_query_ref,
    near_key_ref,
    near_value_ref,
    vel_ref,
    blocks_ref,
    hidden_ref,
    normed_ref,
    query_ref,
    key_ref,
    value_ref,
    att_ref,
):
    me = lax.axis_index("seq")
    side = lax.axis_index("pair")
    width = qkv_ref.shape[0]
    tokens = hidden_ref.shape[0]
    inner = out_ref.shape[0]
    block = own_ref.shape[1]
    places = (me, me ^ 1, me ^ (3 - side), me ^ (2 + side))
    sources = (own_ref, near_ref, first_ref, swapped_ref)
    for place, source in zip(places, sources):
        blocks_ref[place] = source[...]

    value_ref[:, :, 128:256] = jnp.ones((inner // 128, tokens, 128), BF16)
    ready = hidden_rows(first_ref[...], table_ref)
    done = (
        (own_hidden_ref, own_query_ref, own_key_ref, own_value_ref),
        (near_hidden_ref, near_query_ref, near_key_ref, near_value_ref),
    )
    for s, (hidden, query, key, value) in enumerate(done):
        here = slice(s * block, (s + 1) * block)
        hidden_ref[here, :] = hidden[...]
        query_ref[here, :] = query[...]
        key_ref[here, :] = key[...]
        for pair in range(inner // 128):
            value_ref[pair, here, 0:128] = value[pair]
    for s in range(len(done), len(sources)):
        hidden = ready
        if s + 1 < len(sources):
            ready = hidden_rows(sources[s + 1][...], table_ref)
        hidden_ref[s * block : (s + 1) * block, :] = hidden
        normed_ref[s * block : (s + 1) * block, :] = modulated(hidden, mod_ref)
    others = slice(len(done) * block, tokens)
    project(normed_ref[others, :], qkv_ref, gain_ref, query_ref, key_ref, value_ref, others)

    chunk = 256
    even = lax.broadcasted_iota(I32, (chunk, 128), 1) < HEAD
    todo = [(pair, q, half) for pair in range(inner // 128) for q in range(tokens // chunk) for half in range(2)]
    def score(pair, q, half):
        lanes = slice(pair * 128, (pair + 1) * 128)
        query = query_ref[q * chunk : (q + 1) * chunk, lanes]
        kept = jnp.where(even == (half == 0), query, jnp.zeros_like(query))
        return dot_abt(kept, key_ref[:, lanes])
    ready = score(*todo[0])
    parts = []
    for at, (pair, q, half) in enumerate(todo):
        scores = ready
        if at + 1 < len(todo):
            ready = score(*todo[at + 1])
        sums = dot_ab(jnp.exp(scores).astype(BF16), value_ref[pair])
        parts.append(sums[:, 0:128] / sums[:, 128:256])
        if half == 1:
            att_ref[q * chunk : (q + 1) * chunk, pair * 128 : (pair + 1) * 128] = jnp.where(even, parts[0], parts[1]).astype(BF16)
            parts = []

    gate = mod_ref[2]
    head = head_ref[...]
    offset = jnp.sum(head * mod_ref[3], axis=1, keepdims=True)
    head_high, head_low = split_two(head * (1.0 + mod_ref[4]))
    heads = jnp.concatenate([head_high, head_low], axis=0).astype(BF16)
    ones = jnp.ones((16, width), BF16)
    step = 128
    def attended(q):
        return dot_ab(att_ref[q * step : (q + 1) * step, :], out_ref[...])
    def middle(q, product):
        hidden = hidden_ref[q * step : (q + 1) * step, :] + gate * product
        center = hidden - jnp.mean(hidden, axis=1, keepdims=True)
        high = center.astype(BF16)
        low = (center - high.astype(F32)).astype(BF16)
        return high, low
    def last(q, high, low):
        both = dot_abt(heads, high)
        rest = dot_abt(heads, low)
        square = dot_abt(ones, high * high)
        inverse = lax.rsqrt(square[0:LAT] * (1.0 / width) + EPSILON)
        velocity = (both[0:LAT] + both[LAT:] + rest[0:LAT]) * inverse + offset
        for i in range(step // block):
            vel_ref[places[q * (step // block) + i]] = velocity[:, i * block : (i + 1) * block]
    count = tokens // step
    product = attended(0)
    waiting = None
    for q in range(count):
        following = attended(q + 1) if q + 1 < count else None
        centered = middle(q, product)
        if waiting is not None:
            last(*waiting)
        waiting = (q, *centered)
        product = following
    last(*waiting)


def route_kernel(blocks_ref, picks_ref):
    me = lax.axis_index("seq")
    count, _, block = blocks_ref.shape
    table_rows = picks_ref.shape[0]
    slots = table_rows // 2
    capacity = slots // count
    halo = (table_rows - slots) // 2

    owners = jnp.concatenate(
        [blocks_ref[s, ROW_OWNER : ROW_OWNER + 1, :] for s in range(count)], axis=0
    ).astype(I32)
    earlier = (
        lax.broadcasted_iota(I32, (block, block), 0) < lax.broadcasted_iota(I32, (block, block), 1)
    ).astype(F32).astype(BF16)
    starts = lax.broadcasted_iota(I32, (count, block), 0) * capacity
    targets = []
    for step in (0, -1, 1):
        named = owners == me + step
        ranks = dot_ab(named.astype(F32).astype(BF16), earlier).astype(I32)
        slot_of = jnp.where(named, ranks + starts, -1)
        targets.append(jnp.concatenate([slot_of[s : s + 1] for s in range(count)], axis=1))
    tokens = count * block
    rows = lax.broadcasted_iota(I32, (slots, tokens), 0)
    picks_ref[0:slots] = (rows == targets[0]).astype(F32).astype(BF16)
    small = lax.broadcasted_iota(I32, (BLK, tokens), 0)
    for step, direction in ((-1, 1), (1, 0)):
        source = jnp.clip(me + step, 0, count - 1)
        border = blocks_ref[source, ROW_BORDER : ROW_BORDER + 2, :].astype(I32)
        target = targets[1 if step < 0 else 2]
        start = slots + (0 if step < 0 else halo)
        for i in range(halo // BLK):
            wanted = border[direction : direction + 1, i : i + 1] * BLK
            here = slice(start + i * BLK, start + (i + 1) * BLK)
            picks_ref[here] = (small + wanted == target).astype(F32).astype(BF16)


def decode_kernel(
    blocks_ref,
    picks_ref,
    mine_ref,
    other_ref,
    time_ref,
    proj_ref,
    map_ref,
    weight_ref,
    owned_ref,
    fine_ref,
    code_ref,
):
    is_cond = lax.axis_index("pair") == 0
    slots = owned_ref.shape[1]
    offsets = map_ref.shape[0]
    out_channels = fine_ref.shape[0]
    table_rows = code_ref.shape[2]

    cleans = []
    for s in range(blocks_ref.shape[0]):
        mine, other = mine_ref[s], other_ref[s]
        cond = jnp.where(is_cond, mine, other)
        uncond = jnp.where(is_cond, other, mine)
        guided = uncond + GUIDANCE * (cond - uncond)
        cleans.append(blocks_ref[s, 0:LAT, :] - time_ref[0] * guided)
    clean = jnp.concatenate(cleans, axis=1)

    parts = jnp.concatenate(split_three(clean), axis=0).astype(BF16)
    spread = dot_abt(parts, picks_ref[...])
    table = spread[0:LAT] + spread[LAT : 2 * LAT] + spread[2 * LAT :]
    owned_ref[...] = table[:, 0:slots]

    proj_high, proj_low = split_two(proj_ref[...])
    table_high, table_low = split_two(table)
    left = jnp.concatenate([proj_high, proj_high, proj_low, jnp.zeros_like(proj_low)], axis=0)
    right = jnp.concatenate([table_high, table_low, table_high, jnp.zeros_like(table_low)], axis=0)
    before = dot_atb(left.astype(BF16), right.astype(BF16))
    features = (0.5 * before * (1.0 + jnp.tanh(0.5 * before))).astype(BF16)

    count = 3
    groups = [range(k, min(k + count, offsets)) for k in range(0, offsets, count)]

    def multiply(group):
        rows = weight_ref[group[0] * out_channels : (group[-1] + 1) * out_channels]
        return dot_ab(rows, features)

    def code(group, product):
        top = jnp.max(jnp.abs(product), axis=0, keepdims=True)
        top = jnp.maximum(jnp.max(top, axis=1, keepdims=True), TINY)
        scaled = product * (CODE_TOP / top)
        high = scaled.astype(F8)
        low = (scaled - high.astype(F32)).astype(F8)
        for i, k in enumerate(group):
            rows = slice(i * out_channels, (i + 1) * out_channels)
            code_ref[k, 0:out_channels] = high[rows]
            code_ref[k, out_channels : 2 * out_channels] = low[rows]
        return top * (1.0 / CODE_TOP)

    units = []
    ready = multiply(groups[0])
    for i, group in enumerate(groups):
        product = ready
        if i + 1 < len(groups):
            ready = multiply(groups[i + 1])
        units.append(code(group, product))

    fine = map_ref.shape[2]
    width = 256
    table_ids = lax.broadcasted_iota(jnp.int16, (table_rows, width), 0)
    one = jnp.ones((table_rows, width), F8)
    zero = jnp.zeros((table_rows, width), F8)
    for f in range(fine // width):
        here = slice(f * width, (f + 1) * width)
        total = jnp.zeros((out_channels, width), F32)
        for group, unit in zip(groups, units):
            part = jnp.zeros((2 * out_channels, width), F32)
            for k in group:
                index = jnp.broadcast_to(map_ref[k, :, here], (16, width)).astype(jnp.int16)
                index = jnp.broadcast_to(index[None], (table_rows // 16, 16, width))
                chosen = jnp.where(table_ids == index.reshape(table_rows, width), one, zero)
                part = part + dot_ab(code_ref[k], chosen)
            total = total + (part[0:out_channels] + part[out_channels:]) * unit
        fine_ref[:, here] = total.astype(BF16)


def route_call(blocks, table_rows):
    count, _, block = blocks.shape
    return pl.pallas_call(
        route_kernel,
        out_shape=pltpu.VMEM((table_rows, count * block), BF16),
        in_specs=[VMEM],
        out_specs=VMEM,
        compiler_params=pltpu.CompilerParams(vmem_limit_bytes=VMEM_GRANT),
        cost_estimate=pl.CostEstimate(flops=0, bytes_accessed=1 << 20, transcendentals=0),
        name="route",
    )(blocks)


def decode_call(
    blocks, picks, velocity, partner, step_time, decoder_projection, index_rows, weights
):
    offsets, _, fine = index_rows.shape
    out_channels = weights.shape[0] // offsets
    slots = fine // 4
    table_rows = picks.shape[0]
    return pl.pallas_call(
        decode_kernel,
        out_shape=(
            jax.ShapeDtypeStruct((LAT, slots), F32),
            jax.ShapeDtypeStruct((out_channels, fine), BF16),
        ),
        in_specs=[VMEM, VMEM, VMEM, VMEM, SMEM, VMEM, VMEM, VMEM],
        out_specs=(VMEM, VMEM),
        scratch_shapes=[pltpu.VMEM((offsets, 2 * out_channels, table_rows), F8)],
        compiler_params=pltpu.CompilerParams(vmem_limit_bytes=VMEM_GRANT),
        name="decode",
    )(blocks, picks, velocity, partner, step_time, decoder_projection, index_rows, weights)


def swap_pair(x):
    return lax.ppermute(x, "pair", [(0, 1), (1, 0)])


def seq_swap(x, distance_of):
    count = lax.axis_size("seq")
    routes = [
        (p * count + (z ^ distance_of[p]), p * count + z) for p in range(2) for z in range(count)
    ]
    return lax.ppermute(x, ("pair", "seq"), routes)


def whole_asset_velocity(packed, modulation, in_proj, qkv_proj, norm_gain, out_proj, head_proj):
    count = lax.axis_size("seq")
    block = packed.shape[1]
    tokens = count * block
    width = in_proj.shape[1]
    inner = out_proj.shape[0]
    first = seq_swap(packed, (3, 2))
    near = seq_swap(packed, (1, 1))
    swapped = swap_pair(first)
    block_shapes = (
        pltpu.VMEM((block, width), F32),
        pltpu.VMEM((block, inner), BF16),
        pltpu.VMEM((block, inner), BF16),
        pltpu.VMEM((inner // 128, block, 128), BF16),
    )
    block_cost = pl.CostEstimate(
        flops=2 * block * width * 4 * inner, bytes_accessed=6 << 20, transcendentals=0
    )
    pos = jnp.asarray(position_parts(width))
    held = pl.pallas_call(
        own_kernel,
        out_shape=(
            pltpu.VMEM((5, 1, width), F32),
            pltpu.VMEM(qkv_proj.shape, BF16),
            pltpu.VMEM(norm_gain.shape, F32),
            pltpu.VMEM(out_proj.shape, BF16),
            pltpu.VMEM((LAT, width), F32),
            pltpu.VMEM((pos.shape[0] + 32, width), BF16),
            *block_shapes,
        ),
        in_specs=[VMEM] + [HBM] * 7,
        out_specs=(VMEM,) * 10,
        scratch_shapes=[
            pltpu.VMEM(in_proj.shape, F32),
            pltpu.SemaphoreType.DMA((7,)),
        ],
        compiler_params=pltpu.CompilerParams(vmem_limit_bytes=VMEM_GRANT),
        cost_estimate=block_cost,
        name="own_block",
    )(
        packed,
        *in_hbm(
            modulation[0, 0][:, None, :],
            in_proj,
            qkv_proj,
            norm_gain,
            out_proj,
            head_proj.T,
            pos,
        ),
    )
    weights, own_state = held[:6], held[6:]
    mod_rows, qkv_rows, gains, _, _, table = weights
    near_state = pl.pallas_call(
        near_kernel,
        out_shape=block_shapes,
        in_specs=[VMEM] * 6,
        out_specs=(VMEM,) * 4,
        compiler_params=pltpu.CompilerParams(vmem_limit_bytes=VMEM_GRANT),
        cost_estimate=block_cost,
        name="near_block",
    )(near, first, mod_rows, qkv_rows, gains, table)
    return pl.pallas_call(
        velocity_kernel,
        out_shape=(
            pltpu.VMEM((count, LAT, block), F32),
            pltpu.VMEM((count, PACK_ROWS, block), F32),
        ),
        in_specs=[VMEM] * 18,
        out_specs=(VMEM, VMEM),
        scratch_shapes=[
            pltpu.VMEM((tokens, width), F32),
            pltpu.VMEM((tokens, width), BF16),
            pltpu.VMEM((tokens, inner), BF16),
            pltpu.VMEM((tokens, inner), BF16),
            pltpu.VMEM((inner // 128, tokens, 256), BF16),
            pltpu.VMEM((tokens, inner), BF16),
        ],
        compiler_params=pltpu.CompilerParams(vmem_limit_bytes=VMEM_GRANT),
        name="velocity",
    )(packed, near, first, swapped, *weights, *own_state, *near_state)


def layer_norm(values):
    center = values - jnp.mean(values, axis=-1, keepdims=True)
    variance = jnp.mean(center * center, axis=-1, keepdims=True)
    return center / jnp.sqrt(variance + EPSILON)


def position_table(coord_rows, model_width):
    freqs = model_width // 6
    steps = jnp.arange(freqs, dtype=F32) / freqs
    omegas = jnp.exp(-math.log(10000.0) * steps)
    angles = coord_rows.astype(F32)[:, :, None] * omegas[None, None, :]
    halves = jnp.concatenate([jnp.sin(angles), jnp.cos(angles)], axis=2)
    rows_out = jnp.transpose(halves, (1, 0, 2)).reshape(coord_rows.shape[1], 6 * freqs)
    return jnp.pad(rows_out, ((0, 0), (0, model_width - 6 * freqs)))


def head_norm(values, gains):
    row_count = values.shape[0]
    per_head = values.reshape(row_count, HEADS, HEAD)
    mean_square = jnp.mean(per_head * per_head, axis=2, keepdims=True)
    return (per_head / jnp.sqrt(mean_square + EPSILON)).reshape(row_count, HEADS * HEAD) * gains


def gathered_velocity(
    latent_block, coords, modulation, in_proj, qkv_proj, norm_gain, out_proj, head_proj
):
    token_count = latent_block.shape[1]
    model_width = in_proj.shape[1]
    inner_width = out_proj.shape[0]
    factor = HEAD ** (-0.5)
    mod_rows = modulation[0, 0]
    hidden = jnp.dot(latent_block.T, in_proj, precision=TOP_PRECISION) + position_table(
        coords, model_width
    )
    normed = (layer_norm(hidden) * (1.0 + mod_rows[1]) + mod_rows[0]).astype(BF16)
    projected = jnp.dot(normed, qkv_proj, preferred_element_type=F32)
    queries = head_norm(projected[:, :inner_width], norm_gain[0]).astype(BF16)
    keys_in = head_norm(projected[:, inner_width : 2 * inner_width], norm_gain[1]).astype(BF16)
    values_in = projected[:, 2 * inner_width :].astype(BF16)
    query_heads = queries.reshape(token_count, HEADS, HEAD)
    start_pair = (
        jnp.zeros((token_count, HEADS, HEAD), F32),
        jnp.zeros((token_count, HEADS), F32),
    )
    key_rows = lax.all_gather(keys_in, "seq", axis=0, tiled=True)
    value_rows = lax.all_gather(values_in, "seq", axis=0, tiled=True)
    row_count = key_rows.shape[0]
    block_rows = math.gcd(row_count, 512)
    key_blocks = key_rows.reshape(row_count // block_rows, block_rows, HEADS, HEAD)
    value_blocks = value_rows.reshape(row_count // block_rows, block_rows, HEADS, HEAD)

    def one_block(running, block_pair):
        numer_run, denom_run = running
        key_block, value_block = block_pair
        scores = (
            jnp.einsum("qhd,khd->hqk", query_heads, key_block, preferred_element_type=F32) * factor
        )
        exp_scores = jnp.exp(scores)
        numer_run = numer_run + jnp.einsum(
            "hqk,khd->qhd", exp_scores.astype(BF16), value_block, preferred_element_type=F32
        )
        denom_run = denom_run + jnp.sum(exp_scores, axis=2).T
        return ((numer_run, denom_run), None)

    (numerator, denominator), _ = lax.scan(one_block, start_pair, (key_blocks, value_blocks))
    attended = (
        (numerator / denominator[:, :, None]).reshape(token_count, inner_width).astype(BF16)
    )
    hidden = hidden + mod_rows[2] * jnp.dot(attended, out_proj, preferred_element_type=F32)
    final = layer_norm(hidden) * (1.0 + mod_rows[4]) + mod_rows[3]
    velocity = jnp.dot(final, head_proj, precision=TOP_PRECISION).T
    return lax.all_gather(velocity, "seq", axis=0)


def per_device(
    latents,
    voxel_coords,
    owner_map,
    step_time,
    modulation,
    in_proj,
    qkv_proj,
    norm_gain,
    out_proj,
    head_proj,
    decoder_projection,
    border_blocks,
    kernel_map,
    conv_weight,
):
    count = lax.axis_size("seq")
    block = latents.shape[2]
    packed = pl.pallas_call(
        pack_kernel,
        out_shape=pltpu.VMEM((PACK_ROWS, block), F32),
        in_specs=[HBM] * 4,
        out_specs=VMEM,
        scratch_shapes=[
            pltpu.VMEM((3, 1, block), I32),
            pltpu.VMEM((1, block), I32),
            pltpu.VMEM(border_blocks.shape[2:], I32),
            pltpu.SemaphoreType.DMA((4,)),
        ],
        compiler_params=pltpu.CompilerParams(vmem_limit_bytes=VMEM_GRANT),
        name="pack",
    )(
        *in_hbm(
            latents[0],
            jnp.swapaxes(voxel_coords, 0, 1),
            owner_map.reshape(1, block),
            border_blocks[0, 0],
        )
    )
    if count == 4 and count * block <= WHOLE_ASSET:
        velocity, blocks = whole_asset_velocity(
            packed, modulation, in_proj, qkv_proj, norm_gain, out_proj, head_proj
        )
    else:
        blocks = lax.all_gather(packed, "seq", axis=0)
        velocity = gathered_velocity(
            latents[0],
            voxel_coords[0],
            modulation,
            in_proj,
            qkv_proj,
            norm_gain,
            out_proj,
            head_proj,
        )
    partner = swap_pair(velocity)
    picks = route_call(blocks, kernel_map.shape[3] // 2)
    offsets, _, out_channels = conv_weight.shape
    fine = kernel_map.shape[3]
    owned, decoded = decode_call(
        blocks,
        picks,
        velocity,
        partner,
        step_time,
        decoder_projection,
        kernel_map.reshape(offsets, 1, fine),
        jnp.swapaxes(conv_weight, 1, 2).reshape(offsets * out_channels, -1),
    )
    return (owned[None, None], decoded.T[None, None])


def solution(mesh):
    placed = (
        P("asset", None, "seq"),
        P("asset", None, "seq"),
        P("asset", "seq", None),
        P("asset"),
        P("asset", "pair", None, None),
        P(),
        P(),
        P(),
        P(),
        P(),
        P(),
        P("asset", "seq", None, None),
        P("asset", "seq", None, None),
        P(None, None, "pair"),
    )
    return jax.shard_map(
        per_device,
        mesh=mesh,
        in_specs=placed,
        out_specs=(P("asset", "seq", None, None), P("asset", "seq", None, "pair")),
        check_vma=False,
    )
```

```python
import functools
import math

import jax
import jax.numpy as jnp
import numpy as np
from jax import lax
from jax.experimental import pallas as pl
from jax.experimental.pallas import tpu as pltpu
from jax.sharding import PartitionSpec as P

HEADS = 8
HEAD = 64
LAT = 8
BLK = 16
RES = 64

EPSILON = 1e-06
GUIDANCE = 3.0
TOP_PRECISION = lax.Precision.HIGHEST
F32 = jnp.float32
BF16 = jnp.bfloat16
I32 = jnp.int32
F8 = jnp.float8_e4m3fn
CODE_TOP = 256.0
TINY = 1e-30

ROW_COORD = 8
ROW_OWNER = 11
ROW_BORDER = 12
PACK_ROWS = 16
WHOLE_ASSET = 512

VMEM_GRANT = 40 << 20

VMEM = pl.BlockSpec(memory_space=pltpu.VMEM)
HBM = pl.BlockSpec(memory_space=pltpu.HBM)
SMEM = pl.BlockSpec(memory_space=pltpu.SMEM)


def dot_ab(a, b):
    return jnp.dot(a, b, preferred_element_type=F32)


def dot_abt(a, b):
    return lax.dot_general(a, b, (((1,), (1,)), ((), ())), preferred_element_type=F32)


def dot_atb(a, b):
    return lax.dot_general(a, b, (((0,), (0,)), ((), ())), preferred_element_type=F32)


def in_hbm(*arrays):
    return [pltpu.with_memory_space_constraint(x, pltpu.HBM) for x in arrays]


def split_two(x):
    high = x.astype(BF16).astype(F32)
    return high, x - high


def split_three(x):
    high, rest = split_two(x)
    mid, low = split_two(rest)
    return high, mid, low


@functools.lru_cache(None)
def position_parts(model_width):
    freqs = model_width // 6
    steps = np.arange(freqs, dtype=np.float32) / np.float32(freqs)
    omegas = np.exp(np.float32(-math.log(10000.0)) * steps).astype(np.float32)
    angles = (np.arange(RES, dtype=np.float32)[:, None] * omegas[None, :]).astype(np.float64)
    halves = np.concatenate([np.sin(angles), np.cos(angles)], axis=1).astype(np.float32)
    table = np.zeros((3 * RES, model_width), np.float32)
    for c in range(3):
        table[c * RES : (c + 1) * RES, c * 2 * freqs : (c + 1) * 2 * freqs] = halves
    high = table.astype(jnp.bfloat16)
    low = (table - high.astype(np.float32)).astype(jnp.bfloat16)
    return np.concatenate([high, low], axis=0)


def pack_kernel(
    lat_hbm, coord_hbm, owner_hbm, border_hbm, pack_ref, coord_ref, owner_ref, border_ref, sems
):
    pack_ref[...] = jnp.zeros_like(pack_ref)
    copies = [
        pltpu.make_async_copy(source, target, sems.at[i])
        for i, (source, target) in enumerate(
            (
                (lat_hbm, pack_ref.at[0:LAT]),
                (coord_hbm, coord_ref),
                (owner_hbm, owner_ref),
                (border_hbm, border_ref),
            )
        )
    ]
    for copy in copies:
        copy.start()
    for copy in copies:
        copy.wait()
    for c in range(3):
        pack_ref[ROW_COORD + c : ROW_COORD + c + 1] = coord_ref[c].astype(F32)
    pack_ref[ROW_OWNER : ROW_OWNER + 1] = owner_ref[...].astype(F32)
    pack_ref[ROW_BORDER : ROW_BORDER + 2, 0 : border_ref.shape[1]] = border_ref[...].astype(F32)


def hidden_rows(rows, table_ref):
    block = rows.shape[1]
    values = lax.broadcasted_iota(I32, (RES, block), 0).astype(F32)
    hots = [
        (values == rows[ROW_COORD + c : ROW_COORD + c + 1]).astype(F32).astype(BF16)
        for c in range(3)
    ]
    high, low = split_two(rows[0:LAT])
    tail = jnp.concatenate([high, low, high, jnp.zeros_like(low)], axis=0).astype(BF16)
    return dot_atb(jnp.concatenate(hots + hots + [tail], axis=0), table_ref[...])


def modulated(hidden, mod_ref):
    center = hidden - jnp.mean(hidden, axis=1, keepdims=True)
    inverse = lax.rsqrt(jnp.mean(center * center, axis=1, keepdims=True) + EPSILON)
    return (center * inverse * (1.0 + mod_ref[1]) + mod_ref[0]).astype(BF16)


def project(normed, qkv_ref, gain_ref, query_ref, key_ref, value_ref, rows):
    inner = gain_ref.shape[1]
    group = 256
    same_head = (
        lax.broadcasted_iota(I32, (group, group), 0) // HEAD
        == lax.broadcasted_iota(I32, (group, group), 1) // HEAD
    )
    averager = jnp.where(same_head, 1.0 / HEAD, 0.0).astype(BF16)

    def finish(j, projected):
        which, col = divmod(j * group, inner)
        if which == 2:
            for half in range(group // 128):
                lanes = slice(half * 128, (half + 1) * 128)
                value_ref[col // 128 + half, rows, 0:128] = projected[:, lanes].astype(BF16)
        else:
            square = dot_ab((projected * projected).astype(BF16), averager)
            gains = gain_ref[which : which + 1, col : col + group]
            if which == 0:
                gains = gains * (HEAD**-0.5)
            result = (projected * lax.rsqrt(square + EPSILON) * gains).astype(BF16)
            (query_ref, key_ref)[which][rows, col : col + group] = result

    previous = None
    for j in range(3 * inner // group):
        projected = dot_ab(normed, qkv_ref[:, j * group : (j + 1) * group])
        if previous is not None:
            finish(*previous)
        previous = (j, projected)
    finish(*previous)


def first_half():
    return lax.axis_index("seq") < lax.axis_size("seq") // 2


def weight_copies(sources, targets, sems):
    mod_hbm, in_hbm_ref, qkv_hbm, gain_hbm, out_hbm, head_hbm, pos_hbm = sources
    mod_ref, in_ref, qkv_ref, gain_ref, out_ref, head_ref, table_ref = targets
    pairs = (
        (pos_hbm, table_ref.at[0 : pos_hbm.shape[0]]),
        (in_hbm_ref, in_ref),
        (mod_hbm, mod_ref),
        (gain_hbm, gain_ref),
        (qkv_hbm, qkv_ref),
        (head_hbm, head_ref),
        (out_hbm, out_ref),
    )
    return [
        pltpu.make_async_copy(source, target, sems.at[i])
        for i, (source, target) in enumerate(pairs)
    ]


def own_work(pack_ref, in_ref, copies, outs):
    mod_ref, qkv_ref, gain_ref, _, _, table_ref, hidden_ref, query_ref, key_ref, value_ref = outs
    for copy in copies[:4]:
        copy.wait()
    in_high, in_low = split_two(in_ref[...])
    pos_rows = table_ref.shape[0] - 32
    table_ref[pos_rows : pos_rows + 32, :] = jnp.concatenate(
        [in_high, in_high, in_low, jnp.zeros_like(in_low)], axis=0
    ).astype(BF16)
    hidden = hidden_rows(pack_ref[...], table_ref)
    hidden_ref[...] = hidden
    normed = modulated(hidden, mod_ref)
    copies[4].wait()
    rows = slice(0, pack_ref.shape[1])
    project(normed, qkv_ref, gain_ref, query_ref, key_ref, value_ref, rows)
    copies[5].wait()
    copies[6].wait()


def copy_targets(in_ref, outs):
    mod_ref, qkv_ref, gain_ref, out_ref, head_ref, table_ref = outs[:6]
    return mod_ref, in_ref, qkv_ref, gain_ref, out_ref, head_ref, table_ref


def early_kernel(*refs):
    inputs, sources, pack_ref, outs = refs[:4], refs[4:11], refs[11], refs[12:22]
    coord_ref, owner_ref, border_ref, in_ref, pack_sems, sems = refs[22:]
    copies = weight_copies(sources, copy_targets(in_ref, outs), sems)

    @pl.when(first_half())
    def _():
        for copy in copies:
            copy.start()

    pack_kernel(*inputs, pack_ref, coord_ref, owner_ref, border_ref, pack_sems)

    @pl.when(first_half())
    def _():
        own_work(pack_ref, in_ref, copies, outs)


def late_kernel(*refs):
    pack_ref, sources, outs, (in_ref, sems) = refs[0], refs[1:8], refs[18:28], refs[28:]

    @pl.when(jnp.logical_not(first_half()))
    def _():
        copies = weight_copies(sources, copy_targets(in_ref, outs), sems)
        for copy in copies:
            copy.start()
        own_work(pack_ref, in_ref, copies, outs)


def near_kernel(
    near_ref,
    later_ref,
    mod_ref,
    qkv_ref,
    gain_ref,
    table_ref,
    hidden_ref,
    query_ref,
    key_ref,
    value_ref,
):
    hidden = hidden_rows(near_ref[...], table_ref)
    hidden_ref[...] = hidden
    normed = modulated(hidden, mod_ref)
    rows = slice(0, near_ref.shape[1])
    project(normed, qkv_ref, gain_ref, query_ref, key_ref, value_ref, rows)


def velocity_kernel(
    own_ref,
    near_ref,
    first_ref,
    swapped_ref,
    mod_ref,
    qkv_ref,
    gain_ref,
    out_ref,
    head_ref,
    table_ref,
    own_hidden_ref,
    own_query_ref,
    own_key_ref,
    own_value_ref,
    near_hidden_ref,
    near_query_ref,
    near_key_ref,
    near_value_ref,
    vel_ref,
    blocks_ref,
    hidden_ref,
    normed_ref,
    query_ref,
    key_ref,
    value_ref,
    att_ref,
):
    me = lax.axis_index("seq")
    side = lax.axis_index("pair")
    width = qkv_ref.shape[0]
    tokens = hidden_ref.shape[0]
    inner = out_ref.shape[0]
    block = own_ref.shape[1]
    places = (me, me ^ 1, me ^ (3 - side), me ^ (2 + side))
    sources = (own_ref, near_ref, first_ref, swapped_ref)
    for place, source in zip(places, sources):
        blocks_ref[place] = source[...]

    value_ref[:, :, 128:256] = jnp.ones((inner // 128, tokens, 128), BF16)
    ready = hidden_rows(first_ref[...], table_ref)
    done = (
        (own_hidden_ref, own_query_ref, own_key_ref, own_value_ref),
        (near_hidden_ref, near_query_ref, near_key_ref, near_value_ref),
    )
    for s, (hidden, query, key, value) in enumerate(done):
        here = slice(s * block, (s + 1) * block)
        hidden_ref[here, :] = hidden[...]
        query_ref[here, :] = query[...]
        key_ref[here, :] = key[...]
        for pair in range(inner // 128):
            value_ref[pair, here, 0:128] = value[pair]
    for s in range(len(done), len(sources)):
        hidden = ready
        if s + 1 < len(sources):
            ready = hidden_rows(sources[s + 1][...], table_ref)
        hidden_ref[s * block : (s + 1) * block, :] = hidden
        normed_ref[s * block : (s + 1) * block, :] = modulated(hidden, mod_ref)
    others = slice(len(done) * block, tokens)
    project(normed_ref[others, :], qkv_ref, gain_ref, query_ref, key_ref, value_ref, others)

    chunk = 256
    even = lax.broadcasted_iota(I32, (chunk, 128), 1) < HEAD
    todo = [(pair, q, half) for pair in range(inner // 128) for q in range(tokens // chunk) for half in range(2)]
    def score(pair, q, half):
        lanes = slice(pair * 128, (pair + 1) * 128)
        query = query_ref[q * chunk : (q + 1) * chunk, lanes]
        kept = jnp.where(even == (half == 0), query, jnp.zeros_like(query))
        return dot_abt(kept, key_ref[:, lanes])
    ready = score(*todo[0])
    parts = []
    for at, (pair, q, half) in enumerate(todo):
        scores = ready
        if at + 1 < len(todo):
            ready = score(*todo[at + 1])
        sums = dot_ab(jnp.exp(scores).astype(BF16), value_ref[pair])
        parts.append(sums[:, 0:128] / sums[:, 128:256])
        if half == 1:
            att_ref[q * chunk : (q + 1) * chunk, pair * 128 : (pair + 1) * 128] = jnp.where(even, parts[0], parts[1]).astype(BF16)
            parts = []

    gate = mod_ref[2]
    head = head_ref[...]
    offset = jnp.sum(head * mod_ref[3], axis=1, keepdims=True)
    head_high, head_low = split_two(head * (1.0 + mod_ref[4]))
    heads = jnp.concatenate([head_high, head_low], axis=0).astype(BF16)
    ones = jnp.ones((16, width), BF16)
    step = 128
    def attended(q):
        return dot_ab(att_ref[q * step : (q + 1) * step, :], out_ref[...])
    def middle(q, product):
        hidden = hidden_ref[q * step : (q + 1) * step, :] + gate * product
        center = hidden - jnp.mean(hidden, axis=1, keepdims=True)
        high = center.astype(BF16)
        low = (center - high.astype(F32)).astype(BF16)
        return high, low
    def last(q, high, low):
        both = dot_abt(heads, high)
        rest = dot_abt(heads, low)
        square = dot_abt(ones, high * high)
        inverse = lax.rsqrt(square[0:LAT] * (1.0 / width) + EPSILON)
        velocity = (both[0:LAT] + both[LAT:] + rest[0:LAT]) * inverse + offset
        for i in range(step // block):
            vel_ref[places[q * (step // block) + i]] = velocity[:, i * block : (i + 1) * block]
    count = tokens // step
    product = attended(0)
    waiting = None
    for q in range(count):
        following = attended(q + 1) if q + 1 < count else None
        centered = middle(q, product)
        if waiting is not None:
            last(*waiting)
        waiting = (q, *centered)
        product = following
    last(*waiting)


def route_kernel(blocks_ref, picks_ref):
    me = lax.axis_index("seq")
    count, _, block = blocks_ref.shape
    table_rows = picks_ref.shape[0]
    slots = table_rows // 2
    capacity = slots // count
    halo = (table_rows - slots) // 2

    owners = jnp.concatenate(
        [blocks_ref[s, ROW_OWNER : ROW_OWNER + 1, :] for s in range(count)], axis=0
    ).astype(I32)
    earlier = (
        lax.broadcasted_iota(I32, (block, block), 0) < lax.broadcasted_iota(I32, (block, block), 1)
    ).astype(F32).astype(BF16)
    starts = lax.broadcasted_iota(I32, (count, block), 0) * capacity
    targets = []
    for step in (0, -1, 1):
        named = owners == me + step
        ranks = dot_ab(named.astype(F32).astype(BF16), earlier).astype(I32)
        slot_of = jnp.where(named, ranks + starts, -1)
        targets.append(jnp.concatenate([slot_of[s : s + 1] for s in range(count)], axis=1))
    tokens = count * block
    rows = lax.broadcasted_iota(I32, (slots, tokens), 0)
    picks_ref[0:slots] = (rows == targets[0]).astype(F32).astype(BF16)
    small = lax.broadcasted_iota(I32, (BLK, tokens), 0)
    for step, direction in ((-1, 1), (1, 0)):
        source = jnp.clip(me + step, 0, count - 1)
        border = blocks_ref[source, ROW_BORDER : ROW_BORDER + 2, :].astype(I32)
        target = targets[1 if step < 0 else 2]
        start = slots + (0 if step < 0 else halo)
        for i in range(halo // BLK):
            wanted = border[direction : direction + 1, i : i + 1] * BLK
            here = slice(start + i * BLK, start + (i + 1) * BLK)
            picks_ref[here] = (small + wanted == target).astype(F32).astype(BF16)


def decode_kernel(
    blocks_ref,
    picks_ref,
    mine_ref,
    other_ref,
    time_ref,
    proj_ref,
    map_ref,
    weight_ref,
    owned_ref,
    fine_ref,
    code_ref,
):
    is_cond = lax.axis_index("pair") == 0
    slots = owned_ref.shape[1]
    offsets = map_ref.shape[0]
    out_channels = fine_ref.shape[0]
    table_rows = code_ref.shape[2]

    cleans = []
    for s in range(blocks_ref.shape[0]):
        mine, other = mine_ref[s], other_ref[s]
        cond = jnp.where(is_cond, mine, other)
        uncond = jnp.where(is_cond, other, mine)
        guided = uncond + GUIDANCE * (cond - uncond)
        cleans.append(blocks_ref[s, 0:LAT, :] - time_ref[0] * guided)
    clean = jnp.concatenate(cleans, axis=1)

    parts = jnp.concatenate(split_three(clean), axis=0).astype(BF16)
    spread = dot_abt(parts, picks_ref[...])
    table = spread[0:LAT] + spread[LAT : 2 * LAT] + spread[2 * LAT :]
    owned_ref[...] = table[:, 0:slots]

    proj_high, proj_low = split_two(proj_ref[...])
    table_high, table_low = split_two(table)
    left = jnp.concatenate([proj_high, proj_high, proj_low, jnp.zeros_like(proj_low)], axis=0)
    right = jnp.concatenate([table_high, table_low, table_high, jnp.zeros_like(table_low)], axis=0)
    before = dot_atb(left.astype(BF16), right.astype(BF16))
    features = (0.5 * before * (1.0 + jnp.tanh(0.5 * before))).astype(BF16)

    count = 3
    groups = [range(k, min(k + count, offsets)) for k in range(0, offsets, count)]

    def multiply(group):
        rows = weight_ref[group[0] * out_channels : (group[-1] + 1) * out_channels]
        return dot_ab(rows, features)

    def code(group, product):
        top = jnp.max(jnp.abs(product), axis=0, keepdims=True)
        top = jnp.maximum(jnp.max(top, axis=1, keepdims=True), TINY)
        scaled = product * (CODE_TOP / top)
        high = scaled.astype(F8)
        low = (scaled - high.astype(F32)).astype(F8)
        for i, k in enumerate(group):
            rows = slice(i * out_channels, (i + 1) * out_channels)
            code_ref[k, 0:out_channels] = high[rows]
            code_ref[k, out_channels : 2 * out_channels] = low[rows]
        return top * (1.0 / CODE_TOP)

    units = []
    ready = multiply(groups[0])
    for i, group in enumerate(groups):
        product = ready
        if i + 1 < len(groups):
            ready = multiply(groups[i + 1])
        units.append(code(group, product))

    fine = map_ref.shape[2]
    width = 256
    table_ids = lax.broadcasted_iota(jnp.int16, (table_rows, width), 0)
    one = jnp.ones((table_rows, width), F8)
    zero = jnp.zeros((table_rows, width), F8)
    for f in range(fine // width):
        here = slice(f * width, (f + 1) * width)
        total = jnp.zeros((out_channels, width), F32)
        for group, unit in zip(groups, units):
            part = jnp.zeros((2 * out_channels, width), F32)
            for k in group:
                index = jnp.broadcast_to(map_ref[k, :, here], (16, width)).astype(jnp.int16)
                index = jnp.broadcast_to(index[None], (table_rows // 16, 16, width))
                chosen = jnp.where(table_ids == index.reshape(table_rows, width), one, zero)
                part = part + dot_ab(code_ref[k], chosen)
            total = total + (part[0:out_channels] + part[out_channels:]) * unit
        fine_ref[:, here] = total.astype(BF16)


def route_call(blocks, table_rows):
    count, _, block = blocks.shape
    return pl.pallas_call(
        route_kernel,
        out_shape=pltpu.VMEM((table_rows, count * block), BF16),
        in_specs=[VMEM],
        out_specs=VMEM,
        compiler_params=pltpu.CompilerParams(vmem_limit_bytes=VMEM_GRANT),
        cost_estimate=pl.CostEstimate(flops=0, bytes_accessed=1 << 20, transcendentals=0),
        name="route",
    )(blocks)


def decode_call(
    blocks, picks, velocity, partner, step_time, decoder_projection, index_rows, weights
):
    offsets, _, fine = index_rows.shape
    out_channels = weights.shape[0] // offsets
    slots = fine // 4
    table_rows = picks.shape[0]
    return pl.pallas_call(
        decode_kernel,
        out_shape=(
            jax.ShapeDtypeStruct((LAT, slots), F32),
            jax.ShapeDtypeStruct((out_channels, fine), BF16),
        ),
        in_specs=[VMEM, VMEM, VMEM, VMEM, SMEM, VMEM, VMEM, VMEM],
        out_specs=(VMEM, VMEM),
        scratch_shapes=[pltpu.VMEM((offsets, 2 * out_channels, table_rows), F8)],
        compiler_params=pltpu.CompilerParams(vmem_limit_bytes=VMEM_GRANT),
        name="decode",
    )(blocks, picks, velocity, partner, step_time, decoder_projection, index_rows, weights)


def swap_pair(x):
    return lax.ppermute(x, "pair", [(0, 1), (1, 0)])


def seq_swap(x, distance_of):
    count = lax.axis_size("seq")
    routes = [
        (p * count + (z ^ distance_of[p]), p * count + z) for p in range(2) for z in range(count)
    ]
    return lax.ppermute(x, ("pair", "seq"), routes)


def pack_operands(latents, voxel_coords, owner_map, border_blocks):
    return in_hbm(
        latents[0],
        jnp.swapaxes(voxel_coords, 0, 1),
        owner_map.reshape(1, -1),
        border_blocks[0, 0],
    )


def pack_scratch(block, border_blocks):
    return [
        pltpu.VMEM((3, 1, block), I32),
        pltpu.VMEM((1, block), I32),
        pltpu.VMEM(border_blocks.shape[2:], I32),
    ]


def whole_asset_velocity(
    placed, modulation, in_proj, qkv_proj, norm_gain, out_proj, head_proj
):
    latents, _, _, border_blocks = placed
    count = lax.axis_size("seq")
    block = latents.shape[2]
    tokens = count * block
    width = in_proj.shape[1]
    inner = out_proj.shape[0]
    pos = jnp.asarray(position_parts(width))
    block_shapes = (
        pltpu.VMEM((block, width), F32),
        pltpu.VMEM((block, inner), BF16),
        pltpu.VMEM((block, inner), BF16),
        pltpu.VMEM((inner // 128, block, 128), BF16),
    )
    held_shapes = (
        pltpu.VMEM((5, 1, width), F32),
        pltpu.VMEM(qkv_proj.shape, BF16),
        pltpu.VMEM(norm_gain.shape, F32),
        pltpu.VMEM(out_proj.shape, BF16),
        pltpu.VMEM((LAT, width), F32),
        pltpu.VMEM((pos.shape[0] + 32, width), BF16),
        *block_shapes,
    )
    block_cost = pl.CostEstimate(
        flops=2 * block * width * 4 * inner, bytes_accessed=6 << 20, transcendentals=0
    )
    params = pltpu.CompilerParams(vmem_limit_bytes=VMEM_GRANT)
    sources = in_hbm(
        modulation[0, 0][:, None, :],
        in_proj,
        qkv_proj,
        norm_gain,
        out_proj,
        head_proj.T,
        pos,
    )
    weight_scratch = [pltpu.VMEM(in_proj.shape, F32)]
    weight_sems = pltpu.SemaphoreType.DMA((len(sources),))
    packed, *held = pl.pallas_call(
        early_kernel,
        out_shape=(pltpu.VMEM((PACK_ROWS, block), F32), *held_shapes),
        in_specs=[HBM] * 11,
        out_specs=(VMEM,) * 11,
        scratch_shapes=[
            *pack_scratch(block, border_blocks),
            *weight_scratch,
            pltpu.SemaphoreType.DMA((4,)),
            weight_sems,
        ],
        compiler_params=params,
        name="pack_own_block",
    )(*pack_operands(*placed), *sources)
    first = seq_swap(packed, (3, 2))
    near = seq_swap(packed, (1, 1))
    swapped = swap_pair(first)
    held = pl.pallas_call(
        late_kernel,
        out_shape=held_shapes,
        in_specs=[VMEM] + [HBM] * 7 + [VMEM] * 10,
        out_specs=(VMEM,) * 10,
        scratch_shapes=[*weight_scratch, weight_sems],
        input_output_aliases={8 + i: i for i in range(10)},
        compiler_params=params,
        cost_estimate=block_cost,
        name="own_block",
    )(packed, *sources, *held)
    weights, own_state = held[:6], held[6:]
    mod_rows, qkv_rows, gains, _, _, table = weights
    near_state = pl.pallas_call(
        near_kernel,
        out_shape=block_shapes,
        in_specs=[VMEM] * 6,
        out_specs=(VMEM,) * 4,
        compiler_params=pltpu.CompilerParams(vmem_limit_bytes=VMEM_GRANT),
        cost_estimate=block_cost,
        name="near_block",
    )(near, first, mod_rows, qkv_rows, gains, table)
    return pl.pallas_call(
        velocity_kernel,
        out_shape=(
            pltpu.VMEM((count, LAT, block), F32),
            pltpu.VMEM((count, PACK_ROWS, block), F32),
        ),
        in_specs=[VMEM] * 18,
        out_specs=(VMEM, VMEM),
        scratch_shapes=[
            pltpu.VMEM((tokens, width), F32),
            pltpu.VMEM((tokens, width), BF16),
            pltpu.VMEM((tokens, inner), BF16),
            pltpu.VMEM((tokens, inner), BF16),
            pltpu.VMEM((inner // 128, tokens, 256), BF16),
            pltpu.VMEM((tokens, inner), BF16),
        ],
        compiler_params=pltpu.CompilerParams(vmem_limit_bytes=VMEM_GRANT),
        name="velocity",
    )(packed, near, first, swapped, *weights, *own_state, *near_state)


def pack_call(latents, voxel_coords, owner_map, border_blocks):
    block = latents.shape[2]
    return pl.pallas_call(
        pack_kernel,
        out_shape=pltpu.VMEM((PACK_ROWS, block), F32),
        in_specs=[HBM] * 4,
        out_specs=VMEM,
        scratch_shapes=[*pack_scratch(block, border_blocks), pltpu.SemaphoreType.DMA((4,))],
        compiler_params=pltpu.CompilerParams(vmem_limit_bytes=VMEM_GRANT),
        name="pack",
    )(*pack_operands(latents, voxel_coords, owner_map, border_blocks))


def layer_norm(values):
    center = values - jnp.mean(values, axis=-1, keepdims=True)
    variance = jnp.mean(center * center, axis=-1, keepdims=True)
    return center / jnp.sqrt(variance + EPSILON)


def position_table(coord_rows, model_width):
    freqs = model_width // 6
    steps = jnp.arange(freqs, dtype=F32) / freqs
    omegas = jnp.exp(-math.log(10000.0) * steps)
    angles = coord_rows.astype(F32)[:, :, None] * omegas[None, None, :]
    halves = jnp.concatenate([jnp.sin(angles), jnp.cos(angles)], axis=2)
    rows_out = jnp.transpose(halves, (1, 0, 2)).reshape(coord_rows.shape[1], 6 * freqs)
    return jnp.pad(rows_out, ((0, 0), (0, model_width - 6 * freqs)))


def head_norm(values, gains):
    row_count = values.shape[0]
    per_head = values.reshape(row_count, HEADS, HEAD)
    mean_square = jnp.mean(per_head * per_head, axis=2, keepdims=True)
    return (per_head / jnp.sqrt(mean_square + EPSILON)).reshape(row_count, HEADS * HEAD) * gains


def gathered_velocity(
    latent_block, coords, modulation, in_proj, qkv_proj, norm_gain, out_proj, head_proj
):
    token_count = latent_block.shape[1]
    model_width = in_proj.shape[1]
    inner_width = out_proj.shape[0]
    factor = HEAD ** (-0.5)
    mod_rows = modulation[0, 0]
    hidden = jnp.dot(latent_block.T, in_proj, precision=TOP_PRECISION) + position_table(
        coords, model_width
    )
    normed = (layer_norm(hidden) * (1.0 + mod_rows[1]) + mod_rows[0]).astype(BF16)
    projected = jnp.dot(normed, qkv_proj, preferred_element_type=F32)
    queries = head_norm(projected[:, :inner_width], norm_gain[0]).astype(BF16)
    keys_in = head_norm(projected[:, inner_width : 2 * inner_width], norm_gain[1]).astype(BF16)
    values_in = projected[:, 2 * inner_width :].astype(BF16)
    query_heads = queries.reshape(token_count, HEADS, HEAD)
    start_pair = (
        jnp.zeros((token_count, HEADS, HEAD), F32),
        jnp.zeros((token_count, HEADS), F32),
    )
    key_rows = lax.all_gather(keys_in, "seq", axis=0, tiled=True)
    value_rows = lax.all_gather(values_in, "seq", axis=0, tiled=True)
    row_count = key_rows.shape[0]
    block_rows = math.gcd(row_count, 512)
    key_blocks = key_rows.reshape(row_count // block_rows, block_rows, HEADS, HEAD)
    value_blocks = value_rows.reshape(row_count // block_rows, block_rows, HEADS, HEAD)

    def one_block(running, block_pair):
        numer_run, denom_run = running
        key_block, value_block = block_pair
        scores = (
            jnp.einsum("qhd,khd->hqk", query_heads, key_block, preferred_element_type=F32) * factor
        )
        exp_scores = jnp.exp(scores)
        numer_run = numer_run + jnp.einsum(
            "hqk,khd->qhd", exp_scores.astype(BF16), value_block, preferred_element_type=F32
        )
        denom_run = denom_run + jnp.sum(exp_scores, axis=2).T
        return ((numer_run, denom_run), None)

    (numerator, denominator), _ = lax.scan(one_block, start_pair, (key_blocks, value_blocks))
    attended = (
        (numerator / denominator[:, :, None]).reshape(token_count, inner_width).astype(BF16)
    )
    hidden = hidden + mod_rows[2] * jnp.dot(attended, out_proj, preferred_element_type=F32)
    final = layer_norm(hidden) * (1.0 + mod_rows[4]) + mod_rows[3]
    velocity = jnp.dot(final, head_proj, precision=TOP_PRECISION).T
    return lax.all_gather(velocity, "seq", axis=0)


def per_device(
    latents,
    voxel_coords,
    owner_map,
    step_time,
    modulation,
    in_proj,
    qkv_proj,
    norm_gain,
    out_proj,
    head_proj,
    decoder_projection,
    border_blocks,
    kernel_map,
    conv_weight,
):
    count = lax.axis_size("seq")
    block = latents.shape[2]
    placed = (latents, voxel_coords, owner_map, border_blocks)
    if count == 4 and count * block <= WHOLE_ASSET:
        velocity, blocks = whole_asset_velocity(
            placed, modulation, in_proj, qkv_proj, norm_gain, out_proj, head_proj
        )
    else:
        blocks = lax.all_gather(pack_call(*placed), "seq", axis=0)
        velocity = gathered_velocity(
            latents[0],
            voxel_coords[0],
            modulation,
            in_proj,
            qkv_proj,
            norm_gain,
            out_proj,
            head_proj,
        )
    partner = swap_pair(velocity)
    picks = route_call(blocks, kernel_map.shape[3] // 2)
    offsets, _, out_channels = conv_weight.shape
    fine = kernel_map.shape[3]
    owned, decoded = decode_call(
        blocks,
        picks,
        velocity,
        partner,
        step_time,
        decoder_projection,
        kernel_map.reshape(offsets, 1, fine),
        jnp.swapaxes(conv_weight, 1, 2).reshape(offsets * out_channels, -1),
    )
    return (owned[None, None], decoded.T[None, None])


def solution(mesh):
    placed = (
        P("asset", None, "seq"),
        P("asset", None, "seq"),
        P("asset", "seq", None),
        P("asset"),
        P("asset", "pair", None, None),
        P(),
        P(),
        P(),
        P(),
        P(),
        P(),
        P("asset", "seq", None, None),
        P("asset", "seq", None, None),
        P(None, None, "pair"),
    )
    return jax.shard_map(
        per_device,
        mesh=mesh,
        in_specs=placed,
        out_specs=(P("asset", "seq", None, None), P("asset", "seq", None, "pair")),
        check_vma=False,
    )
```

```python
import functools
import math

import jax
import jax.numpy as jnp
import numpy as np
from jax import lax
from jax.experimental import pallas as pl
from jax.experimental.pallas import tpu as pltpu
from jax.sharding import PartitionSpec as P

HEADS = 8
HEAD = 64
LAT = 8
BLK = 16
RES = 64

EPSILON = 1e-06
GUIDANCE = 3.0
TOP_PRECISION = lax.Precision.HIGHEST
F32 = jnp.float32
BF16 = jnp.bfloat16
I32 = jnp.int32
F8 = jnp.float8_e4m3fn
CODE_TOP = 256.0
TINY = 1e-30

ROW_COORD = 8
ROW_OWNER = 11
ROW_BORDER = 12
PACK_ROWS = 16
WHOLE_ASSET = 512

VMEM_GRANT = 40 << 20

VMEM = pl.BlockSpec(memory_space=pltpu.VMEM)
HBM = pl.BlockSpec(memory_space=pltpu.HBM)
SMEM = pl.BlockSpec(memory_space=pltpu.SMEM)


def dot_ab(a, b):
    return jnp.dot(a, b, preferred_element_type=F32)


def dot_abt(a, b):
    return lax.dot_general(a, b, (((1,), (1,)), ((), ())), preferred_element_type=F32)


def dot_atb(a, b):
    return lax.dot_general(a, b, (((0,), (0,)), ((), ())), preferred_element_type=F32)


def in_hbm(*arrays):
    return [pltpu.with_memory_space_constraint(x, pltpu.HBM) for x in arrays]


def split_two(x):
    high = x.astype(BF16).astype(F32)
    return high, x - high


def split_three(x):
    high, rest = split_two(x)
    mid, low = split_two(rest)
    return high, mid, low


@functools.lru_cache(None)
def position_parts(model_width):
    freqs = model_width // 6
    steps = np.arange(freqs, dtype=np.float32) / np.float32(freqs)
    omegas = np.exp(np.float32(-math.log(10000.0)) * steps).astype(np.float32)
    angles = (np.arange(RES, dtype=np.float32)[:, None] * omegas[None, :]).astype(np.float64)
    halves = np.concatenate([np.sin(angles), np.cos(angles)], axis=1).astype(np.float32)
    table = np.zeros((3 * RES, model_width), np.float32)
    for c in range(3):
        table[c * RES : (c + 1) * RES, c * 2 * freqs : (c + 1) * 2 * freqs] = halves
    high = table.astype(jnp.bfloat16)
    low = (table - high.astype(np.float32)).astype(jnp.bfloat16)
    return np.concatenate([high, low], axis=0)


def pack_kernel(
    lat_hbm, coord_hbm, owner_hbm, border_hbm, pack_ref, coord_ref, owner_ref, border_ref, sems
):
    pack_ref[...] = jnp.zeros_like(pack_ref)
    copies = [
        pltpu.make_async_copy(source, target, sems.at[i])
        for i, (source, target) in enumerate(
            (
                (lat_hbm, pack_ref.at[0:LAT]),
                (coord_hbm, coord_ref),
                (owner_hbm, owner_ref),
                (border_hbm, border_ref),
            )
        )
    ]
    for copy in copies:
        copy.start()
    for copy in copies:
        copy.wait()
    for c in range(3):
        pack_ref[ROW_COORD + c : ROW_COORD + c + 1] = coord_ref[c].astype(F32)
    pack_ref[ROW_OWNER : ROW_OWNER + 1] = owner_ref[...].astype(F32)
    pack_ref[ROW_BORDER : ROW_BORDER + 2, 0 : border_ref.shape[1]] = border_ref[...].astype(F32)


def hidden_rows(rows, table_ref):
    block = rows.shape[1]
    values = lax.broadcasted_iota(I32, (RES, block), 0).astype(F32)
    hots = [
        (values == rows[ROW_COORD + c : ROW_COORD + c + 1]).astype(F32).astype(BF16)
        for c in range(3)
    ]
    high, low = split_two(rows[0:LAT])
    tail = jnp.concatenate([high, low, high, jnp.zeros_like(low)], axis=0).astype(BF16)
    return dot_atb(jnp.concatenate(hots + hots + [tail], axis=0), table_ref[...])


def modulated(hidden, mod_ref):
    center = hidden - jnp.mean(hidden, axis=1, keepdims=True)
    inverse = lax.rsqrt(jnp.mean(center * center, axis=1, keepdims=True) + EPSILON)
    return (center * inverse * (1.0 + mod_ref[1]) + mod_ref[0]).astype(BF16)


def project(normed, qkv_ref, gain_ref, query_ref, key_ref, value_ref, rows):
    inner = gain_ref.shape[1]
    group = 256
    same_head = (
        lax.broadcasted_iota(I32, (group, group), 0) // HEAD
        == lax.broadcasted_iota(I32, (group, group), 1) // HEAD
    )
    averager = jnp.where(same_head, 1.0 / HEAD, 0.0).astype(BF16)

    def finish(j, projected):
        which, col = divmod(j * group, inner)
        if which == 2:
            for half in range(group // 128):
                lanes = slice(half * 128, (half + 1) * 128)
                value_ref[col // 128 + half, rows] = projected[:, lanes].astype(BF16)
        else:
            square = dot_ab((projected * projected).astype(BF16), averager)
            gains = gain_ref[which : which + 1, col : col + group]
            if which == 0:
                gains = gains * (HEAD**-0.5)
            result = (projected * lax.rsqrt(square + EPSILON) * gains).astype(BF16)
            (query_ref, key_ref)[which][rows, col : col + group] = result

    previous = None
    for j in range(3 * inner // group):
        projected = dot_ab(normed, qkv_ref[:, j * group : (j + 1) * group])
        if previous is not None:
            finish(*previous)
        previous = (j, projected)
    finish(*previous)


def first_kernel(
    own_ref,
    mixed_ref,
    mod_hbm,
    in_hbm,
    qkv_hbm,
    gain_hbm,
    out_hbm,
    head_hbm,
    pos_hbm,
    mod_ref,
    qkv_ref,
    gain_ref,
    out_ref,
    head_ref,
    table_ref,
    hidden_ref,
    query_ref,
    key_ref,
    value_ref,
    in_ref,
    normed_ref,
    sems,
):
    pos_rows = pos_hbm.shape[0]
    copies = [
        pltpu.make_async_copy(source, target, sems.at[i])
        for i, (source, target) in enumerate(
            (
                (pos_hbm, table_ref.at[0:pos_rows]),
                (in_hbm, in_ref),
                (mod_hbm, mod_ref),
                (gain_hbm, gain_ref),
                (qkv_hbm, qkv_ref),
                (head_hbm, head_ref),
                (out_hbm, out_ref),
            )
        )
    ]
    for copy in copies:
        copy.start()
    for copy in copies[:4]:
        copy.wait()
    in_high, in_low = split_two(in_ref[...])
    table_ref[pos_rows : pos_rows + 32, :] = jnp.concatenate(
        [in_high, in_high, in_low, jnp.zeros_like(in_low)], axis=0
    ).astype(BF16)
    block = own_ref.shape[1]
    hiddens = [hidden_rows(source[...], table_ref) for source in (own_ref, mixed_ref)]
    for s, hidden in enumerate(hiddens):
        hidden_ref[s * block : (s + 1) * block, :] = hidden
        normed_ref[s * block : (s + 1) * block, :] = modulated(hidden, mod_ref)
    copies[4].wait()
    rows = slice(0, len(hiddens) * block)
    project(normed_ref[...], qkv_ref, gain_ref, query_ref, key_ref, value_ref, rows)
    copies[5].wait()
    copies[6].wait()


def velocity_kernel(
    own_ref,
    mixed_ref,
    swapped_ref,
    far_ref,
    mod_ref,
    qkv_ref,
    gain_ref,
    out_ref,
    head_ref,
    table_ref,
    done_hidden_ref,
    done_query_ref,
    done_key_ref,
    done_value_ref,
    vel_ref,
    blocks_ref,
    hidden_ref,
    normed_ref,
    query_ref,
    key_ref,
    value_ref,
    att_ref,
):
    me = lax.axis_index("seq")
    side = lax.axis_index("pair")
    width = qkv_ref.shape[0]
    tokens = hidden_ref.shape[0]
    inner = out_ref.shape[0]
    block = own_ref.shape[1]
    places = (me, me ^ (1 + side), me ^ (2 - side), me ^ 3)
    sources = (own_ref, mixed_ref, swapped_ref, far_ref)
    for place, source in zip(places, sources):
        blocks_ref[place] = source[...]

    done = done_hidden_ref.shape[0] // block
    here = slice(0, done * block)
    ready = hidden_rows(sources[done][...], table_ref)
    hidden_ref[here, :] = done_hidden_ref[...]
    query_ref[here, :] = done_query_ref[...]
    key_ref[here, :] = done_key_ref[...]
    for pair in range(inner // 128):
        value_ref[pair, here] = done_value_ref[pair]
    for s in range(done, len(sources)):
        hidden = ready
        if s + 1 < len(sources):
            ready = hidden_rows(sources[s + 1][...], table_ref)
        hidden_ref[s * block : (s + 1) * block, :] = hidden
        normed_ref[s * block : (s + 1) * block, :] = modulated(hidden, mod_ref)
    others = slice(done * block, tokens)
    project(normed_ref[others, :], qkv_ref, gain_ref, query_ref, key_ref, value_ref, others)

    chunk = min(tokens, 512)
    even = lax.broadcasted_iota(I32, (tokens, 128), 1) < HEAD
    ones_rows = jnp.ones((16, tokens), BF16)
    flipped = [value_ref[pair].T for pair in range(inner // 128)]
    todo = [
        (pair, half, q)
        for pair in range(inner // 128)
        for half in range(2)
        for q in range(tokens // chunk)
    ]

    def score(pair, half, q):
        lanes = slice(pair * 128, (pair + 1) * 128)
        keys = key_ref[:, lanes]
        kept = jnp.where(even == (half == 0), keys, jnp.zeros_like(keys))
        return dot_abt(kept, query_ref[q * chunk : (q + 1) * chunk, lanes])

    ready = [score(*item) for item in todo[:2]]
    for at, (pair, half, q) in enumerate(todo):
        scores = ready.pop(0)
        if at + 2 < len(todo):
            ready.append(score(*todo[at + 2]))
        values = flipped[pair][half * HEAD : (half + 1) * HEAD]
        values = jnp.concatenate([values, ones_rows], axis=0)
        sums = dot_ab(values, jnp.exp(scores).astype(BF16))
        dims = slice(pair * 128 + half * HEAD, pair * 128 + (half + 1) * HEAD)
        mean = sums[0:HEAD] / sums[HEAD : HEAD + 1]
        att_ref[dims, q * chunk : (q + 1) * chunk] = mean.astype(BF16)

    gate = mod_ref[2]
    head = head_ref[...]
    offset = jnp.sum(head * mod_ref[3], axis=1, keepdims=True)
    head_high, head_low = split_two(head * (1.0 + mod_ref[4]))
    heads = jnp.concatenate([head_high, head_low], axis=0).astype(BF16)
    ones = jnp.ones((16, width), BF16)
    step = 128
    def attended(q):
        return dot_atb(att_ref[:, q * step : (q + 1) * step], out_ref[...])
    def middle(q, product):
        hidden = hidden_ref[q * step : (q + 1) * step, :] + gate * product
        center = hidden - jnp.mean(hidden, axis=1, keepdims=True)
        high = center.astype(BF16)
        low = (center - high.astype(F32)).astype(BF16)
        return high, low
    def last(q, high, low):
        both = dot_abt(heads, high)
        rest = dot_abt(heads, low)
        square = dot_abt(ones, high * high)
        inverse = lax.rsqrt(square[0:LAT] * (1.0 / width) + EPSILON)
        velocity = (both[0:LAT] + both[LAT:] + rest[0:LAT]) * inverse + offset
        for i in range(step // block):
            vel_ref[places[q * (step // block) + i]] = velocity[:, i * block : (i + 1) * block]
    count = tokens // step
    product = attended(0)
    waiting = None
    for q in range(count):
        following = attended(q + 1) if q + 1 < count else None
        centered = middle(q, product)
        if waiting is not None:
            last(*waiting)
        waiting = (q, *centered)
        product = following
    last(*waiting)


def route_kernel(blocks_ref, picks_ref):
    me = lax.axis_index("seq")
    count, _, block = blocks_ref.shape
    table_rows = picks_ref.shape[0]
    slots = table_rows // 2
    capacity = slots // count
    halo = (table_rows - slots) // 2

    owners = jnp.concatenate(
        [blocks_ref[s, ROW_OWNER : ROW_OWNER + 1, :] for s in range(count)], axis=0
    ).astype(I32)
    earlier = (
        lax.broadcasted_iota(I32, (block, block), 0) < lax.broadcasted_iota(I32, (block, block), 1)
    ).astype(F32).astype(BF16)
    starts = lax.broadcasted_iota(I32, (count, block), 0) * capacity
    targets = []
    for step in (0, -1, 1):
        named = owners == me + step
        ranks = dot_ab(named.astype(F32).astype(BF16), earlier).astype(I32)
        slot_of = jnp.where(named, ranks + starts, -1)
        targets.append(jnp.concatenate([slot_of[s : s + 1] for s in range(count)], axis=1))
    tokens = count * block
    rows = lax.broadcasted_iota(I32, (slots, tokens), 0)
    picks_ref[0:slots] = (rows == targets[0]).astype(F32).astype(BF16)
    small = lax.broadcasted_iota(I32, (BLK, tokens), 0)
    for step, direction in ((-1, 1), (1, 0)):
        source = jnp.clip(me + step, 0, count - 1)
        border = blocks_ref[source, ROW_BORDER : ROW_BORDER + 2, :].astype(I32)
        target = targets[1 if step < 0 else 2]
        start = slots + (0 if step < 0 else halo)
        for i in range(halo // BLK):
            wanted = border[direction : direction + 1, i : i + 1] * BLK
            here = slice(start + i * BLK, start + (i + 1) * BLK)
            picks_ref[here] = (small + wanted == target).astype(F32).astype(BF16)


def decode_kernel(
    blocks_ref,
    picks_ref,
    mine_ref,
    other_ref,
    time_ref,
    proj_ref,
    map_ref,
    weight_ref,
    owned_ref,
    fine_ref,
    code_ref,
):
    is_cond = lax.axis_index("pair") == 0
    slots = owned_ref.shape[1]
    offsets = map_ref.shape[0]
    out_channels = fine_ref.shape[0]
    table_rows = code_ref.shape[2]

    cleans = []
    for s in range(blocks_ref.shape[0]):
        mine, other = mine_ref[s], other_ref[s]
        cond = jnp.where(is_cond, mine, other)
        uncond = jnp.where(is_cond, other, mine)
        guided = uncond + GUIDANCE * (cond - uncond)
        cleans.append(blocks_ref[s, 0:LAT, :] - time_ref[0] * guided)
    clean = jnp.concatenate(cleans, axis=1)

    parts = jnp.concatenate(split_three(clean), axis=0).astype(BF16)
    spread = dot_abt(parts, picks_ref[...])
    table = spread[0:LAT] + spread[LAT : 2 * LAT] + spread[2 * LAT :]
    owned_ref[...] = table[:, 0:slots]

    proj_high, proj_low = split_two(proj_ref[...])
    table_high, table_low = split_two(table)
    left = jnp.concatenate([proj_high, proj_high, proj_low, jnp.zeros_like(proj_low)], axis=0)
    right = jnp.concatenate([table_high, table_low, table_high, jnp.zeros_like(table_low)], axis=0)
    before = dot_atb(left.astype(BF16), right.astype(BF16))
    features = (0.5 * before * (1.0 + jnp.tanh(0.5 * before))).astype(BF16)

    count = 3
    groups = [range(k, min(k + count, offsets)) for k in range(0, offsets, count)]

    def multiply(group):
        rows = weight_ref[group[0] * out_channels : (group[-1] + 1) * out_channels]
        return dot_ab(rows, features)

    def code(group, product):
        top = jnp.max(jnp.abs(product), axis=0, keepdims=True)
        top = jnp.maximum(jnp.max(top, axis=1, keepdims=True), TINY)
        scaled = product * (CODE_TOP / top)
        high = scaled.astype(F8)
        low = (scaled - high.astype(F32)).astype(F8)
        for i, k in enumerate(group):
            rows = slice(i * out_channels, (i + 1) * out_channels)
            code_ref[k, 0:out_channels] = high[rows]
            code_ref[k, out_channels : 2 * out_channels] = low[rows]
        return top * (1.0 / CODE_TOP)

    units = []
    ready = multiply(groups[0])
    for i, group in enumerate(groups):
        product = ready
        if i + 1 < len(groups):
            ready = multiply(groups[i + 1])
        units.append(code(group, product))

    fine = map_ref.shape[2]
    width = 256
    table_ids = lax.broadcasted_iota(jnp.int16, (table_rows, width), 0)
    one = jnp.ones((table_rows, width), F8)
    zero = jnp.zeros((table_rows, width), F8)
    for f in range(fine // width):
        here = slice(f * width, (f + 1) * width)
        total = jnp.zeros((out_channels, width), F32)
        for group, unit in zip(groups, units):
            part = jnp.zeros((2 * out_channels, width), F32)
            for k in group:
                index = jnp.broadcast_to(map_ref[k, :, here], (16, width)).astype(jnp.int16)
                index = jnp.broadcast_to(index[None], (table_rows // 16, 16, width))
                chosen = jnp.where(table_ids == index.reshape(table_rows, width), one, zero)
                part = part + dot_ab(code_ref[k], chosen)
            total = total + (part[0:out_channels] + part[out_channels:]) * unit
        fine_ref[:, here] = total.astype(BF16)


def route_call(blocks, table_rows):
    count, _, block = blocks.shape
    return pl.pallas_call(
        route_kernel,
        out_shape=pltpu.VMEM((table_rows, count * block), BF16),
        in_specs=[VMEM],
        out_specs=VMEM,
        compiler_params=pltpu.CompilerParams(vmem_limit_bytes=VMEM_GRANT),
        cost_estimate=pl.CostEstimate(flops=0, bytes_accessed=1 << 20, transcendentals=0),
        name="route",
    )(blocks)


def decode_call(
    blocks, picks, velocity, partner, step_time, decoder_projection, index_rows, weights
):
    offsets, _, fine = index_rows.shape
    out_channels = weights.shape[0] // offsets
    slots = fine // 4
    table_rows = picks.shape[0]
    return pl.pallas_call(
        decode_kernel,
        out_shape=(
            jax.ShapeDtypeStruct((LAT, slots), F32),
            jax.ShapeDtypeStruct((out_channels, fine), BF16),
        ),
        in_specs=[VMEM, VMEM, VMEM, VMEM, SMEM, VMEM, VMEM, VMEM],
        out_specs=(VMEM, VMEM),
        scratch_shapes=[pltpu.VMEM((offsets, 2 * out_channels, table_rows), F8)],
        compiler_params=pltpu.CompilerParams(vmem_limit_bytes=VMEM_GRANT),
        name="decode",
    )(blocks, picks, velocity, partner, step_time, decoder_projection, index_rows, weights)


def swap_pair(x):
    return lax.ppermute(x, "pair", [(0, 1), (1, 0)])


def seq_swap(x, distance_of):
    count = lax.axis_size("seq")
    routes = [
        (p * count + (z ^ distance_of[p]), p * count + z) for p in range(2) for z in range(count)
    ]
    return lax.ppermute(x, ("pair", "seq"), routes)


def whole_asset_velocity(packed, modulation, in_proj, qkv_proj, norm_gain, out_proj, head_proj):
    count = lax.axis_size("seq")
    block = packed.shape[1]
    tokens = count * block
    width = in_proj.shape[1]
    inner = out_proj.shape[0]
    far = seq_swap(packed, (3, 3))
    mixed = seq_swap(packed, (1, 2))
    swapped = swap_pair(mixed)
    pos = jnp.asarray(position_parts(width))
    held = pl.pallas_call(
        first_kernel,
        out_shape=(
            pltpu.VMEM((5, 1, width), F32),
            pltpu.VMEM(qkv_proj.shape, BF16),
            pltpu.VMEM(norm_gain.shape, F32),
            pltpu.VMEM(out_proj.shape, BF16),
            pltpu.VMEM((LAT, width), F32),
            pltpu.VMEM((pos.shape[0] + 32, width), BF16),
            pltpu.VMEM((2 * block, width), F32),
            pltpu.VMEM((2 * block, inner), BF16),
            pltpu.VMEM((2 * block, inner), BF16),
            pltpu.VMEM((inner // 128, 2 * block, 128), BF16),
        ),
        in_specs=[VMEM] * 2 + [HBM] * 7,
        out_specs=(VMEM,) * 10,
        scratch_shapes=[
            pltpu.VMEM(in_proj.shape, F32),
            pltpu.VMEM((2 * block, width), BF16),
            pltpu.SemaphoreType.DMA((7,)),
        ],
        compiler_params=pltpu.CompilerParams(vmem_limit_bytes=VMEM_GRANT),
        cost_estimate=pl.CostEstimate(
            flops=4 * block * width * 4 * inner, bytes_accessed=6 << 20, transcendentals=0
        ),
        name="first_blocks",
    )(
        packed,
        mixed,
        *in_hbm(
            modulation[0, 0][:, None, :],
            in_proj,
            qkv_proj,
            norm_gain,
            out_proj,
            head_proj.T,
            pos,
        ),
    )
    return pl.pallas_call(
        velocity_kernel,
        out_shape=(
            pltpu.VMEM((count, LAT, block), F32),
            pltpu.VMEM((count, PACK_ROWS, block), F32),
        ),
        in_specs=[VMEM] * 14,
        out_specs=(VMEM, VMEM),
        scratch_shapes=[
            pltpu.VMEM((tokens, width), F32),
            pltpu.VMEM((tokens, width), BF16),
            pltpu.VMEM((tokens, inner), BF16),
            pltpu.VMEM((tokens, inner), BF16),
            pltpu.VMEM((inner // 128, tokens, 128), BF16),
            pltpu.VMEM((inner, tokens), BF16),
        ],
        compiler_params=pltpu.CompilerParams(vmem_limit_bytes=VMEM_GRANT),
        name="velocity",
    )(packed, mixed, swapped, far, *held)


def layer_norm(values):
    center = values - jnp.mean(values, axis=-1, keepdims=True)
    variance = jnp.mean(center * center, axis=-1, keepdims=True)
    return center / jnp.sqrt(variance + EPSILON)


def position_table(coord_rows, model_width):
    freqs = model_width // 6
    steps = jnp.arange(freqs, dtype=F32) / freqs
    omegas = jnp.exp(-math.log(10000.0) * steps)
    angles = coord_rows.astype(F32)[:, :, None] * omegas[None, None, :]
    halves = jnp.concatenate([jnp.sin(angles), jnp.cos(angles)], axis=2)
    rows_out = jnp.transpose(halves, (1, 0, 2)).reshape(coord_rows.shape[1], 6 * freqs)
    return jnp.pad(rows_out, ((0, 0), (0, model_width - 6 * freqs)))


def head_norm(values, gains):
    row_count = values.shape[0]
    per_head = values.reshape(row_count, HEADS, HEAD)
    mean_square = jnp.mean(per_head * per_head, axis=2, keepdims=True)
    return (per_head / jnp.sqrt(mean_square + EPSILON)).reshape(row_count, HEADS * HEAD) * gains


def gathered_velocity(
    latent_block, coords, modulation, in_proj, qkv_proj, norm_gain, out_proj, head_proj
):
    token_count = latent_block.shape[1]
    model_width = in_proj.shape[1]
    inner_width = out_proj.shape[0]
    factor = HEAD ** (-0.5)
    mod_rows = modulation[0, 0]
    hidden = jnp.dot(latent_block.T, in_proj, precision=TOP_PRECISION) + position_table(
        coords, model_width
    )
    normed = (layer_norm(hidden) * (1.0 + mod_rows[1]) + mod_rows[0]).astype(BF16)
    projected = jnp.dot(normed, qkv_proj, preferred_element_type=F32)
    queries = head_norm(projected[:, :inner_width], norm_gain[0]).astype(BF16)
    keys_in = head_norm(projected[:, inner_width : 2 * inner_width], norm_gain[1]).astype(BF16)
    values_in = projected[:, 2 * inner_width :].astype(BF16)
    query_heads = queries.reshape(token_count, HEADS, HEAD)
    start_pair = (
        jnp.zeros((token_count, HEADS, HEAD), F32),
        jnp.zeros((token_count, HEADS), F32),
    )
    key_rows = lax.all_gather(keys_in, "seq", axis=0, tiled=True)
    value_rows = lax.all_gather(values_in, "seq", axis=0, tiled=True)
    row_count = key_rows.shape[0]
    block_rows = math.gcd(row_count, 512)
    key_blocks = key_rows.reshape(row_count // block_rows, block_rows, HEADS, HEAD)
    value_blocks = value_rows.reshape(row_count // block_rows, block_rows, HEADS, HEAD)

    def one_block(running, block_pair):
        numer_run, denom_run = running
        key_block, value_block = block_pair
        scores = (
            jnp.einsum("qhd,khd->hqk", query_heads, key_block, preferred_element_type=F32) * factor
        )
        exp_scores = jnp.exp(scores)
        numer_run = numer_run + jnp.einsum(
            "hqk,khd->qhd", exp_scores.astype(BF16), value_block, preferred_element_type=F32
        )
        denom_run = denom_run + jnp.sum(exp_scores, axis=2).T
        return ((numer_run, denom_run), None)

    (numerator, denominator), _ = lax.scan(one_block, start_pair, (key_blocks, value_blocks))
    attended = (
        (numerator / denominator[:, :, None]).reshape(token_count, inner_width).astype(BF16)
    )
    hidden = hidden + mod_rows[2] * jnp.dot(attended, out_proj, preferred_element_type=F32)
    final = layer_norm(hidden) * (1.0 + mod_rows[4]) + mod_rows[3]
    velocity = jnp.dot(final, head_proj, precision=TOP_PRECISION).T
    return lax.all_gather(velocity, "seq", axis=0)


def per_device(
    latents,
    voxel_coords,
    owner_map,
    step_time,
    modulation,
    in_proj,
    qkv_proj,
    norm_gain,
    out_proj,
    head_proj,
    decoder_projection,
    border_blocks,
    kernel_map,
    conv_weight,
):
    count = lax.axis_size("seq")
    block = latents.shape[2]
    packed = pl.pallas_call(
        pack_kernel,
        out_shape=pltpu.VMEM((PACK_ROWS, block), F32),
        in_specs=[HBM] * 4,
        out_specs=VMEM,
        scratch_shapes=[
            pltpu.VMEM((3, 1, block), I32),
            pltpu.VMEM((1, block), I32),
            pltpu.VMEM(border_blocks.shape[2:], I32),
            pltpu.SemaphoreType.DMA((4,)),
        ],
        compiler_params=pltpu.CompilerParams(vmem_limit_bytes=VMEM_GRANT),
        name="pack",
    )(
        *in_hbm(
            latents[0],
            jnp.swapaxes(voxel_coords, 0, 1),
            owner_map.reshape(1, block),
            border_blocks[0, 0],
        )
    )
    if count == 4 and count * block <= WHOLE_ASSET:
        velocity, blocks = whole_asset_velocity(
            packed, modulation, in_proj, qkv_proj, norm_gain, out_proj, head_proj
        )
    else:
        blocks = lax.all_gather(packed, "seq", axis=0)
        velocity = gathered_velocity(
            latents[0],
            voxel_coords[0],
            modulation,
            in_proj,
            qkv_proj,
            norm_gain,
            out_proj,
            head_proj,
        )
    partner = swap_pair(velocity)
    picks = route_call(blocks, kernel_map.shape[3] // 2)
    offsets, _, out_channels = conv_weight.shape
    fine = kernel_map.shape[3]
    owned, decoded = decode_call(
        blocks,
        picks,
        velocity,
        partner,
        step_time,
        decoder_projection,
        kernel_map.reshape(offsets, 1, fine),
        jnp.swapaxes(conv_weight, 1, 2).reshape(offsets * out_channels, -1),
    )
    return (owned[None, None], decoded.T[None, None])


def solution(mesh):
    placed = (
        P("asset", None, "seq"),
        P("asset", None, "seq"),
        P("asset", "seq", None),
        P("asset"),
        P("asset", "pair", None, None),
        P(),
        P(),
        P(),
        P(),
        P(),
        P(),
        P("asset", "seq", None, None),
        P("asset", "seq", None, None),
        P(None, None, "pair"),
    )
    return jax.shard_map(
        per_device,
        mesh=mesh,
        in_specs=placed,
        out_specs=(P("asset", "seq", None, None), P("asset", "seq", None, "pair")),
        check_vma=False,
    )
```

```python
import functools
import math

import jax
import jax.numpy as jnp
import numpy as np
from jax import lax
from jax.experimental import pallas as pl
from jax.experimental.pallas import tpu as pltpu
from jax.sharding import PartitionSpec as P

HEADS = 8
HEAD = 64
LAT = 8
BLK = 16
RES = 64

EPSILON = 1e-06
GUIDANCE = 3.0
TOP_PRECISION = lax.Precision.HIGHEST
F32 = jnp.float32
BF16 = jnp.bfloat16
I32 = jnp.int32
F8 = jnp.float8_e4m3fn
CODE_TOP = 256.0
TINY = 1e-30

ROW_COORD = 8
ROW_OWNER = 11
ROW_BORDER = 12
PACK_ROWS = 16
WHOLE_ASSET = 512

VMEM_GRANT = 40 << 20

VMEM = pl.BlockSpec(memory_space=pltpu.VMEM)
HBM = pl.BlockSpec(memory_space=pltpu.HBM)
SMEM = pl.BlockSpec(memory_space=pltpu.SMEM)


def dot_ab(a, b):
    return jnp.dot(a, b, preferred_element_type=F32)


def dot_abt(a, b):
    return lax.dot_general(a, b, (((1,), (1,)), ((), ())), preferred_element_type=F32)


def dot_atb(a, b):
    return lax.dot_general(a, b, (((0,), (0,)), ((), ())), preferred_element_type=F32)


def in_hbm(*arrays):
    return [pltpu.with_memory_space_constraint(x, pltpu.HBM) for x in arrays]


def split_two(x):
    high = x.astype(BF16).astype(F32)
    return high, x - high


def split_three(x):
    high, rest = split_two(x)
    mid, low = split_two(rest)
    return high, mid, low


@functools.lru_cache(None)
def position_parts(model_width):
    freqs = model_width // 6
    steps = np.arange(freqs, dtype=np.float32) / np.float32(freqs)
    omegas = np.exp(np.float32(-math.log(10000.0)) * steps).astype(np.float32)
    angles = (np.arange(RES, dtype=np.float32)[:, None] * omegas[None, :]).astype(np.float64)
    halves = np.concatenate([np.sin(angles), np.cos(angles)], axis=1).astype(np.float32)
    table = np.zeros((3 * RES, model_width), np.float32)
    for c in range(3):
        table[c * RES : (c + 1) * RES, c * 2 * freqs : (c + 1) * 2 * freqs] = halves
    high = table.astype(jnp.bfloat16)
    low = (table - high.astype(np.float32)).astype(jnp.bfloat16)
    return np.concatenate([high, low], axis=0)


def pack_kernel(
    lat_hbm, coord_hbm, owner_hbm, border_hbm, pack_ref, coord_ref, owner_ref, border_ref, sems
):
    pack_ref[...] = jnp.zeros_like(pack_ref)
    copies = [
        pltpu.make_async_copy(source, target, sems.at[i])
        for i, (source, target) in enumerate(
            (
                (lat_hbm, pack_ref.at[0:LAT]),
                (coord_hbm, coord_ref),
                (owner_hbm, owner_ref),
                (border_hbm, border_ref),
            )
        )
    ]
    for copy in copies:
        copy.start()
    for copy in copies:
        copy.wait()
    for c in range(3):
        pack_ref[ROW_COORD + c : ROW_COORD + c + 1] = coord_ref[c].astype(F32)
    pack_ref[ROW_OWNER : ROW_OWNER + 1] = owner_ref[...].astype(F32)
    pack_ref[ROW_BORDER : ROW_BORDER + 2, 0 : border_ref.shape[1]] = border_ref[...].astype(F32)


def hidden_rows(rows, table_ref):
    block = rows.shape[1]
    values = lax.broadcasted_iota(I32, (RES, block), 0).astype(F32)
    hots = [
        (values == rows[ROW_COORD + c : ROW_COORD + c + 1]).astype(F32).astype(BF16)
        for c in range(3)
    ]
    high, low = split_two(rows[0:LAT])
    tail = jnp.concatenate([high, low, high, jnp.zeros_like(low)], axis=0).astype(BF16)
    return dot_atb(jnp.concatenate(hots + hots + [tail], axis=0), table_ref[...])


def modulated(hidden, mod_ref):
    center = hidden - jnp.mean(hidden, axis=1, keepdims=True)
    inverse = lax.rsqrt(jnp.mean(center * center, axis=1, keepdims=True) + EPSILON)
    return (center * inverse * (1.0 + mod_ref[1]) + mod_ref[0]).astype(BF16)


def project(normed, qkv_ref, gain_ref, query_ref, key_ref, value_ref, rows):
    inner = gain_ref.shape[1]
    group = 256
    same_head = (
        lax.broadcasted_iota(I32, (group, group), 0) // HEAD
        == lax.broadcasted_iota(I32, (group, group), 1) // HEAD
    )
    averager = jnp.where(same_head, 1.0 / HEAD, 0.0).astype(BF16)

    def finish(j, projected):
        which, col = divmod(j * group, inner)
        if which == 2:
            for half in range(group // 128):
                lanes = slice(half * 128, (half + 1) * 128)
                value_ref[col // 128 + half, rows] = projected[:, lanes].astype(BF16)
        else:
            square = dot_ab((projected * projected).astype(BF16), averager)
            gains = gain_ref[which : which + 1, col : col + group]
            if which == 0:
                gains = gains * (HEAD**-0.5)
            result = (projected * lax.rsqrt(square + EPSILON) * gains).astype(BF16)
            (query_ref, key_ref)[which][rows, col : col + group] = result

    previous = None
    for j in range(3 * inner // group):
        projected = dot_ab(normed, qkv_ref[:, j * group : (j + 1) * group])
        if previous is not None:
            finish(*previous)
        previous = (j, projected)
    finish(*previous)


def at_front():
    return lax.axis_index("seq") == 0


def weight_copies(sources, targets, sems):
    mod_hbm, in_hbm_ref, qkv_hbm, gain_hbm, out_hbm, head_hbm, pos_hbm = sources
    mod_ref, in_ref, qkv_ref, gain_ref, out_ref, head_ref, table_ref = targets
    pairs = (
        (pos_hbm, table_ref.at[0 : pos_hbm.shape[0]]),
        (in_hbm_ref, in_ref),
        (mod_hbm, mod_ref),
        (gain_hbm, gain_ref),
        (qkv_hbm, qkv_ref),
        (head_hbm, head_ref),
        (out_hbm, out_ref),
    )
    return [
        pltpu.make_async_copy(source, target, sems.at[i])
        for i, (source, target) in enumerate(pairs)
    ]


def finish_table(in_ref, table_ref):
    in_high, in_low = split_two(in_ref[...])
    rows = table_ref.shape[0] - 32
    table_ref[rows : rows + 32, :] = jnp.concatenate(
        [in_high, in_high, in_low, jnp.zeros_like(in_low)], axis=0
    ).astype(BF16)


def copy_targets(in_ref, outs):
    mod_ref, qkv_ref, gain_ref, out_ref, head_ref, table_ref = outs[:6]
    return mod_ref, in_ref, qkv_ref, gain_ref, out_ref, head_ref, table_ref


def early_kernel(*refs):
    inputs, sources, pack_ref, outs = refs[:4], refs[4:11], refs[11], refs[12:18]
    coord_ref, owner_ref, border_ref, in_ref, pack_sems, sems = refs[18:]
    copies = weight_copies(sources, copy_targets(in_ref, outs), sems)

    @pl.when(at_front())
    def _():
        for copy in copies:
            copy.start()

    pack_kernel(*inputs, pack_ref, coord_ref, owner_ref, border_ref, pack_sems)

    @pl.when(at_front())
    def _():
        for copy in copies:
            copy.wait()
        finish_table(in_ref, outs[5])


def first_kernel(*refs):
    own_ref, mixed_ref, sources, outs, state = refs[0], refs[1], refs[2:9], refs[15:21], refs[21:25]
    in_ref, normed_ref, sems = refs[25:]
    mod_ref, qkv_ref, gain_ref, _, _, table_ref = outs
    hidden_ref, query_ref, key_ref, value_ref = state
    copies = weight_copies(sources, copy_targets(in_ref, outs), sems)
    missing = jnp.logical_not(at_front())

    @pl.when(missing)
    def _():
        for copy in copies:
            copy.start()
        for copy in copies[:4]:
            copy.wait()
        finish_table(in_ref, table_ref)

    block = own_ref.shape[1]
    hiddens = [hidden_rows(source[...], table_ref) for source in (own_ref, mixed_ref)]
    for s, hidden in enumerate(hiddens):
        hidden_ref[s * block : (s + 1) * block, :] = hidden
        normed_ref[s * block : (s + 1) * block, :] = modulated(hidden, mod_ref)

    @pl.when(missing)
    def _():
        for copy in copies[4:]:
            copy.wait()

    rows = slice(0, len(hiddens) * block)
    project(normed_ref[...], qkv_ref, gain_ref, query_ref, key_ref, value_ref, rows)


def velocity_kernel(
    own_ref,
    mixed_ref,
    swapped_ref,
    far_ref,
    mod_ref,
    qkv_ref,
    gain_ref,
    out_ref,
    head_ref,
    table_ref,
    done_hidden_ref,
    done_query_ref,
    done_key_ref,
    done_value_ref,
    vel_ref,
    blocks_ref,
    hidden_ref,
    normed_ref,
    query_ref,
    key_ref,
    value_ref,
    att_ref,
):
    me = lax.axis_index("seq")
    side = lax.axis_index("pair")
    width = qkv_ref.shape[0]
    tokens = hidden_ref.shape[0]
    inner = out_ref.shape[0]
    block = own_ref.shape[1]
    places = (me, me ^ (1 + side), me ^ (2 - side), me ^ 3)
    sources = (own_ref, mixed_ref, swapped_ref, far_ref)
    for place, source in zip(places, sources):
        blocks_ref[place] = source[...]

    done = done_hidden_ref.shape[0] // block
    here = slice(0, done * block)
    ready = hidden_rows(sources[done][...], table_ref)
    hidden_ref[here, :] = done_hidden_ref[...]
    query_ref[here, :] = done_query_ref[...]
    key_ref[here, :] = done_key_ref[...]
    for pair in range(inner // 128):
        value_ref[pair, here] = done_value_ref[pair]
    for s in range(done, len(sources)):
        hidden = ready
        if s + 1 < len(sources):
            ready = hidden_rows(sources[s + 1][...], table_ref)
        hidden_ref[s * block : (s + 1) * block, :] = hidden
        normed_ref[s * block : (s + 1) * block, :] = modulated(hidden, mod_ref)
    others = slice(done * block, tokens)
    project(normed_ref[others, :], qkv_ref, gain_ref, query_ref, key_ref, value_ref, others)

    chunk = min(tokens, 512)
    even = lax.broadcasted_iota(I32, (tokens, 128), 1) < HEAD
    ones_rows = jnp.ones((16, tokens), BF16)
    flipped = [value_ref[pair].T for pair in range(inner // 128)]
    todo = [
        (pair, half, q)
        for pair in range(inner // 128)
        for half in range(2)
        for q in range(tokens // chunk)
    ]

    def score(pair, half, q):
        lanes = slice(pair * 128, (pair + 1) * 128)
        keys = key_ref[:, lanes]
        kept = jnp.where(even == (half == 0), keys, jnp.zeros_like(keys))
        return dot_abt(kept, query_ref[q * chunk : (q + 1) * chunk, lanes])

    ready = [score(*item) for item in todo[:2]]
    for at, (pair, half, q) in enumerate(todo):
        scores = ready.pop(0)
        if at + 2 < len(todo):
            ready.append(score(*todo[at + 2]))
        values = flipped[pair][half * HEAD : (half + 1) * HEAD]
        values = jnp.concatenate([values, ones_rows], axis=0)
        sums = dot_ab(values, jnp.exp(scores).astype(BF16))
        dims = slice(pair * 128 + half * HEAD, pair * 128 + (half + 1) * HEAD)
        mean = sums[0:HEAD] / sums[HEAD : HEAD + 1]
        att_ref[dims, q * chunk : (q + 1) * chunk] = mean.astype(BF16)

    gate = mod_ref[2]
    head = head_ref[...]
    offset = jnp.sum(head * mod_ref[3], axis=1, keepdims=True)
    head_high, head_low = split_two(head * (1.0 + mod_ref[4]))
    heads = jnp.concatenate([head_high, head_low], axis=0).astype(BF16)
    ones = jnp.ones((16, width), BF16)
    step = 128
    def attended(q):
        return dot_atb(att_ref[:, q * step : (q + 1) * step], out_ref[...])
    def middle(q, product):
        hidden = hidden_ref[q * step : (q + 1) * step, :] + gate * product
        center = hidden - jnp.mean(hidden, axis=1, keepdims=True)
        high = center.astype(BF16)
        low = (center - high.astype(F32)).astype(BF16)
        return high, low
    def last(q, high, low):
        both = dot_abt(heads, high)
        rest = dot_abt(heads, low)
        square = dot_abt(ones, high * high)
        inverse = lax.rsqrt(square[0:LAT] * (1.0 / width) + EPSILON)
        velocity = (both[0:LAT] + both[LAT:] + rest[0:LAT]) * inverse + offset
        for i in range(step // block):
            vel_ref[places[q * (step // block) + i]] = velocity[:, i * block : (i + 1) * block]
    count = tokens // step
    product = attended(0)
    waiting = None
    for q in range(count):
        following = attended(q + 1) if q + 1 < count else None
        centered = middle(q, product)
        if waiting is not None:
            last(*waiting)
        waiting = (q, *centered)
        product = following
    last(*waiting)


def route_kernel(blocks_ref, picks_ref):
    me = lax.axis_index("seq")
    count, _, block = blocks_ref.shape
    table_rows = picks_ref.shape[0]
    slots = table_rows // 2
    capacity = slots // count
    halo = (table_rows - slots) // 2

    owners = jnp.concatenate(
        [blocks_ref[s, ROW_OWNER : ROW_OWNER + 1, :] for s in range(count)], axis=0
    ).astype(I32)
    earlier = (
        lax.broadcasted_iota(I32, (block, block), 0) < lax.broadcasted_iota(I32, (block, block), 1)
    ).astype(F32).astype(BF16)
    starts = lax.broadcasted_iota(I32, (count, block), 0) * capacity
    targets = []
    for step in (0, -1, 1):
        named = owners == me + step
        ranks = dot_ab(named.astype(F32).astype(BF16), earlier).astype(I32)
        slot_of = jnp.where(named, ranks + starts, -1)
        targets.append(jnp.concatenate([slot_of[s : s + 1] for s in range(count)], axis=1))
    tokens = count * block
    rows = lax.broadcasted_iota(I32, (slots, tokens), 0)
    picks_ref[0:slots] = (rows == targets[0]).astype(F32).astype(BF16)
    small = lax.broadcasted_iota(I32, (BLK, tokens), 0)
    for step, direction in ((-1, 1), (1, 0)):
        source = jnp.clip(me + step, 0, count - 1)
        border = blocks_ref[source, ROW_BORDER : ROW_BORDER + 2, :].astype(I32)
        target = targets[1 if step < 0 else 2]
        start = slots + (0 if step < 0 else halo)
        for i in range(halo // BLK):
            wanted = border[direction : direction + 1, i : i + 1] * BLK
            here = slice(start + i * BLK, start + (i + 1) * BLK)
            picks_ref[here] = (small + wanted == target).astype(F32).astype(BF16)


def decode_kernel(
    blocks_ref,
    picks_ref,
    mine_ref,
    other_ref,
    time_ref,
    proj_ref,
    map_ref,
    weight_ref,
    owned_ref,
    fine_ref,
    code_ref,
):
    is_cond = lax.axis_index("pair") == 0
    slots = owned_ref.shape[1]
    offsets = map_ref.shape[0]
    out_channels = fine_ref.shape[0]
    table_rows = code_ref.shape[2]

    cleans = []
    for s in range(blocks_ref.shape[0]):
        mine, other = mine_ref[s], other_ref[s]
        cond = jnp.where(is_cond, mine, other)
        uncond = jnp.where(is_cond, other, mine)
        guided = uncond + GUIDANCE * (cond - uncond)
        cleans.append(blocks_ref[s, 0:LAT, :] - time_ref[0] * guided)
    clean = jnp.concatenate(cleans, axis=1)

    parts = jnp.concatenate(split_three(clean), axis=0).astype(BF16)
    spread = dot_abt(parts, picks_ref[...])
    table = spread[0:LAT] + spread[LAT : 2 * LAT] + spread[2 * LAT :]
    owned_ref[...] = table[:, 0:slots]

    proj_high, proj_low = split_two(proj_ref[...])
    table_high, table_low = split_two(table)
    left = jnp.concatenate([proj_high, proj_high, proj_low, jnp.zeros_like(proj_low)], axis=0)
    right = jnp.concatenate([table_high, table_low, table_high, jnp.zeros_like(table_low)], axis=0)
    before = dot_atb(left.astype(BF16), right.astype(BF16))
    features = (0.5 * before * (1.0 + jnp.tanh(0.5 * before))).astype(BF16)

    count = 3
    groups = [range(k, min(k + count, offsets)) for k in range(0, offsets, count)]

    def multiply(group):
        rows = weight_ref[group[0] * out_channels : (group[-1] + 1) * out_channels]
        return dot_ab(rows, features)

    def code(group, product):
        top = jnp.max(jnp.abs(product), axis=0, keepdims=True)
        top = jnp.maximum(jnp.max(top, axis=1, keepdims=True), TINY)
        scaled = product * (CODE_TOP / top)
        high = scaled.astype(F8)
        low = (scaled - high.astype(F32)).astype(F8)
        for i, k in enumerate(group):
            rows = slice(i * out_channels, (i + 1) * out_channels)
            code_ref[k, 0:out_channels] = high[rows]
            code_ref[k, out_channels : 2 * out_channels] = low[rows]
        return top * (1.0 / CODE_TOP)

    units = []
    ready = multiply(groups[0])
    for i, group in enumerate(groups):
        product = ready
        if i + 1 < len(groups):
            ready = multiply(groups[i + 1])
        units.append(code(group, product))

    fine = map_ref.shape[2]
    width = 256
    table_ids = lax.broadcasted_iota(jnp.int16, (table_rows, width), 0)
    one = jnp.ones((table_rows, width), F8)
    zero = jnp.zeros((table_rows, width), F8)
    for f in range(fine // width):
        here = slice(f * width, (f + 1) * width)
        total = jnp.zeros((out_channels, width), F32)
        for group, unit in zip(groups, units):
            part = jnp.zeros((2 * out_channels, width), F32)
            for k in group:
                index = jnp.broadcast_to(map_ref[k, :, here], (16, width)).astype(jnp.int16)
                index = jnp.broadcast_to(index[None], (table_rows // 16, 16, width))
                chosen = jnp.where(table_ids == index.reshape(table_rows, width), one, zero)
                part = part + dot_ab(code_ref[k], chosen)
            total = total + (part[0:out_channels] + part[out_channels:]) * unit
        fine_ref[:, here] = total.astype(BF16)


def route_call(blocks, table_rows):
    count, _, block = blocks.shape
    return pl.pallas_call(
        route_kernel,
        out_shape=pltpu.VMEM((table_rows, count * block), BF16),
        in_specs=[VMEM],
        out_specs=VMEM,
        compiler_params=pltpu.CompilerParams(vmem_limit_bytes=VMEM_GRANT),
        cost_estimate=pl.CostEstimate(flops=0, bytes_accessed=1 << 20, transcendentals=0),
        name="route",
    )(blocks)


def decode_call(
    blocks, picks, velocity, partner, step_time, decoder_projection, index_rows, weights
):
    offsets, _, fine = index_rows.shape
    out_channels = weights.shape[0] // offsets
    slots = fine // 4
    table_rows = picks.shape[0]
    return pl.pallas_call(
        decode_kernel,
        out_shape=(
            jax.ShapeDtypeStruct((LAT, slots), F32),
            jax.ShapeDtypeStruct((out_channels, fine), BF16),
        ),
        in_specs=[VMEM, VMEM, VMEM, VMEM, SMEM, VMEM, VMEM, VMEM],
        out_specs=(VMEM, VMEM),
        scratch_shapes=[pltpu.VMEM((offsets, 2 * out_channels, table_rows), F8)],
        compiler_params=pltpu.CompilerParams(vmem_limit_bytes=VMEM_GRANT),
        name="decode",
    )(blocks, picks, velocity, partner, step_time, decoder_projection, index_rows, weights)


def swap_pair(x):
    return lax.ppermute(x, "pair", [(0, 1), (1, 0)])


def seq_swap(x, distance_of):
    count = lax.axis_size("seq")
    routes = [
        (p * count + (z ^ distance_of[p]), p * count + z) for p in range(2) for z in range(count)
    ]
    return lax.ppermute(x, ("pair", "seq"), routes)


def pack_operands(latents, voxel_coords, owner_map, border_blocks):
    return in_hbm(
        latents[0],
        jnp.swapaxes(voxel_coords, 0, 1),
        owner_map.reshape(1, -1),
        border_blocks[0, 0],
    )


def pack_scratch(block, border_blocks):
    return [
        pltpu.VMEM((3, 1, block), I32),
        pltpu.VMEM((1, block), I32),
        pltpu.VMEM(border_blocks.shape[2:], I32),
    ]


def whole_asset_velocity(
    placed, modulation, in_proj, qkv_proj, norm_gain, out_proj, head_proj
):
    latents, _, _, border_blocks = placed
    count = lax.axis_size("seq")
    block = latents.shape[2]
    tokens = count * block
    width = in_proj.shape[1]
    inner = out_proj.shape[0]
    pos = jnp.asarray(position_parts(width))
    block_shapes = (
        pltpu.VMEM((2 * block, width), F32),
        pltpu.VMEM((2 * block, inner), BF16),
        pltpu.VMEM((2 * block, inner), BF16),
        pltpu.VMEM((inner // 128, 2 * block, 128), BF16),
    )
    held_shapes = (
        pltpu.VMEM((5, 1, width), F32),
        pltpu.VMEM(qkv_proj.shape, BF16),
        pltpu.VMEM(norm_gain.shape, F32),
        pltpu.VMEM(out_proj.shape, BF16),
        pltpu.VMEM((LAT, width), F32),
        pltpu.VMEM((pos.shape[0] + 32, width), BF16),
    )
    block_cost = pl.CostEstimate(
        flops=4 * block * width * 4 * inner, bytes_accessed=6 << 20, transcendentals=0
    )
    params = pltpu.CompilerParams(vmem_limit_bytes=VMEM_GRANT)
    sources = in_hbm(
        modulation[0, 0][:, None, :],
        in_proj,
        qkv_proj,
        norm_gain,
        out_proj,
        head_proj.T,
        pos,
    )
    weight_scratch = [pltpu.VMEM(in_proj.shape, F32)]
    weight_sems = pltpu.SemaphoreType.DMA((len(sources),))
    packed, *held = pl.pallas_call(
        early_kernel,
        out_shape=(pltpu.VMEM((PACK_ROWS, block), F32), *held_shapes),
        in_specs=[HBM] * 11,
        out_specs=(VMEM,) * 7,
        scratch_shapes=[
            *pack_scratch(block, border_blocks),
            *weight_scratch,
            pltpu.SemaphoreType.DMA((4,)),
            weight_sems,
        ],
        compiler_params=params,
        name="pack",
    )(*pack_operands(*placed), *sources)
    mixed = seq_swap(packed, (1, 2))
    far = seq_swap(packed, (3, 3))
    swapped = swap_pair(mixed)
    held = pl.pallas_call(
        first_kernel,
        out_shape=(*held_shapes, *block_shapes),
        in_specs=[VMEM] * 2 + [HBM] * 7 + [VMEM] * 6,
        out_specs=(VMEM,) * 10,
        scratch_shapes=[*weight_scratch, pltpu.VMEM((2 * block, width), BF16), weight_sems],
        input_output_aliases={9 + i: i for i in range(6)},
        compiler_params=params,
        cost_estimate=block_cost,
        name="first_blocks",
    )(packed, mixed, *sources, *held)
    return pl.pallas_call(
        velocity_kernel,
        out_shape=(
            pltpu.VMEM((count, LAT, block), F32),
            pltpu.VMEM((count, PACK_ROWS, block), F32),
        ),
        in_specs=[VMEM] * 14,
        out_specs=(VMEM, VMEM),
        scratch_shapes=[
            pltpu.VMEM((tokens, width), F32),
            pltpu.VMEM((tokens, width), BF16),
            pltpu.VMEM((tokens, inner), BF16),
            pltpu.VMEM((tokens, inner), BF16),
            pltpu.VMEM((inner // 128, tokens, 128), BF16),
            pltpu.VMEM((inner, tokens), BF16),
        ],
        compiler_params=pltpu.CompilerParams(vmem_limit_bytes=VMEM_GRANT),
        name="velocity",
    )(packed, mixed, swapped, far, *held)


def pack_call(latents, voxel_coords, owner_map, border_blocks):
    block = latents.shape[2]
    return pl.pallas_call(
        pack_kernel,
        out_shape=pltpu.VMEM((PACK_ROWS, block), F32),
        in_specs=[HBM] * 4,
        out_specs=VMEM,
        scratch_shapes=[*pack_scratch(block, border_blocks), pltpu.SemaphoreType.DMA((4,))],
        compiler_params=pltpu.CompilerParams(vmem_limit_bytes=VMEM_GRANT),
        name="pack",
    )(*pack_operands(latents, voxel_coords, owner_map, border_blocks))


def layer_norm(values):
    center = values - jnp.mean(values, axis=-1, keepdims=True)
    variance = jnp.mean(center * center, axis=-1, keepdims=True)
    return center / jnp.sqrt(variance + EPSILON)


def position_table(coord_rows, model_width):
    freqs = model_width // 6
    steps = jnp.arange(freqs, dtype=F32) / freqs
    omegas = jnp.exp(-math.log(10000.0) * steps)
    angles = coord_rows.astype(F32)[:, :, None] * omegas[None, None, :]
    halves = jnp.concatenate([jnp.sin(angles), jnp.cos(angles)], axis=2)
    rows_out = jnp.transpose(halves, (1, 0, 2)).reshape(coord_rows.shape[1], 6 * freqs)
    return jnp.pad(rows_out, ((0, 0), (0, model_width - 6 * freqs)))


def head_norm(values, gains):
    row_count = values.shape[0]
    per_head = values.reshape(row_count, HEADS, HEAD)
    mean_square = jnp.mean(per_head * per_head, axis=2, keepdims=True)
    return (per_head / jnp.sqrt(mean_square + EPSILON)).reshape(row_count, HEADS * HEAD) * gains


def gathered_velocity(
    latent_block, coords, modulation, in_proj, qkv_proj, norm_gain, out_proj, head_proj
):
    token_count = latent_block.shape[1]
    model_width = in_proj.shape[1]
    inner_width = out_proj.shape[0]
    factor = HEAD ** (-0.5)
    mod_rows = modulation[0, 0]
    hidden = jnp.dot(latent_block.T, in_proj, precision=TOP_PRECISION) + position_table(
        coords, model_width
    )
    normed = (layer_norm(hidden) * (1.0 + mod_rows[1]) + mod_rows[0]).astype(BF16)
    projected = jnp.dot(normed, qkv_proj, preferred_element_type=F32)
    queries = head_norm(projected[:, :inner_width], norm_gain[0]).astype(BF16)
    keys_in = head_norm(projected[:, inner_width : 2 * inner_width], norm_gain[1]).astype(BF16)
    values_in = projected[:, 2 * inner_width :].astype(BF16)
    query_heads = queries.reshape(token_count, HEADS, HEAD)
    start_pair = (
        jnp.zeros((token_count, HEADS, HEAD), F32),
        jnp.zeros((token_count, HEADS), F32),
    )
    key_rows = lax.all_gather(keys_in, "seq", axis=0, tiled=True)
    value_rows = lax.all_gather(values_in, "seq", axis=0, tiled=True)
    row_count = key_rows.shape[0]
    block_rows = math.gcd(row_count, 512)
    key_blocks = key_rows.reshape(row_count // block_rows, block_rows, HEADS, HEAD)
    value_blocks = value_rows.reshape(row_count // block_rows, block_rows, HEADS, HEAD)

    def one_block(running, block_pair):
        numer_run, denom_run = running
        key_block, value_block = block_pair
        scores = (
            jnp.einsum("qhd,khd->hqk", query_heads, key_block, preferred_element_type=F32) * factor
        )
        exp_scores = jnp.exp(scores)
        numer_run = numer_run + jnp.einsum(
            "hqk,khd->qhd", exp_scores.astype(BF16), value_block, preferred_element_type=F32
        )
        denom_run = denom_run + jnp.sum(exp_scores, axis=2).T
        return ((numer_run, denom_run), None)

    (numerator, denominator), _ = lax.scan(one_block, start_pair, (key_blocks, value_blocks))
    attended = (
        (numerator / denominator[:, :, None]).reshape(token_count, inner_width).astype(BF16)
    )
    hidden = hidden + mod_rows[2] * jnp.dot(attended, out_proj, preferred_element_type=F32)
    final = layer_norm(hidden) * (1.0 + mod_rows[4]) + mod_rows[3]
    velocity = jnp.dot(final, head_proj, precision=TOP_PRECISION).T
    return lax.all_gather(velocity, "seq", axis=0)


def per_device(
    latents,
    voxel_coords,
    owner_map,
    step_time,
    modulation,
    in_proj,
    qkv_proj,
    norm_gain,
    out_proj,
    head_proj,
    decoder_projection,
    border_blocks,
    kernel_map,
    conv_weight,
):
    count = lax.axis_size("seq")
    block = latents.shape[2]
    placed = (latents, voxel_coords, owner_map, border_blocks)
    if count == 4 and count * block <= WHOLE_ASSET:
        velocity, blocks = whole_asset_velocity(
            placed, modulation, in_proj, qkv_proj, norm_gain, out_proj, head_proj
        )
    else:
        blocks = lax.all_gather(pack_call(*placed), "seq", axis=0)
        velocity = gathered_velocity(
            latents[0],
            voxel_coords[0],
            modulation,
            in_proj,
            qkv_proj,
            norm_gain,
            out_proj,
            head_proj,
        )
    partner = swap_pair(velocity)
    picks = route_call(blocks, kernel_map.shape[3] // 2)
    offsets, _, out_channels = conv_weight.shape
    fine = kernel_map.shape[3]
    owned, decoded = decode_call(
        blocks,
        picks,
        velocity,
        partner,
        step_time,
        decoder_projection,
        kernel_map.reshape(offsets, 1, fine),
        jnp.swapaxes(conv_weight, 1, 2).reshape(offsets * out_channels, -1),
    )
    return (owned[None, None], decoded.T[None, None])


def solution(mesh):
    placed = (
        P("asset", None, "seq"),
        P("asset", None, "seq"),
        P("asset", "seq", None),
        P("asset"),
        P("asset", "pair", None, None),
        P(),
        P(),
        P(),
        P(),
        P(),
        P(),
        P("asset", "seq", None, None),
        P("asset", "seq", None, None),
        P(None, None, "pair"),
    )
    return jax.shard_map(
        per_device,
        mesh=mesh,
        in_specs=placed,
        out_specs=(P("asset", "seq", None, None), P("asset", "seq", None, "pair")),
        check_vma=False,
    )
```

```python
import functools
import math

import jax
import jax.numpy as jnp
import numpy as np
from jax import lax
from jax.experimental import pallas as pl
from jax.experimental.pallas import tpu as pltpu
from jax.sharding import PartitionSpec as P

HEADS = 8
HEAD = 64
LAT = 8
BLK = 16
RES = 64

EPSILON = 1e-06
GUIDANCE = 3.0
TOP_PRECISION = lax.Precision.HIGHEST
F32 = jnp.float32
BF16 = jnp.bfloat16
I32 = jnp.int32
F8 = jnp.float8_e4m3fn
CODE_TOP = 256.0
TINY = 1e-30

ROW_COORD = 8
ROW_OWNER = 11
ROW_BORDER = 12
PACK_ROWS = 16
WHOLE_ASSET = 512

VMEM_GRANT = 40 << 20

VMEM = pl.BlockSpec(memory_space=pltpu.VMEM)
HBM = pl.BlockSpec(memory_space=pltpu.HBM)
SMEM = pl.BlockSpec(memory_space=pltpu.SMEM)


def dot_ab(a, b):
    return jnp.dot(a, b, preferred_element_type=F32)


def dot_abt(a, b):
    return lax.dot_general(a, b, (((1,), (1,)), ((), ())), preferred_element_type=F32)


def dot_atb(a, b):
    return lax.dot_general(a, b, (((0,), (0,)), ((), ())), preferred_element_type=F32)


def in_hbm(*arrays):
    return [pltpu.with_memory_space_constraint(x, pltpu.HBM) for x in arrays]


def split_two(x):
    high = x.astype(BF16).astype(F32)
    return high, x - high


def split_three(x):
    high, rest = split_two(x)
    mid, low = split_two(rest)
    return high, mid, low


@functools.lru_cache(None)
def position_parts(model_width):
    freqs = model_width // 6
    steps = np.arange(freqs, dtype=np.float32) / np.float32(freqs)
    omegas = np.exp(np.float32(-math.log(10000.0)) * steps).astype(np.float32)
    angles = (np.arange(RES, dtype=np.float32)[:, None] * omegas[None, :]).astype(np.float64)
    halves = np.concatenate([np.sin(angles), np.cos(angles)], axis=1).astype(np.float32)
    table = np.zeros((3 * RES, model_width), np.float32)
    for c in range(3):
        table[c * RES : (c + 1) * RES, c * 2 * freqs : (c + 1) * 2 * freqs] = halves
    high = table.astype(jnp.bfloat16)
    low = (table - high.astype(np.float32)).astype(jnp.bfloat16)
    return np.concatenate([high, low], axis=0)


def pack_kernel(
    lat_hbm, coord_hbm, owner_hbm, border_hbm, pack_ref, coord_ref, owner_ref, border_ref, sems
):
    pack_ref[...] = jnp.zeros_like(pack_ref)
    copies = [
        pltpu.make_async_copy(source, target, sems.at[i])
        for i, (source, target) in enumerate(
            (
                (lat_hbm, pack_ref.at[0:LAT]),
                (coord_hbm, coord_ref),
                (owner_hbm, owner_ref),
                (border_hbm, border_ref),
            )
        )
    ]
    for copy in copies:
        copy.start()
    for copy in copies:
        copy.wait()
    for c in range(3):
        pack_ref[ROW_COORD + c : ROW_COORD + c + 1] = coord_ref[c].astype(F32)
    pack_ref[ROW_OWNER : ROW_OWNER + 1] = owner_ref[...].astype(F32)
    pack_ref[ROW_BORDER : ROW_BORDER + 2, 0 : border_ref.shape[1]] = border_ref[...].astype(F32)


def hidden_rows(rows, table_ref):
    block = rows.shape[1]
    values = lax.broadcasted_iota(I32, (RES, block), 0).astype(F32)
    hots = [
        (values == rows[ROW_COORD + c : ROW_COORD + c + 1]).astype(F32).astype(BF16)
        for c in range(3)
    ]
    high, low = split_two(rows[0:LAT])
    tail = jnp.concatenate([high, low, high, jnp.zeros_like(low)], axis=0).astype(BF16)
    return dot_atb(jnp.concatenate(hots + hots + [tail], axis=0), table_ref[...])


def modulated(hidden, mod_ref):
    center = hidden - jnp.mean(hidden, axis=1, keepdims=True)
    inverse = lax.rsqrt(jnp.mean(center * center, axis=1, keepdims=True) + EPSILON)
    return (center * inverse * (1.0 + mod_ref[1]) + mod_ref[0]).astype(BF16)


def project(normed, qkv_ref, gain_ref, query_ref, key_ref, value_ref, rows):
    inner = gain_ref.shape[1]
    group = 256
    same_head = (
        lax.broadcasted_iota(I32, (group, group), 0) // HEAD
        == lax.broadcasted_iota(I32, (group, group), 1) // HEAD
    )
    averager = jnp.where(same_head, 1.0 / HEAD, 0.0).astype(BF16)

    def finish(j, projected):
        which, col = divmod(j * group, inner)
        if which == 2:
            for half in range(group // 128):
                lanes = slice(half * 128, (half + 1) * 128)
                value_ref[col // 128 + half, rows] = projected[:, lanes].astype(BF16)
        else:
            square = dot_ab((projected * projected).astype(BF16), averager)
            gains = gain_ref[which : which + 1, col : col + group]
            if which == 0:
                gains = gains * (HEAD**-0.5)
            result = (projected * lax.rsqrt(square + EPSILON) * gains).astype(BF16)
            (query_ref, key_ref)[which][rows, col : col + group] = result

    previous = None
    for j in range(3 * inner // group):
        projected = dot_ab(normed, qkv_ref[:, j * group : (j + 1) * group])
        if previous is not None:
            finish(*previous)
        previous = (j, projected)
    finish(*previous)


def at_front():
    return lax.axis_index("seq") == 0


def weight_copies(sources, targets, sems):
    mod_hbm, in_hbm_ref, qkv_hbm, gain_hbm, out_hbm, head_hbm, pos_hbm = sources
    mod_ref, in_ref, qkv_ref, gain_ref, out_ref, head_ref, table_ref = targets
    pairs = (
        (pos_hbm, table_ref.at[0 : pos_hbm.shape[0]]),
        (in_hbm_ref, in_ref),
        (mod_hbm, mod_ref),
        (gain_hbm, gain_ref),
        (qkv_hbm, qkv_ref),
        (head_hbm, head_ref),
        (out_hbm, out_ref),
    )
    return [
        pltpu.make_async_copy(source, target, sems.at[i])
        for i, (source, target) in enumerate(pairs)
    ]


def finish_table(in_ref, table_ref):
    in_high, in_low = split_two(in_ref[...])
    rows = table_ref.shape[0] - 32
    table_ref[rows : rows + 32, :] = jnp.concatenate(
        [in_high, in_high, in_low, jnp.zeros_like(in_low)], axis=0
    ).astype(BF16)


def copy_targets(in_ref, outs):
    mod_ref, qkv_ref, gain_ref, out_ref, head_ref, table_ref = outs[:6]
    return mod_ref, in_ref, qkv_ref, gain_ref, out_ref, head_ref, table_ref


def early_kernel(*refs):
    inputs, sources, pack_ref, outs = refs[:4], refs[4:11], refs[11], refs[12:18]
    coord_ref, owner_ref, border_ref, in_ref, pack_sems, sems = refs[18:]
    copies = weight_copies(sources, copy_targets(in_ref, outs), sems)

    @pl.when(at_front())
    def _():
        for copy in copies[:5]:
            copy.start()

    pack_kernel(*inputs, pack_ref, coord_ref, owner_ref, border_ref, pack_sems)

    @pl.when(at_front())
    def _():
        for copy in copies[:5]:
            copy.wait()
        finish_table(in_ref, outs[5])


def first_kernel(*refs):
    own_ref, mixed_ref, sources, outs, state = refs[0], refs[1], refs[2:9], refs[15:21], refs[21:25]
    in_ref, normed_ref, sems = refs[25:]
    mod_ref, qkv_ref, gain_ref, _, _, table_ref = outs
    hidden_ref, query_ref, key_ref, value_ref = state
    copies = weight_copies(sources, copy_targets(in_ref, outs), sems)
    missing = jnp.logical_not(at_front())

    @pl.when(missing)
    def _():
        for copy in copies[:5]:
            copy.start()

    for copy in copies[5:]:
        copy.start()

    @pl.when(missing)
    def _():
        for copy in copies[:4]:
            copy.wait()
        finish_table(in_ref, table_ref)

    block = own_ref.shape[1]
    hiddens = [hidden_rows(source[...], table_ref) for source in (own_ref, mixed_ref)]
    for s, hidden in enumerate(hiddens):
        hidden_ref[s * block : (s + 1) * block, :] = hidden
        normed_ref[s * block : (s + 1) * block, :] = modulated(hidden, mod_ref)

    @pl.when(missing)
    def _():
        copies[4].wait()

    rows = slice(0, len(hiddens) * block)
    project(normed_ref[...], qkv_ref, gain_ref, query_ref, key_ref, value_ref, rows)
    for copy in copies[5:]:
        copy.wait()


def velocity_kernel(
    own_ref,
    mixed_ref,
    swapped_ref,
    far_ref,
    mod_ref,
    qkv_ref,
    gain_ref,
    out_ref,
    head_ref,
    table_ref,
    done_hidden_ref,
    done_query_ref,
    done_key_ref,
    done_value_ref,
    vel_ref,
    blocks_ref,
    hidden_ref,
    normed_ref,
    query_ref,
    key_ref,
    value_ref,
    att_ref,
):
    me = lax.axis_index("seq")
    side = lax.axis_index("pair")
    width = qkv_ref.shape[0]
    tokens = hidden_ref.shape[0]
    inner = out_ref.shape[0]
    block = own_ref.shape[1]
    places = (me, me ^ (1 + side), me ^ (2 - side), me ^ 3)
    sources = (own_ref, mixed_ref, swapped_ref, far_ref)
    for place, source in zip(places, sources):
        blocks_ref[place] = source[...]

    done = done_hidden_ref.shape[0] // block
    here = slice(0, done * block)
    ready = hidden_rows(sources[done][...], table_ref)
    hidden_ref[here, :] = done_hidden_ref[...]
    query_ref[here, :] = done_query_ref[...]
    key_ref[here, :] = done_key_ref[...]
    for pair in range(inner // 128):
        value_ref[pair, here] = done_value_ref[pair]
    for s in range(done, len(sources)):
        hidden = ready
        if s + 1 < len(sources):
            ready = hidden_rows(sources[s + 1][...], table_ref)
        hidden_ref[s * block : (s + 1) * block, :] = hidden
        normed_ref[s * block : (s + 1) * block, :] = modulated(hidden, mod_ref)
    others = slice(done * block, tokens)
    project(normed_ref[others, :], qkv_ref, gain_ref, query_ref, key_ref, value_ref, others)

    chunk = min(tokens, 512)
    even = lax.broadcasted_iota(I32, (tokens, 128), 1) < HEAD
    ones_rows = jnp.ones((16, tokens), BF16)
    flipped = [value_ref[pair].T for pair in range(inner // 128)]
    todo = [
        (pair, half, q)
        for pair in range(inner // 128)
        for half in range(2)
        for q in range(tokens // chunk)
    ]

    def score(pair, half, q):
        lanes = slice(pair * 128, (pair + 1) * 128)
        keys = key_ref[:, lanes]
        kept = jnp.where(even == (half == 0), keys, jnp.zeros_like(keys))
        return dot_abt(kept, query_ref[q * chunk : (q + 1) * chunk, lanes])

    ready = [score(*item) for item in todo[:2]]
    for at, (pair, half, q) in enumerate(todo):
        scores = ready.pop(0)
        if at + 2 < len(todo):
            ready.append(score(*todo[at + 2]))
        values = flipped[pair][half * HEAD : (half + 1) * HEAD]
        values = jnp.concatenate([values, ones_rows], axis=0)
        sums = dot_ab(values, jnp.exp(scores).astype(BF16))
        dims = slice(pair * 128 + half * HEAD, pair * 128 + (half + 1) * HEAD)
        mean = sums[0:HEAD] / sums[HEAD : HEAD + 1]
        att_ref[dims, q * chunk : (q + 1) * chunk] = mean.astype(BF16)

    gate = mod_ref[2]
    head = head_ref[...]
    offset = jnp.sum(head * mod_ref[3], axis=1, keepdims=True)
    head_high, head_low = split_two(head * (1.0 + mod_ref[4]))
    heads = jnp.concatenate([head_high, head_low], axis=0).astype(BF16)
    ones = jnp.ones((16, width), BF16)
    step = 128
    def attended(q):
        return dot_atb(att_ref[:, q * step : (q + 1) * step], out_ref[...])
    def middle(q, product):
        hidden = hidden_ref[q * step : (q + 1) * step, :] + gate * product
        center = hidden - jnp.mean(hidden, axis=1, keepdims=True)
        high = center.astype(BF16)
        low = (center - high.astype(F32)).astype(BF16)
        return high, low
    def last(q, high, low):
        both = dot_abt(heads, high)
        rest = dot_abt(heads, low)
        square = dot_abt(ones, high * high)
        inverse = lax.rsqrt(square[0:LAT] * (1.0 / width) + EPSILON)
        velocity = (both[0:LAT] + both[LAT:] + rest[0:LAT]) * inverse + offset
        for i in range(step // block):
            vel_ref[places[q * (step // block) + i]] = velocity[:, i * block : (i + 1) * block]
    count = tokens // step
    product = attended(0)
    waiting = None
    for q in range(count):
        following = attended(q + 1) if q + 1 < count else None
        centered = middle(q, product)
        if waiting is not None:
            last(*waiting)
        waiting = (q, *centered)
        product = following
    last(*waiting)


def route_kernel(blocks_ref, picks_ref):
    me = lax.axis_index("seq")
    count, _, block = blocks_ref.shape
    table_rows = picks_ref.shape[0]
    slots = table_rows // 2
    capacity = slots // count
    halo = (table_rows - slots) // 2

    owners = jnp.concatenate(
        [blocks_ref[s, ROW_OWNER : ROW_OWNER + 1, :] for s in range(count)], axis=0
    ).astype(I32)
    earlier = (
        lax.broadcasted_iota(I32, (block, block), 0) < lax.broadcasted_iota(I32, (block, block), 1)
    ).astype(F32).astype(BF16)
    starts = lax.broadcasted_iota(I32, (count, block), 0) * capacity
    targets = []
    for step in (0, -1, 1):
        named = owners == me + step
        ranks = dot_ab(named.astype(F32).astype(BF16), earlier).astype(I32)
        slot_of = jnp.where(named, ranks + starts, -1)
        targets.append(jnp.concatenate([slot_of[s : s + 1] for s in range(count)], axis=1))
    tokens = count * block
    rows = lax.broadcasted_iota(I32, (slots, tokens), 0)
    picks_ref[0:slots] = (rows == targets[0]).astype(F32).astype(BF16)
    small = lax.broadcasted_iota(I32, (BLK, tokens), 0)
    for step, direction in ((-1, 1), (1, 0)):
        source = jnp.clip(me + step, 0, count - 1)
        border = blocks_ref[source, ROW_BORDER : ROW_BORDER + 2, :].astype(I32)
        target = targets[1 if step < 0 else 2]
        start = slots + (0 if step < 0 else halo)
        for i in range(halo // BLK):
            wanted = border[direction : direction + 1, i : i + 1] * BLK
            here = slice(start + i * BLK, start + (i + 1) * BLK)
            picks_ref[here] = (small + wanted == target).astype(F32).astype(BF16)


def decode_kernel(
    blocks_ref,
    picks_ref,
    mine_ref,
    other_ref,
    time_ref,
    proj_ref,
    map_ref,
    weight_ref,
    owned_ref,
    fine_ref,
    code_ref,
):
    is_cond = lax.axis_index("pair") == 0
    slots = owned_ref.shape[1]
    offsets = map_ref.shape[0]
    out_channels = fine_ref.shape[0]
    table_rows = code_ref.shape[2]

    cleans = []
    for s in range(blocks_ref.shape[0]):
        mine, other = mine_ref[s], other_ref[s]
        cond = jnp.where(is_cond, mine, other)
        uncond = jnp.where(is_cond, other, mine)
        guided = uncond + GUIDANCE * (cond - uncond)
        cleans.append(blocks_ref[s, 0:LAT, :] - time_ref[0] * guided)
    clean = jnp.concatenate(cleans, axis=1)

    parts = jnp.concatenate(split_three(clean), axis=0).astype(BF16)
    spread = dot_abt(parts, picks_ref[...])
    table = spread[0:LAT] + spread[LAT : 2 * LAT] + spread[2 * LAT :]
    owned_ref[...] = table[:, 0:slots]

    proj_high, proj_low = split_two(proj_ref[...])
    table_high, table_low = split_two(table)
    left = jnp.concatenate([proj_high, proj_high, proj_low, jnp.zeros_like(proj_low)], axis=0)
    right = jnp.concatenate([table_high, table_low, table_high, jnp.zeros_like(table_low)], axis=0)
    before = dot_atb(left.astype(BF16), right.astype(BF16))
    features = (0.5 * before * (1.0 + jnp.tanh(0.5 * before))).astype(BF16)

    count = 3
    groups = [range(k, min(k + count, offsets)) for k in range(0, offsets, count)]

    def multiply(group):
        rows = weight_ref[group[0] * out_channels : (group[-1] + 1) * out_channels]
        return dot_ab(rows, features)

    def code(group, product):
        top = jnp.max(jnp.abs(product), axis=0, keepdims=True)
        top = jnp.maximum(jnp.max(top, axis=1, keepdims=True), TINY)
        scaled = product * (CODE_TOP / top)
        high = scaled.astype(F8)
        low = (scaled - high.astype(F32)).astype(F8)
        for i, k in enumerate(group):
            rows = slice(i * out_channels, (i + 1) * out_channels)
            code_ref[k, 0:out_channels] = high[rows]
            code_ref[k, out_channels : 2 * out_channels] = low[rows]
        return top * (1.0 / CODE_TOP)

    units = []
    ready = multiply(groups[0])
    for i, group in enumerate(groups):
        product = ready
        if i + 1 < len(groups):
            ready = multiply(groups[i + 1])
        units.append(code(group, product))

    fine = map_ref.shape[2]
    width = 256
    table_ids = lax.broadcasted_iota(jnp.int16, (table_rows, width), 0)
    one = jnp.ones((table_rows, width), F8)
    zero = jnp.zeros((table_rows, width), F8)
    for f in range(fine // width):
        here = slice(f * width, (f + 1) * width)
        total = jnp.zeros((out_channels, width), F32)
        for group, unit in zip(groups, units):
            part = jnp.zeros((2 * out_channels, width), F32)
            for k in group:
                index = jnp.broadcast_to(map_ref[k, :, here], (16, width)).astype(jnp.int16)
                index = jnp.broadcast_to(index[None], (table_rows // 16, 16, width))
                chosen = jnp.where(table_ids == index.reshape(table_rows, width), one, zero)
                part = part + dot_ab(code_ref[k], chosen)
            total = total + (part[0:out_channels] + part[out_channels:]) * unit
        fine_ref[:, here] = total.astype(BF16)


def route_call(blocks, table_rows):
    count, _, block = blocks.shape
    return pl.pallas_call(
        route_kernel,
        out_shape=pltpu.VMEM((table_rows, count * block), BF16),
        in_specs=[VMEM],
        out_specs=VMEM,
        compiler_params=pltpu.CompilerParams(vmem_limit_bytes=VMEM_GRANT),
        cost_estimate=pl.CostEstimate(flops=0, bytes_accessed=1 << 20, transcendentals=0),
        name="route",
    )(blocks)


def decode_call(
    blocks, picks, velocity, partner, step_time, decoder_projection, index_rows, weights
):
    offsets, _, fine = index_rows.shape
    out_channels = weights.shape[0] // offsets
    slots = fine // 4
    table_rows = picks.shape[0]
    return pl.pallas_call(
        decode_kernel,
        out_shape=(
            jax.ShapeDtypeStruct((LAT, slots), F32),
            jax.ShapeDtypeStruct((out_channels, fine), BF16),
        ),
        in_specs=[VMEM, VMEM, VMEM, VMEM, SMEM, VMEM, VMEM, VMEM],
        out_specs=(VMEM, VMEM),
        scratch_shapes=[pltpu.VMEM((offsets, 2 * out_channels, table_rows), F8)],
        compiler_params=pltpu.CompilerParams(vmem_limit_bytes=VMEM_GRANT),
        name="decode",
    )(blocks, picks, velocity, partner, step_time, decoder_projection, index_rows, weights)


def swap_pair(x):
    return lax.ppermute(x, "pair", [(0, 1), (1, 0)])


def seq_swap(x, distance_of):
    count = lax.axis_size("seq")
    routes = [
        (p * count + (z ^ distance_of[p]), p * count + z) for p in range(2) for z in range(count)
    ]
    return lax.ppermute(x, ("pair", "seq"), routes)


def pack_operands(latents, voxel_coords, owner_map, border_blocks):
    return in_hbm(
        latents[0],
        jnp.swapaxes(voxel_coords, 0, 1),
        owner_map.reshape(1, -1),
        border_blocks[0, 0],
    )


def pack_scratch(block, border_blocks):
    return [
        pltpu.VMEM((3, 1, block), I32),
        pltpu.VMEM((1, block), I32),
        pltpu.VMEM(border_blocks.shape[2:], I32),
    ]


def whole_asset_velocity(
    placed, modulation, in_proj, qkv_proj, norm_gain, out_proj, head_proj
):
    latents, _, _, border_blocks = placed
    count = lax.axis_size("seq")
    block = latents.shape[2]
    tokens = count * block
    width = in_proj.shape[1]
    inner = out_proj.shape[0]
    pos = jnp.asarray(position_parts(width))
    block_shapes = (
        pltpu.VMEM((2 * block, width), F32),
        pltpu.VMEM((2 * block, inner), BF16),
        pltpu.VMEM((2 * block, inner), BF16),
        pltpu.VMEM((inner // 128, 2 * block, 128), BF16),
    )
    held_shapes = (
        pltpu.VMEM((5, 1, width), F32),
        pltpu.VMEM(qkv_proj.shape, BF16),
        pltpu.VMEM(norm_gain.shape, F32),
        pltpu.VMEM(out_proj.shape, BF16),
        pltpu.VMEM((LAT, width), F32),
        pltpu.VMEM((pos.shape[0] + 32, width), BF16),
    )
    block_cost = pl.CostEstimate(
        flops=4 * block * width * 4 * inner, bytes_accessed=6 << 20, transcendentals=0
    )
    params = pltpu.CompilerParams(vmem_limit_bytes=VMEM_GRANT)
    sources = in_hbm(
        modulation[0, 0][:, None, :],
        in_proj,
        qkv_proj,
        norm_gain,
        out_proj,
        head_proj.T,
        pos,
    )
    weight_scratch = [pltpu.VMEM(in_proj.shape, F32)]
    weight_sems = pltpu.SemaphoreType.DMA((len(sources),))
    packed, *held = pl.pallas_call(
        early_kernel,
        out_shape=(pltpu.VMEM((PACK_ROWS, block), F32), *held_shapes),
        in_specs=[HBM] * 11,
        out_specs=(VMEM,) * 7,
        scratch_shapes=[
            *pack_scratch(block, border_blocks),
            *weight_scratch,
            pltpu.SemaphoreType.DMA((4,)),
            weight_sems,
        ],
        compiler_params=params,
        name="pack",
    )(*pack_operands(*placed), *sources)
    mixed = seq_swap(packed, (1, 2))
    far = seq_swap(packed, (3, 3))
    swapped = swap_pair(mixed)
    held = pl.pallas_call(
        first_kernel,
        out_shape=(*held_shapes, *block_shapes),
        in_specs=[VMEM] * 2 + [HBM] * 7 + [VMEM] * 6,
        out_specs=(VMEM,) * 10,
        scratch_shapes=[*weight_scratch, pltpu.VMEM((2 * block, width), BF16), weight_sems],
        input_output_aliases={9 + i: i for i in range(6)},
        compiler_params=params,
        cost_estimate=block_cost,
        name="first_blocks",
    )(packed, mixed, *sources, *held)
    return pl.pallas_call(
        velocity_kernel,
        out_shape=(
            pltpu.VMEM((count, LAT, block), F32),
            pltpu.VMEM((count, PACK_ROWS, block), F32),
        ),
        in_specs=[VMEM] * 14,
        out_specs=(VMEM, VMEM),
        scratch_shapes=[
            pltpu.VMEM((tokens, width), F32),
            pltpu.VMEM((tokens, width), BF16),
            pltpu.VMEM((tokens, inner), BF16),
            pltpu.VMEM((tokens, inner), BF16),
            pltpu.VMEM((inner // 128, tokens, 128), BF16),
            pltpu.VMEM((inner, tokens), BF16),
        ],
        compiler_params=pltpu.CompilerParams(vmem_limit_bytes=VMEM_GRANT),
        name="velocity",
    )(packed, mixed, swapped, far, *held)


def pack_call(latents, voxel_coords, owner_map, border_blocks):
    block = latents.shape[2]
    return pl.pallas_call(
        pack_kernel,
        out_shape=pltpu.VMEM((PACK_ROWS, block), F32),
        in_specs=[HBM] * 4,
        out_specs=VMEM,
        scratch_shapes=[*pack_scratch(block, border_blocks), pltpu.SemaphoreType.DMA((4,))],
        compiler_params=pltpu.CompilerParams(vmem_limit_bytes=VMEM_GRANT),
        name="pack",
    )(*pack_operands(latents, voxel_coords, owner_map, border_blocks))


def layer_norm(values):
    center = values - jnp.mean(values, axis=-1, keepdims=True)
    variance = jnp.mean(center * center, axis=-1, keepdims=True)
    return center / jnp.sqrt(variance + EPSILON)


def position_table(coord_rows, model_width):
    freqs = model_width // 6
    steps = jnp.arange(freqs, dtype=F32) / freqs
    omegas = jnp.exp(-math.log(10000.0) * steps)
    angles = coord_rows.astype(F32)[:, :, None] * omegas[None, None, :]
    halves = jnp.concatenate([jnp.sin(angles), jnp.cos(angles)], axis=2)
    rows_out = jnp.transpose(halves, (1, 0, 2)).reshape(coord_rows.shape[1], 6 * freqs)
    return jnp.pad(rows_out, ((0, 0), (0, model_width - 6 * freqs)))


def head_norm(values, gains):
    row_count = values.shape[0]
    per_head = values.reshape(row_count, HEADS, HEAD)
    mean_square = jnp.mean(per_head * per_head, axis=2, keepdims=True)
    return (per_head / jnp.sqrt(mean_square + EPSILON)).reshape(row_count, HEADS * HEAD) * gains


def gathered_velocity(
    latent_block, coords, modulation, in_proj, qkv_proj, norm_gain, out_proj, head_proj
):
    token_count = latent_block.shape[1]
    model_width = in_proj.shape[1]
    inner_width = out_proj.shape[0]
    factor = HEAD ** (-0.5)
    mod_rows = modulation[0, 0]
    hidden = jnp.dot(latent_block.T, in_proj, precision=TOP_PRECISION) + position_table(
        coords, model_width
    )
    normed = (layer_norm(hidden) * (1.0 + mod_rows[1]) + mod_rows[0]).astype(BF16)
    projected = jnp.dot(normed, qkv_proj, preferred_element_type=F32)
    queries = head_norm(projected[:, :inner_width], norm_gain[0]).astype(BF16)
    keys_in = head_norm(projected[:, inner_width : 2 * inner_width], norm_gain[1]).astype(BF16)
    values_in = projected[:, 2 * inner_width :].astype(BF16)
    query_heads = queries.reshape(token_count, HEADS, HEAD)
    start_pair = (
        jnp.zeros((token_count, HEADS, HEAD), F32),
        jnp.zeros((token_count, HEADS), F32),
    )
    key_rows = lax.all_gather(keys_in, "seq", axis=0, tiled=True)
    value_rows = lax.all_gather(values_in, "seq", axis=0, tiled=True)
    row_count = key_rows.shape[0]
    block_rows = math.gcd(row_count, 512)
    key_blocks = key_rows.reshape(row_count // block_rows, block_rows, HEADS, HEAD)
    value_blocks = value_rows.reshape(row_count // block_rows, block_rows, HEADS, HEAD)

    def one_block(running, block_pair):
        numer_run, denom_run = running
        key_block, value_block = block_pair
        scores = (
            jnp.einsum("qhd,khd->hqk", query_heads, key_block, preferred_element_type=F32) * factor
        )
        exp_scores = jnp.exp(scores)
        numer_run = numer_run + jnp.einsum(
            "hqk,khd->qhd", exp_scores.astype(BF16), value_block, preferred_element_type=F32
        )
        denom_run = denom_run + jnp.sum(exp_scores, axis=2).T
        return ((numer_run, denom_run), None)

    (numerator, denominator), _ = lax.scan(one_block, start_pair, (key_blocks, value_blocks))
    attended = (
        (numerator / denominator[:, :, None]).reshape(token_count, inner_width).astype(BF16)
    )
    hidden = hidden + mod_rows[2] * jnp.dot(attended, out_proj, preferred_element_type=F32)
    final = layer_norm(hidden) * (1.0 + mod_rows[4]) + mod_rows[3]
    velocity = jnp.dot(final, head_proj, precision=TOP_PRECISION).T
    return lax.all_gather(velocity, "seq", axis=0)


def per_device(
    latents,
    voxel_coords,
    owner_map,
    step_time,
    modulation,
    in_proj,
    qkv_proj,
    norm_gain,
    out_proj,
    head_proj,
    decoder_projection,
    border_blocks,
    kernel_map,
    conv_weight,
):
    count = lax.axis_size("seq")
    block = latents.shape[2]
    placed = (latents, voxel_coords, owner_map, border_blocks)
    if count == 4 and count * block <= WHOLE_ASSET:
        velocity, blocks = whole_asset_velocity(
            placed, modulation, in_proj, qkv_proj, norm_gain, out_proj, head_proj
        )
    else:
        blocks = lax.all_gather(pack_call(*placed), "seq", axis=0)
        velocity = gathered_velocity(
            latents[0],
            voxel_coords[0],
            modulation,
            in_proj,
            qkv_proj,
            norm_gain,
            out_proj,
            head_proj,
        )
    partner = swap_pair(velocity)
    picks = route_call(blocks, kernel_map.shape[3] // 2)
    offsets, _, out_channels = conv_weight.shape
    fine = kernel_map.shape[3]
    owned, decoded = decode_call(
        blocks,
        picks,
        velocity,
        partner,
        step_time,
        decoder_projection,
        kernel_map.reshape(offsets, 1, fine),
        jnp.swapaxes(conv_weight, 1, 2).reshape(offsets * out_channels, -1),
    )
    return (owned[None, None], decoded.T[None, None])


def solution(mesh):
    placed = (
        P("asset", None, "seq"),
        P("asset", None, "seq"),
        P("asset", "seq", None),
        P("asset"),
        P("asset", "pair", None, None),
        P(),
        P(),
        P(),
        P(),
        P(),
        P(),
        P("asset", "seq", None, None),
        P("asset", "seq", None, None),
        P(None, None, "pair"),
    )
    return jax.shard_map(
        per_device,
        mesh=mesh,
        in_specs=placed,
        out_specs=(P("asset", "seq", None, None), P("asset", "seq", None, "pair")),
        check_vma=False,
    )
```
